32 devices in a mesh: dp: 8 (over y, x, core), tensor: 4 (over z).
Axes of the slice: x: 2, y: 2, z: 4, core: 2. Of those that a mesh axis runs over, the one named last changes fastest.
Arguments:
- tokens: bfloat16 [4096, 8192], P('dp', 'tensor'), may hold values from -6 to 6
- row_adapter_index: int32 [4096, 1], P('dp'), may hold values from 0 to 63; in each aligned block of 512 rows (0 to 511, 512 to 1023, ...) at most 16 rows name the same one
- adapter_storage_slot: int32 [64], replicated, may hold values from 0 to 63, each once
- key_value_base_weight: bfloat16 [8192, 2, 1024], P('tensor'), may hold values from -0.09375 to 0.09375
- adapter_down_weight: bfloat16 [64, 8192, 128], P('dp', 'tensor'), may hold values from -0.0625 to 0.0625
- adapter_up_weight: bfloat16 [64, 2, 64, 1024], P('dp', None, None, 'tensor'), may hold values from -0.75 to 0.75
Outputs:
- key_value: bfloat16 [4096, 2, 1024], P('dp', None, 'tensor')
The draws below stay inside these ranges and needn't reach their ends.
Inputs may be any that keep to these rules, and one draw needn't show every extreme that they name: `row_adapter_index`: within the rows of one index of dp no adapter is named by more than 16 rows, a bound that some block reaches. `adapter_storage_slot`: A permutation of the slots.
All inputs are finite; a program needn't handle non-finite values.
Results may differ from the reference program's by a relative error of at most 0.0034.
Values may be sent and summed in bfloat16 or wider, within the bound.
No kernel may reach another device: no remote copies, remote signals or barrier semaphores. Data moves between devices by JAX's collectives and lax.ppermute only.
A program may use at most 64 MiB of HBM per device.

```python
import math
import jax
import jax.numpy as jnp
import numpy as np
from jax import lax

MODEL_WIDTH = 8192
KEY_VALUE_WIDTH = 1024
ADAPTER_RANK = 64
TOK_DEV = 512
ADAPTER_TOTAL = 64
CAP = 16
TOKENS = 4096
N_DP = 8
N_TENSOR = 4


def spiked(drawn, key, source, target, blocks, factor):
    def block_of(position):
        return (jnp.arange(drawn.shape[position]) // (drawn.shape[position] // blocks)).reshape((-1,) + (1,) * (drawn.ndim - 1 - position))

    first = jax.random.permutation(key, blocks)[block_of(target)]
    other_side = (block_of(target) + blocks // 2) % blocks
    return jnp.where((block_of(source) == first) | (block_of(source) == other_side), factor * drawn, drawn)


def shard_levels(stream_key, extent, pieces, smallest, largest):
    loudness = 1.0
    for position, parts in pieces:
        draws = jax.random.uniform(jax.random.fold_in(jax.random.fold_in(stream_key, 6), position), (parts,), jnp.float32, smallest / len(pieces), largest / len(pieces))
        loudness = loudness * jnp.repeat(jnp.exp(draws), extent[position] // parts).reshape((-1,) + (1,) * (len(extent) - 1 - position))
    return loudness


def routed_block(stream_key, own, number, rows, amount, top, most, skew):
    ranking = jax.random.permutation(stream_key, amount)
    packed, common = portions_of(amount, rows * top, most, skew, True), portions_of(amount, rows * top, most, skew, False)
    places = jnp.arange(amount)

    def named(lengths, offset_by):
        used = int((lengths > 0).sum())
        fixed = max(1, used // 4)
        passed = fixed + (places - fixed + offset_by * (used - fixed)) % max(1, amount - fixed)
        return jnp.zeros((amount,), jnp.int32).at[ranking[jnp.where(places < fixed, places, passed)]].set(jnp.asarray(lengths, jnp.int32))

    lengths = jnp.where(number % 4 == 0, named(packed, number // 4), named(common, number - number // 4 - 1))
    mixed = jax.random.permutation(jax.random.fold_in(own, 3), amount)
    source_of, sink = mixed[0:amount // 2 * 2:2], mixed[1:amount // 2 * 2:2]
    margin = jnp.minimum(lengths[source_of] - 1, most - lengths[sink]) // 2
    margin = jnp.where((source_of == ranking[0]) | (sink == ranking[0]) | (lengths[sink] == 0), 0, jnp.maximum(margin, 0))
    passed = jax.random.randint(jax.random.fold_in(own, 4), (amount // 2,), 0, 1 << 20) % (margin + 1)
    lengths = lengths.at[source_of].add(-passed).at[sink].add(passed)
    items = jnp.searchsorted(jnp.cumsum(lengths), jnp.arange(rows * top), side="right").astype(jnp.int32)
    grid = items.reshape(top, rows).T
    grid = grid[jax.random.permutation(jax.random.fold_in(own, 1), rows)]
    offset_by = jax.random.randint(jax.random.fold_in(own, 2), (rows, 1), 0, top)
    return jnp.take_along_axis(grid, (jnp.arange(top)[None, :] + offset_by) % top, axis=1)


def portions_of(count, total, limit, slope, full):
    weights = [(1 << 20) // math.isqrt(standing ** slope) + 1 for standing in range(1, count + 1)]
    largest = limit if full else min(limit, max(-(-total // count), total * weights[0] // sum(weights)))
    least = 1 if total - largest >= count - 1 else 0
    given, surplus = [largest] + [least] * (count - 1), total - largest - least * (count - 1)
    while surplus > 0:
        candidates = [i for i in range(1, count) if given[i] < largest] or [i for i in range(1, count) if given[i] < limit]
        whole, remaining = sum([weights[i] for i in candidates]), surplus
        for i in candidates:
            addition = min(limit - given[i], max(1, remaining * weights[i] // whole), surplus)
            given[i] = given[i] + addition
            surplus = surplus - addition
    return np.array(given)


def scatter_about(own_key, shape, scale, limit, shards=(), held_as=jnp.bfloat16):
    factor_of = shard_levels(own_key, shape, shards, -0.22, 0.18) if shards else 1.0
    array = jax.random.normal(own_key, shape, jnp.float32) * scale * factor_of
    return jnp.minimum(jnp.maximum(array, -limit), limit).astype(held_as)


def heavy_noise(rng, shape, width, limit, shards, heavy, held_as=jnp.bfloat16):
    array = width * jax.random.normal(rng, shape, jnp.float32)
    if shards:
        array = array * shard_levels(rng, shape, shards, -0.22, 0.18)
    return jnp.clip(spiked(array, jax.random.fold_in(rng, 3), *heavy), -limit, limit).astype(held_as)


def setup_inputs(seed: int = 0) -> dict:
    seeds = jax.random.split(jax.random.key(seed), 7)
    tokens = scatter_about(seeds[0], (TOKENS, MODEL_WIDTH), 1.0, 6.0, ((0, 8), (1, 4)))
    row_adapter_index_keys = jax.random.split(jax.random.fold_in(seeds[1], 1), TOKENS // TOK_DEV)
    row_adapter_index_turns = jax.random.permutation(jax.random.fold_in(seeds[1], 3), TOKENS // TOK_DEV)
    row_adapter_index = jax.vmap(lambda own, number: routed_block(jax.random.fold_in(seeds[1], 2), own, number, TOK_DEV, ADAPTER_TOTAL, 1, CAP, 2))(row_adapter_index_keys, row_adapter_index_turns).reshape((TOKENS, 1))
    adapter_storage_slot = jax.random.permutation(seeds[2], ADAPTER_TOTAL).astype(jnp.int32)
    key_value_base_weight = heavy_noise(seeds[3], (MODEL_WIDTH, 2, KEY_VALUE_WIDTH), MODEL_WIDTH ** -0.5, 0.09375, ((0, 4),), (0, 2, 4, 2.0))
    adapter_down_weight = scatter_about(seeds[4], (ADAPTER_TOTAL, MODEL_WIDTH, 2 * ADAPTER_RANK), MODEL_WIDTH ** -0.5, 0.0625, ((0, 8), (1, 4)))
    adapter_up_weight = scatter_about(seeds[5], (ADAPTER_TOTAL, 2, ADAPTER_RANK, KEY_VALUE_WIDTH), ADAPTER_RANK ** -0.5, 0.75, ((0, 8), (3, 4)))
    return {"tokens": tokens, "row_adapter_index": row_adapter_index, "adapter_storage_slot": adapter_storage_slot, "key_value_base_weight": key_value_base_weight, "adapter_down_weight": adapter_down_weight, "adapter_up_weight": adapter_up_weight}


adapter_scale = 0.5


def reference(tokens, row_adapter_index, adapter_storage_slot, key_value_base_weight, adapter_down_weight, adapter_up_weight):
    count_rows, full_width = tokens.shape
    shard_width = full_width // N_TENSOR
    blocked_x = tokens.reshape(count_rows, N_TENSOR, shard_width)
    blocked_w = key_value_base_weight.reshape(N_TENSOR, shard_width, 2 * KEY_VALUE_WIDTH)

    def add_block(summed, block_index):
        piece_x = lax.dynamic_index_in_dim(blocked_x, block_index, 1, keepdims=False)
        piece_w = lax.dynamic_index_in_dim(blocked_w, block_index, 0, keepdims=False)
        product = jnp.dot(piece_x, piece_w, preferred_element_type=jnp.float32)
        return summed + product, None

    base, unused = lax.scan(add_block, jnp.zeros((count_rows, 2 * KEY_VALUE_WIDTH), jnp.float32),
                            jnp.arange(N_TENSOR, dtype=jnp.int32))
    base = base.reshape(count_rows, 2, KEY_VALUE_WIDTH)

    adapter_of = row_adapter_index[:, 0]
    order_rows = jnp.argsort(adapter_of, stable=True).astype(jnp.int32)
    counts = jnp.zeros((ADAPTER_TOTAL,), jnp.int32).at[adapter_of].add(1)
    starts = jnp.cumsum(counts) - counts
    most_rows = N_DP * CAP
    offsets = jnp.arange(most_rows, dtype=jnp.int32)

    def one_adapter(adapter):
        is_used = offsets < counts[adapter]
        chosen_rows = order_rows[jnp.minimum(starts[adapter] + offsets, count_rows - 1)]
        storage_device = adapter_storage_slot[adapter]
        reduced_rows = jnp.dot(tokens[chosen_rows], adapter_down_weight[storage_device], preferred_element_type=jnp.float32).astype(jnp.bfloat16)
        reduced_rows = lax.optimization_barrier(reduced_rows)
        reduced_rows = reduced_rows.astype(jnp.float32).reshape(most_rows, 2, ADAPTER_RANK)
        adapter_delta = jnp.einsum("ave,vef->avf", reduced_rows, adapter_up_weight[storage_device].astype(jnp.float32))
        adapter_delta = (adapter_scale * adapter_delta).astype(jnp.bfloat16)
        adapter_delta = jnp.where(is_used[:, None, None], adapter_delta, jnp.zeros_like(adapter_delta))
        return chosen_rows, adapter_delta

    picked_all, updates = lax.map(one_adapter, jnp.arange(ADAPTER_TOTAL, dtype=jnp.int32))
    updates = lax.optimization_barrier(updates)
    summed = jnp.zeros((count_rows, 2, KEY_VALUE_WIDTH), jnp.float32).at[picked_all.reshape(-1)].add(
        updates.reshape(-1, 2, KEY_VALUE_WIDTH).astype(jnp.float32))
    return (base + summed).astype(jnp.bfloat16)
```

```python
import functools

import jax
import jax.numpy as jnp
from jax import lax
from jax.experimental import pallas as pl
from jax.experimental.pallas import tpu as pltpu
from jax.sharding import PartitionSpec as P

adapter_scale = 0.5
BF = jnp.bfloat16
F32 = jnp.float32
VMEM_LIMIT = 48 * 1024 * 1024


def round_up(value, unit):
    return (value + unit - 1) // unit * unit


def dot(a, b, contract=((1,), (0,))):
    return lax.dot_general(a, b, (contract, ((), ())), preferred_element_type=F32)


def pack_kernel(shape, place_ref, adapter_ref, slot_ref, tokens_ref, *refs):
    sizes, first_rows, chip_slots, flag_lane = shape
    messages = len(sizes)
    outs, spread_ref, pick = refs[:messages], refs[messages], refs[messages + 1]
    rows, width = tokens_ref.shape
    experts = slot_ref.shape[1]
    offsets = [sum(round_up(s, 128) for s in sizes[:m]) for m in range(messages)]

    @pl.when(pl.program_id(0) == 0)
    def _():
        named = (lax.broadcasted_iota(jnp.int32, (experts, rows), 0) == adapter_ref[...]).astype(BF)
        slots = jnp.broadcast_to(slot_ref[...].astype(F32), (16, experts)).astype(BF)
        slot = dot(slots, named)[0:1, :].astype(jnp.int32)
        shift = (slot // chip_slots) ^ place_ref[0]
        within = (slot % chip_slots + 1).astype(F32)
        lanes = round_up(messages, 16)
        goes = lax.broadcasted_iota(jnp.int32, (lanes, rows), 0) == shift
        earlier = lax.broadcasted_iota(jnp.int32, (rows, rows), 0) < lax.broadcasted_iota(jnp.int32, (rows, rows), 1)
        goes_f = goes.astype(F32)
        rank = dot(goes_f.astype(BF), earlier.astype(F32).astype(BF))
        position = jnp.sum(rank * goes_f, axis=0, keepdims=True).astype(jnp.int32)
        counts = jnp.sum(goes_f, axis=1, keepdims=True)
        sub = lax.broadcasted_iota(jnp.int32, (lanes, 1), 0)
        limit = jnp.zeros((lanes, 1), F32)
        for m in range(messages):
            limit = jnp.where(sub == m, F32(first_rows[m] + sizes[m] - 1), limit)
        over = jnp.max(jnp.where((sub < messages) & (counts > limit), 1.0, 0.0), axis=0, keepdims=True)
        within8 = jnp.broadcast_to(within, (16, rows)).astype(BF)
        for m in range(messages):
            padded = round_up(sizes[m], 128)
            target = lax.broadcasted_iota(jnp.int32, (padded, rows), 0)
            hit = (target + first_rows[m] == position) & (shift == m) & (target < sizes[m] - 1)
            chosen = hit.astype(F32).astype(BF)
            pick[offsets[m]:offsets[m] + padded, :] = chosen
            spread_ref[:, offsets[m]:offsets[m] + padded] = hit.astype(F32).T.astype(BF)
            places = dot(within8, chosen, ((1,), (1,)))[0:1, :]
            if padded < width:
                places = jnp.concatenate([places, jnp.zeros((1, width - padded), F32)], axis=1)
            lane = lax.broadcasted_iota(jnp.int32, (1, width), 1)
            places = jnp.where(lane == flag_lane, over, places)
            body = dot(chosen, tokens_ref[...])[:sizes[m], :]
            row = lax.broadcasted_iota(jnp.int32, (sizes[m], 1), 0)
            outs[m][...] = jnp.where(row == sizes[m] - 1, places, body).astype(BF)

    @pl.when(pl.program_id(0) > 0)
    def _():
        for m in range(messages):
            outs[m][...] = dot(pick[offsets[m]:offsets[m] + sizes[m], :], tokens_ref[...]).astype(BF)


def pack(chip, adapters, slots, tokens, sizes, first_rows, chip_slots, steps=4):
    rows, width = tokens.shape
    block = width // steps
    spread = sum(round_up(s, 128) for s in sizes)
    return pl.pallas_call(
        functools.partial(pack_kernel, (sizes, first_rows, chip_slots, block - 1)),
        grid=(steps,),
        in_specs=[
            pl.BlockSpec(memory_space=pltpu.SMEM),
            pl.BlockSpec((1, rows), lambda i: (0, 0)),
            pl.BlockSpec((1, slots.shape[1]), lambda i: (0, 0)),
            pl.BlockSpec((rows, block), lambda i: (0, i)),
        ],
        out_specs=[pl.BlockSpec((s, block), lambda i: (0, i)) for s in sizes]
        + [pl.BlockSpec((rows, spread), lambda i: (0, 0))],
        out_shape=[jax.ShapeDtypeStruct((s, width), BF) for s in sizes] + [jax.ShapeDtypeStruct((rows, spread), BF)],
        scratch_shapes=[pltpu.VMEM((spread, rows), BF)],
        compiler_params=pltpu.CompilerParams(vmem_limit_bytes=VMEM_LIMIT),
        name="pack_rows",
    )(chip, adapters, slots, tokens)


def shrink_kernel(count, flag_lane, core_ref, *refs):
    messages, (mine, sibling), (out, place_out, flag_out) = refs[:count], refs[count:count + 2], refs[count + 2:count + 5]
    total, places = refs[count + 5:]
    step = pl.program_id(0)
    local = 2 * pl.num_programs(0)
    sizes = [m.shape[0] for m in messages]

    @pl.when(step == 0)
    def _():
        flag = jnp.zeros((1, 1), F32)
        start = 0
        for m, size in zip(messages, sizes):
            padded = round_up(size, 128)
            tail = m[size - 16:size, 0:padded].astype(F32)[15:16, :]
            same = lax.broadcasted_iota(jnp.int32, (size, padded), 0) == lax.broadcasted_iota(jnp.int32, (size, padded), 1)
            column = jnp.sum(jnp.where(same, tail, 0.0), axis=1, keepdims=True)
            places[start:start + size, :] = jnp.broadcast_to(column, (size, 128))
            block = m[size - 16:size, flag_lane - 127:flag_lane + 1].astype(F32)[15:16, :]
            last = lax.broadcasted_iota(jnp.int32, (1, 128), 1) == 127
            flag = jnp.maximum(flag, jnp.max(jnp.where(last, block, 0.0), axis=1, keepdims=True))
            start += size
        place_out[...] = places[...].astype(BF)
        flag_out[...] = jnp.broadcast_to(flag, (8, 128))
        total[...] = jnp.zeros_like(total)

    rows = messages[0][...] if count == 1 else jnp.concatenate([m[...] for m in messages], axis=0)
    place = places[...]
    core = core_ref[0]
    for weights, side in ((mine, core), (sibling, 1 - core)):
        product = dot(rows, jnp.concatenate([weights[0], weights[1]], axis=1))
        first = (side * local + 2 * step + 1).astype(F32)
        total[...] += jnp.where(place == first, product[:, :128], 0.0) + jnp.where(
            place == first + 1.0, product[:, 128:], 0.0
        )

    @pl.when(step == pl.num_programs(0) - 1)
    def _():
        out[...] = total[...].astype(BF)


def shrink(core, messages, mine, sibling, flag_lane):
    local, width, both = mine.shape
    rows = sum(m.shape[0] for m in messages)
    whole = [pl.BlockSpec(m.shape, lambda i: (0, 0)) for m in messages]
    pair = pl.BlockSpec((2, width, both), lambda i: (i, 0, 0))
    keep = pl.BlockSpec((rows, both), lambda i: (0, 0))
    return pl.pallas_call(
        functools.partial(shrink_kernel, len(messages), flag_lane),
        grid=(local // 2,),
        in_specs=[pl.BlockSpec(memory_space=pltpu.SMEM)] + whole + [pair, pair],
        out_specs=[keep, keep, pl.BlockSpec((8, 128), lambda i: (0, 0))],
        out_shape=[
            jax.ShapeDtypeStruct((rows, both), BF),
            jax.ShapeDtypeStruct((rows, both), BF),
            jax.ShapeDtypeStruct((8, 128), F32),
        ],
        scratch_shapes=[pltpu.VMEM((rows, both), F32), pltpu.VMEM((rows, both), F32)],
        compiler_params=pltpu.CompilerParams(vmem_limit_bytes=VMEM_LIMIT),
        name="shrink_rows",
    )(core, *messages, mine, sibling)


def grow_kernel(shares, sizes, core_ref, *refs):
    parts, place_ref, mine, sibling = refs[:shares], refs[shares], refs[shares + 1], refs[shares + 2]
    outs = refs[shares + 3:]
    summed = parts[0][...].astype(F32)
    for part in parts[1:]:
        summed = summed + part[...].astype(F32)
    shrunk = summed.astype(BF).astype(F32)
    place = place_ref[...].astype(F32)
    local, _, rank, columns = mine.shape
    core = core_ref[0]
    low = lax.broadcasted_iota(jnp.int32, shrunk.shape, 1) < rank
    turned = pltpu.roll(shrunk, rank, 1)
    result = []
    for j in range(2):
        twice = jnp.where(low, shrunk, turned) if j == 0 else jnp.where(low, turned, shrunk)
        total = None
        for weights, side in ((mine, core), (sibling, 1 - core)):
            left = []
            for e in range(0, local, 2):
                first = (side * local + e + 1).astype(F32)
                wanted = jnp.where(low, first, first + 1.0)
                left.append(jnp.where(place == wanted, twice, 0.0).astype(BF))
            right = weights[:, j].reshape(local * rank, columns)
            product = dot(jnp.concatenate(left, axis=1), right)
            total = product if total is None else total + product
        result.append((adapter_scale * total).astype(BF))
    start = 0
    for out, size in zip(outs, sizes):
        out[:, :columns] = result[0][start:start + size, :]
        out[:, columns:] = result[1][start:start + size, :]
        start += size


def grow(core, parts, place, mine, sibling, sizes):
    columns = mine.shape[3]
    vmem = pl.BlockSpec(memory_space=pltpu.VMEM)
    return pl.pallas_call(
        functools.partial(grow_kernel, len(parts), sizes),
        in_specs=[pl.BlockSpec(memory_space=pltpu.SMEM)] + [vmem] * (len(parts) + 3),
        out_specs=[vmem] * len(sizes),
        out_shape=[jax.ShapeDtypeStruct((s, 2 * columns), BF) for s in sizes],
        compiler_params=pltpu.CompilerParams(vmem_limit_bytes=VMEM_LIMIT),
        name="grow_rows",
    )(core, *parts, place, mine, sibling)


def place_kernel(sizes, spread_ref, *refs):
    updates, out = refs[:-1], refs[-1]
    total = None
    start = 0
    for update, size in zip(updates, sizes):
        padded = round_up(size, 128)
        rows = update[...]
        if padded > size:
            rows = jnp.concatenate([rows, jnp.zeros((padded - size, rows.shape[1]), rows.dtype)], axis=0)
        product = dot(spread_ref[:, start:start + padded], rows)
        total = product if total is None else total + product
        start += padded
    out[...] = total


def place_rows(spread, updates):
    sizes = tuple(u.shape[0] for u in updates)
    vmem = pl.BlockSpec(memory_space=pltpu.VMEM)
    return pl.pallas_call(
        functools.partial(place_kernel, sizes),
        in_specs=[vmem] * (len(updates) + 1),
        out_specs=vmem,
        out_shape=jax.ShapeDtypeStruct((spread.shape[0], updates[0].shape[1]), F32),
        compiler_params=pltpu.CompilerParams(vmem_limit_bytes=VMEM_LIMIT),
        name="place_rows",
    )(spread, *updates)


def exchange(array, axis, shift):
    size = lax.axis_size(axis)
    return lax.ppermute(array, axis, [(i, i ^ shift) for i in range(size)])


def after(array, *others):
    return lax.optimization_barrier((array,) + others)[0]


def bits(value):
    return bin(value).count("1")


def per_device(
    tokens,
    row_adapter_index,
    adapter_storage_slot,
    key_value_base_weight,
    adapter_down_weight,
    adapter_up_weight,
):
    row_count, width = tokens.shape
    local = adapter_down_weight.shape[0]
    groups = lax.axis_size("dp")
    blocks = lax.axis_size("tensor")
    experts = local * groups
    chips = groups // 2
    capacity = max(2, 2 * row_count // experts)
    chip_slots = 2 * local
    full = chip_slots * capacity

    me = lax.axis_index("dp").astype(jnp.int32)
    chip, core = (me // 2).reshape(1), (me % 2).reshape(1)
    adapters = row_adapter_index.reshape(1, row_count)
    slots = adapter_storage_slot.reshape(1, experts)
    flag_lane = width // 4 - 1

    down_sibling = exchange(adapter_down_weight, "dp", 1)
    up_sibling = exchange(adapter_up_weight, "dp", 1)

    near = [m for m in range(chips) if bits(m) <= 1]
    far = [m for m in range(chips) if bits(m) > 1]

    def update_of(sizes, first_rows, meanwhile):
        packed = pack(chip, adapters, slots, tokens, sizes, first_rows, chip_slots)
        sent, spread = list(packed[:-1]), packed[-1]
        arrived, returned = {0: sent[0]}, {}
        for m in near[1:]:
            arrived[m] = exchange(sent[m], "dp", 2 * m)
        held = meanwhile(sent)
        for m in far:
            arrived[m] = exchange(after(sent[m], held) if held is not None else sent[m], "dp", 2 * m)
        for part in (near, far):
            if not part:
                continue
            group = [arrived[m] for m in part]
            share, place, flag = shrink(core, group, adapter_down_weight, down_sibling, flag_lane)
            shares = [share] + [exchange(share, "tensor", t) for t in range(1, blocks)]
            grown = grow(core, shares, place, adapter_up_weight, up_sibling, tuple(sizes[m] for m in part))
            for m, update in zip(part, grown):
                returned[m] = update if m == 0 else exchange(update, "dp", 2 * m)
        return place_rows(spread, [returned[m] for m in range(chips)])

    base = []

    def base_part(j):
        partial = dot(tokens, key_value_base_weight[:, j, :])
        return partial.reshape(row_count, blocks, partial.shape[1] // blocks)

    def reduce_part(partial):
        t = lax.axis_index("tensor")
        step = 1
        while step < blocks:
            halves = partial.reshape(row_count, partial.shape[1] // 2, 2, partial.shape[2])
            bit = (t // step) % 2
            send = lax.dynamic_index_in_dim(halves, 1 - bit, 2, keepdims=False).astype(BF)
            keep = lax.dynamic_index_in_dim(halves, bit, 2, keepdims=False)
            partial = keep + exchange(send, "tensor", step).astype(F32)
            step *= 2
        return partial[:, 0, :]

    def meanwhile(sent):
        parts = [base_part(j) for j in range(2)]
        base.extend(reduce_part(p) for p in parts)
        return parts[1]

    message = round_up(full + 1, 16)
    update = update_of((message,) * chips, (0,) * chips, meanwhile)
    summed = jnp.stack(base, axis=1) + update.reshape(row_count, 2, update.shape[1] // 2)
    return summed.astype(BF)


def solution(mesh):
    placed = (
        P("dp", "tensor"),
        P("dp", None),
        P(),
        P("tensor", None, None),
        P("dp", "tensor", None),
        P("dp", None, None, "tensor"),
    )
    return jax.shard_map(
        per_device, mesh=mesh, in_specs=placed, out_specs=P("dp", None, "tensor"), check_vma=False
    )
```

```python
import functools

import jax
import jax.numpy as jnp
from jax import lax
from jax.experimental import pallas as pl
from jax.experimental.pallas import tpu as pltpu
from jax.sharding import PartitionSpec as P

adapter_scale = 0.5
BF = jnp.bfloat16
F32 = jnp.float32
VMEM_LIMIT = 48 * 1024 * 1024


def round_up(value, unit):
    return (value + unit - 1) // unit * unit


def dot(a, b, contract=((1,), (0,))):
    return lax.dot_general(a, b, (contract, ((), ())), preferred_element_type=F32)


def pack_kernel(shape, place_ref, adapter_ref, slot_ref, tokens_ref, *refs):
    sizes, first_rows, chip_slots, flag_lane = shape
    messages = len(sizes)
    outs, spread_ref, pick = refs[:messages], refs[messages], refs[messages + 1]
    rows, width = tokens_ref.shape
    experts = slot_ref.shape[1]
    offsets = [sum(round_up(s, 128) for s in sizes[:m]) for m in range(messages)]

    @pl.when(pl.program_id(0) == 0)
    def _():
        named = (lax.broadcasted_iota(jnp.int32, (experts, rows), 0) == adapter_ref[...]).astype(BF)
        slots = jnp.broadcast_to(slot_ref[...].astype(F32), (16, experts)).astype(BF)
        slot = dot(slots, named)[0:1, :].astype(jnp.int32)
        shift = (slot // chip_slots) ^ place_ref[0]
        within = (slot % chip_slots + 1).astype(F32)
        lanes = round_up(messages, 16)
        goes = lax.broadcasted_iota(jnp.int32, (lanes, rows), 0) == shift
        earlier = lax.broadcasted_iota(jnp.int32, (rows, rows), 0) < lax.broadcasted_iota(jnp.int32, (rows, rows), 1)
        goes_f = goes.astype(F32)
        rank = dot(goes_f.astype(BF), earlier.astype(F32).astype(BF))
        position = jnp.sum(rank * goes_f, axis=0, keepdims=True).astype(jnp.int32)
        counts = jnp.sum(goes_f, axis=1, keepdims=True)
        sub = lax.broadcasted_iota(jnp.int32, (lanes, 1), 0)
        limit = jnp.zeros((lanes, 1), F32)
        for m in range(messages):
            limit = jnp.where(sub == m, F32(first_rows[m] + sizes[m] - 1), limit)
        over = jnp.max(jnp.where((sub < messages) & (counts > limit), 1.0, 0.0), axis=0, keepdims=True)
        within8 = jnp.broadcast_to(within, (16, rows)).astype(BF)
        for m in range(messages):
            padded = round_up(sizes[m], 128)
            target = lax.broadcasted_iota(jnp.int32, (padded, rows), 0)
            hit = (target + first_rows[m] == position) & (shift == m) & (target < sizes[m] - 1)
            chosen = hit.astype(F32).astype(BF)
            pick[offsets[m]:offsets[m] + padded, :] = chosen
            spread_ref[:, offsets[m]:offsets[m] + padded] = hit.astype(F32).T.astype(BF)
            places = dot(within8, chosen, ((1,), (1,)))[0:1, :]
            if padded < width:
                places = jnp.concatenate([places, jnp.zeros((1, width - padded), F32)], axis=1)
            lane = lax.broadcasted_iota(jnp.int32, (1, width), 1)
            places = jnp.where(lane == flag_lane, over, places)
            body = dot(chosen, tokens_ref[...])[:sizes[m], :]
            row = lax.broadcasted_iota(jnp.int32, (sizes[m], 1), 0)
            outs[m][...] = jnp.where(row == sizes[m] - 1, places, body).astype(BF)

    @pl.when(pl.program_id(0) > 0)
    def _():
        for m in range(messages):
            outs[m][...] = dot(pick[offsets[m]:offsets[m] + sizes[m], :], tokens_ref[...]).astype(BF)


def pack(chip, adapters, slots, tokens, sizes, first_rows, chip_slots, steps=4):
    rows, width = tokens.shape
    block = width // steps
    spread = sum(round_up(s, 128) for s in sizes)
    return pl.pallas_call(
        functools.partial(pack_kernel, (sizes, first_rows, chip_slots, block - 1)),
        grid=(steps,),
        in_specs=[
            pl.BlockSpec(memory_space=pltpu.SMEM),
            pl.BlockSpec((1, rows), lambda i: (0, 0)),
            pl.BlockSpec((1, slots.shape[1]), lambda i: (0, 0)),
            pl.BlockSpec((rows, block), lambda i: (0, i)),
        ],
        out_specs=[pl.BlockSpec((s, block), lambda i: (0, i)) for s in sizes]
        + [pl.BlockSpec((rows, spread), lambda i: (0, 0))],
        out_shape=[jax.ShapeDtypeStruct((s, width), BF) for s in sizes] + [jax.ShapeDtypeStruct((rows, spread), BF)],
        scratch_shapes=[pltpu.VMEM((spread, rows), BF)],
        compiler_params=pltpu.CompilerParams(vmem_limit_bytes=VMEM_LIMIT),
        name="pack_rows",
    )(chip, adapters, slots, tokens)


def shrink_kernel(count, flag_lane, core_ref, *refs):
    messages, (mine, sibling), (out, place_out, flag_out) = refs[:count], refs[count:count + 2], refs[count + 2:count + 5]
    total, places = refs[count + 5:]
    step = pl.program_id(0)
    local = 2 * pl.num_programs(0)
    sizes = [m.shape[0] for m in messages]

    @pl.when(step == 0)
    def _():
        flag = jnp.zeros((1, 1), F32)
        start = 0
        for m, size in zip(messages, sizes):
            padded = round_up(size, 128)
            tail = m[size - 16:size, 0:padded].astype(F32)[15:16, :]
            same = lax.broadcasted_iota(jnp.int32, (size, padded), 0) == lax.broadcasted_iota(jnp.int32, (size, padded), 1)
            column = jnp.sum(jnp.where(same, tail, 0.0), axis=1, keepdims=True)
            places[start:start + size, :] = jnp.broadcast_to(column, (size, 128))
            block = m[size - 16:size, flag_lane - 127:flag_lane + 1].astype(F32)[15:16, :]
            last = lax.broadcasted_iota(jnp.int32, (1, 128), 1) == 127
            flag = jnp.maximum(flag, jnp.max(jnp.where(last, block, 0.0), axis=1, keepdims=True))
            start += size
        place_out[...] = places[...].astype(BF)
        flag_out[...] = jnp.broadcast_to(flag, (8, 128))
        total[...] = jnp.zeros_like(total)

    rows = messages[0][...] if count == 1 else jnp.concatenate([m[...] for m in messages], axis=0)
    place = places[...]
    core = core_ref[0]
    for weights, side in ((mine, core), (sibling, 1 - core)):
        product = dot(rows, jnp.concatenate([weights[0], weights[1]], axis=1))
        first = (side * local + 2 * step + 1).astype(F32)
        total[...] += jnp.where(place == first, product[:, :128], 0.0) + jnp.where(
            place == first + 1.0, product[:, 128:], 0.0
        )

    @pl.when(step == pl.num_programs(0) - 1)
    def _():
        out[...] = total[...].astype(BF)


def shrink(core, messages, mine, sibling, flag_lane):
    local, width, both = mine.shape
    rows = sum(m.shape[0] for m in messages)
    whole = [pl.BlockSpec(m.shape, lambda i: (0, 0)) for m in messages]
    pair = pl.BlockSpec((2, width, both), lambda i: (i, 0, 0))
    keep = pl.BlockSpec((rows, both), lambda i: (0, 0))
    return pl.pallas_call(
        functools.partial(shrink_kernel, len(messages), flag_lane),
        grid=(local // 2,),
        in_specs=[pl.BlockSpec(memory_space=pltpu.SMEM)] + whole + [pair, pair],
        out_specs=[keep, keep, pl.BlockSpec((8, 128), lambda i: (0, 0))],
        out_shape=[
            jax.ShapeDtypeStruct((rows, both), BF),
            jax.ShapeDtypeStruct((rows, both), BF),
            jax.ShapeDtypeStruct((8, 128), F32),
        ],
        scratch_shapes=[pltpu.VMEM((rows, both), F32), pltpu.VMEM((rows, both), F32)],
        compiler_params=pltpu.CompilerParams(vmem_limit_bytes=VMEM_LIMIT),
        name="shrink_rows",
    )(core, *messages, mine, sibling)


def grow_kernel(shares, sizes, core_ref, *refs):
    parts, place_ref, mine, sibling = refs[:shares], refs[shares], refs[shares + 1], refs[shares + 2]
    outs = refs[shares + 3:]
    summed = parts[0][...].astype(F32)
    for part in parts[1:]:
        summed = summed + part[...].astype(F32)
    shrunk = summed.astype(BF).astype(F32)
    place = place_ref[...].astype(F32)
    local, _, rank, columns = mine.shape
    core = core_ref[0]
    low = lax.broadcasted_iota(jnp.int32, shrunk.shape, 1) < rank
    turned = pltpu.roll(shrunk, rank, 1)
    result = []
    for j in range(2):
        twice = jnp.where(low, shrunk, turned) if j == 0 else jnp.where(low, turned, shrunk)
        total = None
        for weights, side in ((mine, core), (sibling, 1 - core)):
            left = []
            for e in range(0, local, 2):
                first = (side * local + e + 1).astype(F32)
                wanted = jnp.where(low, first, first + 1.0)
                left.append(jnp.where(place == wanted, twice, 0.0).astype(BF))
            right = weights[:, j].reshape(local * rank, columns)
            product = dot(jnp.concatenate(left, axis=1), right)
            total = product if total is None else total + product
        result.append((adapter_scale * total).astype(BF))
    start = 0
    for out, size in zip(outs, sizes):
        out[:, :columns] = result[0][start:start + size, :]
        out[:, columns:] = result[1][start:start + size, :]
        start += size


def grow(core, parts, place, mine, sibling, sizes):
    columns = mine.shape[3]
    vmem = pl.BlockSpec(memory_space=pltpu.VMEM)
    return pl.pallas_call(
        functools.partial(grow_kernel, len(parts), sizes),
        in_specs=[pl.BlockSpec(memory_space=pltpu.SMEM)] + [vmem] * (len(parts) + 3),
        out_specs=[vmem] * len(sizes),
        out_shape=[jax.ShapeDtypeStruct((s, 2 * columns), BF) for s in sizes],
        compiler_params=pltpu.CompilerParams(vmem_limit_bytes=VMEM_LIMIT),
        name="grow_rows",
    )(core, *parts, place, mine, sibling)


def block_kernel(steps, count, block_ref, tokens_ref, weight_ref, *refs):
    arrived, out, total = refs[:count], refs[count], refs[count + 1]
    step = pl.program_id(0)
    weight = jnp.swapaxes(weight_ref[...], 0, 1)
    columns = weight.shape[2]

    @pl.when(step == 0)
    def _():
        start = jnp.zeros(total.shape, F32)
        for one in arrived:
            start = start + one[...].astype(F32)
        total[...] = start

    for j in range(2):
        total[:, j * columns:(j + 1) * columns] += dot(tokens_ref[...], weight[j])

    @pl.when(step == steps - 1)
    def _():
        out[...] = total[...].astype(out.dtype)


def base_block(block, tokens, weight, columns, arrived, dtype, steps=4):
    rows, width = tokens.shape
    if columns % 128:
        part = lax.dynamic_slice_in_dim(weight, block[0] * columns, columns, 2)
        total = dot(tokens, part.reshape(width, 2 * columns))
        for one in arrived:
            total = total + one.astype(F32)
        return total.astype(dtype)
    deep = width // steps
    keep = pl.BlockSpec((rows, 2 * columns), lambda i, b: (0, 0))
    return pl.pallas_call(
        functools.partial(block_kernel, steps, len(arrived)),
        grid_spec=pltpu.PrefetchScalarGridSpec(
            num_scalar_prefetch=1,
            grid=(steps,),
            in_specs=[
                pl.BlockSpec((rows, deep), lambda i, b: (0, i)),
                pl.BlockSpec((deep, 2, columns), lambda i, b: (i, 0, b[0])),
            ]
            + [keep] * len(arrived),
            out_specs=keep,
            scratch_shapes=[pltpu.VMEM((rows, 2 * columns), F32)],
        ),
        out_shape=jax.ShapeDtypeStruct((rows, 2 * columns), dtype),
        compiler_params=pltpu.CompilerParams(vmem_limit_bytes=VMEM_LIMIT),
        name="base_block",
    )(block, tokens, weight, *arrived)


def finish_kernel(sizes, base_ref, spread_ref, *refs):
    updates, out = refs[:-1], refs[-1]
    total = base_ref[...]
    update_rows = jnp.zeros(total.shape, F32)
    start = 0
    for update, size in zip(updates, sizes):
        padded = round_up(size, 128)
        rows = update[...]
        if padded > size:
            rows = jnp.concatenate([rows, jnp.zeros((padded - size, rows.shape[1]), rows.dtype)], axis=0)
        update_rows = update_rows + dot(spread_ref[:, start:start + padded], rows)
        start += padded
    total = total + update_rows
    columns = out.shape[2]
    if columns % 128:
        out[:, 0, :] = total[:, :columns].astype(BF)
        out[:, 1, :] = total[:, columns:].astype(BF)
    else:
        both = jnp.stack([total[:, :columns], total[:, columns:]], axis=0).astype(BF)
        out[...] = jnp.swapaxes(both, 0, 1)


def finish(base, spread, updates):
    sizes = tuple(u.shape[0] for u in updates)
    rows, both = base.shape
    vmem = pl.BlockSpec(memory_space=pltpu.VMEM)
    return pl.pallas_call(
        functools.partial(finish_kernel, sizes),
        in_specs=[vmem] * (len(updates) + 2),
        out_specs=vmem,
        out_shape=jax.ShapeDtypeStruct((rows, 2, both // 2), BF),
        compiler_params=pltpu.CompilerParams(vmem_limit_bytes=VMEM_LIMIT),
        name="finish_rows",
    )(base, spread, *updates)


def exchange(array, axis, shift):
    size = lax.axis_size(axis)
    return lax.ppermute(array, axis, [(i, i ^ shift) for i in range(size)])


def after(array, *others):
    return lax.optimization_barrier((array,) + others)[0]


def bits(value):
    return bin(value).count("1")


def per_device(
    tokens,
    row_adapter_index,
    adapter_storage_slot,
    key_value_base_weight,
    adapter_down_weight,
    adapter_up_weight,
):
    row_count, width = tokens.shape
    local = adapter_down_weight.shape[0]
    groups = lax.axis_size("dp")
    blocks = lax.axis_size("tensor")
    experts = local * groups
    chips = groups // 2
    capacity = max(2, 2 * row_count // experts)
    chip_slots = 2 * local
    full = chip_slots * capacity

    me = lax.axis_index("dp").astype(jnp.int32)
    chip, core = (me // 2).reshape(1), (me % 2).reshape(1)
    adapters = row_adapter_index.reshape(1, row_count)
    slots = adapter_storage_slot.reshape(1, experts)
    flag_lane = width // 4 - 1

    down_sibling = exchange(adapter_down_weight, "dp", 1)
    up_sibling = exchange(adapter_up_weight, "dp", 1)

    near = [m for m in range(chips) if bits(m) <= 1]
    far = [m for m in range(chips) if bits(m) > 1]
    message = round_up(full + 1, 16)
    sizes, first_rows = (message,) * chips, (0,) * chips

    packed = pack(chip, adapters, slots, tokens, sizes, first_rows, chip_slots)
    sent, spread = list(packed[:-1]), packed[-1]
    arrived, returned = {0: sent[0]}, {}
    for m in near[1:]:
        arrived[m] = exchange(sent[m], "dp", 2 * m)

    columns = key_value_base_weight.shape[2] // blocks
    t = lax.axis_index("tensor").astype(jnp.int32)
    came = {}

    def summands(r):
        return [came[key] for key in sorted(came) if key[1] == r]

    def base_of(r, dtype):
        return base_block((t ^ r).reshape(1), tokens, key_value_base_weight, columns, summands(r), dtype)

    order = sorted(range(1, blocks), key=lambda r: (r & -r, -r))
    for r in order:
        low = r & -r
        if r == 2:
            for m in far:
                arrived[m] = exchange(after(sent[m], came_last), "dp", 2 * m)
        part = base_of(r, BF)
        came_last = part
        came[(low, r ^ low)] = exchange(part, "tensor", low)

    for part in (near, far):
        if not part:
            continue
        group = [arrived[m] for m in part]
        share, place, flag = shrink(core, group, adapter_down_weight, down_sibling, flag_lane)
        shares = [share] + [exchange(share, "tensor", z) for z in range(1, blocks)]
        grown = grow(core, shares, place, adapter_up_weight, up_sibling, tuple(sizes[m] for m in part))
        for m, update in zip(part, grown):
            returned[m] = update if m == 0 else exchange(update, "dp", 2 * m)
    base = base_of(0, F32)
    return finish(base, spread, [returned[m] for m in range(chips)])


def solution(mesh):
    placed = (
        P("dp", "tensor"),
        P("dp", None),
        P(),
        P("tensor", None, None),
        P("dp", "tensor", None),
        P("dp", None, None, "tensor"),
    )
    return jax.shard_map(
        per_device, mesh=mesh, in_specs=placed, out_specs=P("dp", None, "tensor"), check_vma=False
    )
```

```python
import functools

import jax
import jax.numpy as jnp
from jax import lax
from jax.experimental import pallas as pl
from jax.experimental.pallas import tpu as pltpu
from jax.sharding import PartitionSpec as P

adapter_scale = 0.5
BF = jnp.bfloat16
F32 = jnp.float32
VMEM_LIMIT = 26 * 1024 * 1024
COST = pl.CostEstimate(flops=1000, bytes_accessed=1000, transcendentals=0)


def round_up(value, unit):
    return (value + unit - 1) // unit * unit


def dot(a, b, contract=((1,), (0,))):
    return lax.dot_general(a, b, (contract, ((), ())), preferred_element_type=F32)


def pack_kernel(shape, place_ref, adapter_ref, slot_ref, tokens_ref, *refs):
    sizes, first_rows, chip_slots, flag_lane = shape
    messages = len(sizes)
    outs, spread_ref, pick = refs[:messages], refs[messages], refs[messages + 1]
    rows, width = tokens_ref.shape
    experts = slot_ref.shape[1]
    offsets = [sum(round_up(s, 128) for s in sizes[:m]) for m in range(messages)]

    @pl.when(pl.program_id(0) == 0)
    def _():
        named = (lax.broadcasted_iota(jnp.int32, (experts, rows), 0) == adapter_ref[...]).astype(BF)
        slots = jnp.broadcast_to(slot_ref[...].astype(F32), (16, experts)).astype(BF)
        slot = dot(slots, named)[0:1, :].astype(jnp.int32)
        shift = (slot // chip_slots) ^ place_ref[0]
        within = (slot % chip_slots + 1).astype(F32)
        lanes = round_up(messages, 16)
        goes = lax.broadcasted_iota(jnp.int32, (lanes, rows), 0) == shift
        earlier = lax.broadcasted_iota(jnp.int32, (rows, rows), 0) < lax.broadcasted_iota(jnp.int32, (rows, rows), 1)
        goes_f = goes.astype(F32)
        rank = dot(goes_f.astype(BF), earlier.astype(F32).astype(BF))
        position = jnp.sum(rank * goes_f, axis=0, keepdims=True).astype(jnp.int32)
        counts = jnp.sum(goes_f, axis=1, keepdims=True)
        sub = lax.broadcasted_iota(jnp.int32, (lanes, 1), 0)
        limit = jnp.zeros((lanes, 1), F32)
        for m in range(messages):
            limit = jnp.where(sub == m, F32(first_rows[m] + sizes[m] - 1), limit)
        over = jnp.max(jnp.where((sub < messages) & (counts > limit), 1.0, 0.0), axis=0, keepdims=True)
        key = jnp.broadcast_to(position + shift * 65536, (8, rows))
        key_column = key.astype(F32).T[:, 0:1].astype(jnp.int32)
        within8 = jnp.broadcast_to(within, (16, rows)).astype(BF)
        for m in range(messages):
            padded = round_up(sizes[m], 128)
            target = lax.broadcasted_iota(jnp.int32, (padded, rows), 0)
            hit = (target + first_rows[m] == position) & (shift == m) & (target < sizes[m] - 1)
            chosen = hit.astype(F32).astype(BF)
            pick[offsets[m]:offsets[m] + padded, :] = chosen
            lane_target = lax.broadcasted_iota(jnp.int32, (rows, padded), 1)
            back = (lane_target == key_column - first_rows[m] - m * 65536) & (lane_target < sizes[m] - 1)
            spread_ref[:, offsets[m]:offsets[m] + padded] = back.astype(F32).astype(BF)
            places = dot(within8, chosen, ((1,), (1,)))[0:1, :]
            if padded < width:
                places = jnp.concatenate([places, jnp.zeros((1, width - padded), F32)], axis=1)
            lane = lax.broadcasted_iota(jnp.int32, (1, width), 1)
            places = jnp.where(lane == flag_lane, over, places)
            body = dot(chosen, tokens_ref[...])[:sizes[m], :]
            row = lax.broadcasted_iota(jnp.int32, (sizes[m], 1), 0)
            outs[m][...] = jnp.where(row == sizes[m] - 1, places, body).astype(BF)

    @pl.when(pl.program_id(0) > 0)
    def _():
        for m in range(messages):
            outs[m][...] = dot(pick[offsets[m]:offsets[m] + sizes[m], :], tokens_ref[...]).astype(BF)


def pack(chip, adapters, slots, tokens, sizes, first_rows, chip_slots, steps=4):
    rows, width = tokens.shape
    block = width // steps
    spread = sum(round_up(s, 128) for s in sizes)
    return pl.pallas_call(
        functools.partial(pack_kernel, (sizes, first_rows, chip_slots, block - 1)),
        grid=(steps,),
        in_specs=[
            pl.BlockSpec(memory_space=pltpu.SMEM),
            pl.BlockSpec((1, rows), lambda i: (0, 0)),
            pl.BlockSpec((1, slots.shape[1]), lambda i: (0, 0)),
            pl.BlockSpec((rows, block), lambda i: (0, i)),
        ],
        out_specs=[pl.BlockSpec((s, block), lambda i: (0, i)) for s in sizes]
        + [pl.BlockSpec((rows, spread), lambda i: (0, 0))],
        out_shape=[jax.ShapeDtypeStruct((s, width), BF) for s in sizes] + [jax.ShapeDtypeStruct((rows, spread), BF)],
        scratch_shapes=[pltpu.VMEM((spread, rows), BF)],
        cost_estimate=COST,
        compiler_params=pltpu.CompilerParams(vmem_limit_bytes=VMEM_LIMIT),
        name="pack_rows",
    )(chip, adapters, slots, tokens)


def shrink_kernel(count, carried, flag_lane, core_ref, *refs):
    messages, (mine, sibling) = refs[:count], refs[count:count + 2]
    carry, refs = refs[count + 2:count + 2 + carried], refs[count + 2 + carried:]
    out, place_out, flag_out, total, places = refs
    kept = carry[0].shape[0] if carried else 0
    step = pl.program_id(0)
    local = 2 * pl.num_programs(0)
    sizes = [m.shape[0] for m in messages]

    @pl.when(step == 0)
    def _():
        flag = jnp.zeros((1, 1), F32)
        start = 0
        for m, size in zip(messages, sizes):
            padded = round_up(size, 128)
            tail = m[size - 16:size, 0:padded].astype(F32)[15:16, :]
            same = lax.broadcasted_iota(jnp.int32, (size, padded), 0) == lax.broadcasted_iota(jnp.int32, (size, padded), 1)
            column = jnp.sum(jnp.where(same, tail, 0.0), axis=1, keepdims=True)
            places[start:start + size, :] = jnp.broadcast_to(column, (size, 128))
            block = m[size - 16:size, flag_lane - 127:flag_lane + 1].astype(F32)[15:16, :]
            last = lax.broadcasted_iota(jnp.int32, (1, 128), 1) == 127
            flag = jnp.maximum(flag, jnp.max(jnp.where(last, block, 0.0), axis=1, keepdims=True))
            start += size
        place_out[kept:, :] = places[...].astype(BF)
        if carried:
            out[:kept, :] = carry[0][...]
            place_out[:kept, :] = carry[1][...]
            flag = jnp.maximum(flag, carry[2][0:1, 0:1])
        flag_out[...] = jnp.broadcast_to(flag, (8, 128))
        total[...] = jnp.zeros_like(total)

    rows = messages[0][...] if count == 1 else jnp.concatenate([m[...] for m in messages], axis=0)
    place = places[...]
    core = core_ref[0]
    for weights, side in ((mine, core), (sibling, 1 - core)):
        product = dot(rows, jnp.concatenate([weights[0], weights[1]], axis=1))
        first = (side * local + 2 * step + 1).astype(F32)
        total[...] += jnp.where(place == first, product[:, :128], 0.0) + jnp.where(
            place == first + 1.0, product[:, 128:], 0.0
        )

    @pl.when(step == pl.num_programs(0) - 1)
    def _():
        out[kept:, :] = total[...].astype(BF)


def shrink(core, messages, mine, sibling, flag_lane, carry=()):
    local, width, both = mine.shape
    rows = sum(m.shape[0] for m in messages)
    whole = [pl.BlockSpec(m.shape, lambda i: (0, 0)) for m in messages]
    pair = pl.BlockSpec((2, width, both), lambda i: (i, 0, 0))
    every = rows + (carry[0].shape[0] if carry else 0)
    keep = pl.BlockSpec((every, both), lambda i: (0, 0))
    whole_carry = [pl.BlockSpec(c.shape, lambda i: (0, 0)) for c in carry]
    return pl.pallas_call(
        functools.partial(shrink_kernel, len(messages), len(carry), flag_lane),
        grid=(local // 2,),
        in_specs=[pl.BlockSpec(memory_space=pltpu.SMEM)] + whole + [pair, pair] + whole_carry,
        out_specs=[keep, keep, pl.BlockSpec((8, 128), lambda i: (0, 0))],
        out_shape=[
            jax.ShapeDtypeStruct((every, both), BF),
            jax.ShapeDtypeStruct((every, both), BF),
            jax.ShapeDtypeStruct((8, 128), F32),
        ],
        scratch_shapes=[pltpu.VMEM((rows, both), F32), pltpu.VMEM((rows, both), F32)],
        cost_estimate=COST,
        compiler_params=pltpu.CompilerParams(vmem_limit_bytes=VMEM_LIMIT),
        name="shrink_rows",
    )(core, *messages, mine, sibling, *carry)


def grow_kernel(shares, sizes, core_ref, *refs):
    parts, place_ref, mine, sibling = refs[:shares], refs[shares], refs[shares + 1], refs[shares + 2]
    outs = refs[shares + 3:]
    summed = parts[0][...].astype(F32)
    for part in parts[1:]:
        summed = summed + part[...].astype(F32)
    shrunk = summed.astype(BF).astype(F32)
    place = place_ref[...].astype(F32)
    local, _, rank, columns = mine.shape
    core = core_ref[0]
    low = lax.broadcasted_iota(jnp.int32, shrunk.shape, 1) < rank
    turned = pltpu.roll(shrunk, rank, 1)
    result = []
    for j in range(2):
        twice = jnp.where(low, shrunk, turned) if j == 0 else jnp.where(low, turned, shrunk)
        total = None
        for weights, side in ((mine, core), (sibling, 1 - core)):
            left = []
            for e in range(0, local, 2):
                first = (side * local + e + 1).astype(F32)
                wanted = jnp.where(low, first, first + 1.0)
                left.append(jnp.where(place == wanted, twice, 0.0).astype(BF))
            right = weights[:, j].reshape(local * rank, columns)
            product = dot(jnp.concatenate(left, axis=1), right)
            total = product if total is None else total + product
        result.append((adapter_scale * total).astype(BF))
    start = 0
    for out, size in zip(outs, sizes):
        out[:, :columns] = result[0][start:start + size, :]
        out[:, columns:] = result[1][start:start + size, :]
        start += size


def grow(core, parts, place, mine, sibling, sizes):
    columns = mine.shape[3]
    vmem = pl.BlockSpec(memory_space=pltpu.VMEM)
    return pl.pallas_call(
        functools.partial(grow_kernel, len(parts), sizes),
        in_specs=[pl.BlockSpec(memory_space=pltpu.SMEM)] + [vmem] * (len(parts) + 3),
        out_specs=[vmem] * len(sizes),
        out_shape=[jax.ShapeDtypeStruct((s, 2 * columns), BF) for s in sizes],
        cost_estimate=COST,
        compiler_params=pltpu.CompilerParams(vmem_limit_bytes=VMEM_LIMIT),
        name="grow_rows",
    )(core, *parts, place, mine, sibling)


def base_kernel(steps, blocks, place_ref, tokens_ref, weight_ref, *refs):
    outs, total = refs[:blocks], refs[blocks]
    step = pl.program_id(0)
    weight = jnp.swapaxes(weight_ref[...], 0, 1)
    columns = total.shape[2] // blocks
    for j in range(2):
        product = dot(tokens_ref[...], weight[j])

        @pl.when(step == 0)
        def _():
            total[j] = product

        @pl.when(step > 0)
        def _():
            total[j] += product

    @pl.when(step == steps - 1)
    def _():
        for r, out in enumerate(outs):
            start = pl.multiple_of((place_ref[0] ^ r) * columns, columns)
            for j in range(2):
                out[:, j * columns:(j + 1) * columns] = total[j, :, pl.ds(start, columns)].astype(out.dtype)


def base_parts(t, tokens, weight, blocks, steps=4):
    rows, width = tokens.shape
    columns = weight.shape[2] // blocks
    types = [BF if r % 2 else F32 for r in range(blocks)]
    if columns % 128:
        total = jnp.einsum("rd,djn->rjn", tokens, weight, preferred_element_type=F32)
        cut = [lax.dynamic_slice_in_dim(total, (t ^ r) * columns, columns, 2) for r in range(blocks)]
        return [c.reshape(rows, 2 * columns).astype(k) for c, k in zip(cut, types)]
    deep = width // steps
    return pl.pallas_call(
        functools.partial(base_kernel, steps, blocks),
        grid=(steps,),
        in_specs=[
            pl.BlockSpec(memory_space=pltpu.SMEM),
            pl.BlockSpec((rows, deep), lambda i: (0, i)),
            pl.BlockSpec((deep, 2, weight.shape[2]), lambda i: (i, 0, 0)),
        ],
        out_specs=[pl.BlockSpec((rows, 2 * columns), lambda i: (0, 0))] * blocks,
        out_shape=[jax.ShapeDtypeStruct((rows, 2 * columns), k) for k in types],
        scratch_shapes=[pltpu.VMEM((2, rows, weight.shape[2]), F32)],
        cost_estimate=COST,
        compiler_params=pltpu.CompilerParams(vmem_limit_bytes=VMEM_LIMIT),
        name="base_parts",
    )(t.reshape(1), tokens, weight)


def finish_kernel(sizes, count, *refs):
    bases, spread_ref, updates, out = refs[:count], refs[count], refs[count + 1:-1], refs[-1]
    total = bases[0][...]
    for base in bases[1:]:
        total = total + base[...].astype(F32)
    update_rows = jnp.zeros(total.shape, F32)
    start = 0
    for update, size in zip(updates, sizes):
        padded = round_up(size, 128)
        rows = update[...]
        if padded > size:
            rows = jnp.concatenate([rows, jnp.zeros((padded - size, rows.shape[1]), rows.dtype)], axis=0)
        update_rows = update_rows + dot(spread_ref[:, start:start + padded], rows)
        start += padded
    total = total + update_rows
    columns = out.shape[2]
    if columns % 128:
        out[:, 0, :] = total[:, :columns].astype(BF)
        out[:, 1, :] = total[:, columns:].astype(BF)
    else:
        both = jnp.stack([total[:, :columns], total[:, columns:]], axis=0).astype(BF)
        out[...] = jnp.swapaxes(both, 0, 1)


def finish(bases, spread, updates):
    sizes = tuple(u.shape[0] for u in updates)
    rows, both = bases[0].shape
    vmem = pl.BlockSpec(memory_space=pltpu.VMEM)
    return pl.pallas_call(
        functools.partial(finish_kernel, sizes, len(bases)),
        in_specs=[vmem] * (len(bases) + 1 + len(updates)),
        out_specs=vmem,
        out_shape=jax.ShapeDtypeStruct((rows, 2, both // 2), BF),
        cost_estimate=COST,
        compiler_params=pltpu.CompilerParams(vmem_limit_bytes=VMEM_LIMIT),
        name="finish_rows",
    )(*bases, spread, *updates)


def exchange(array, axis, shift):
    size = lax.axis_size(axis)
    return lax.ppermute(array, axis, [(i, i ^ shift) for i in range(size)])


def after(array, *others):
    return lax.optimization_barrier((array,) + others)[0]


def bits(value):
    return bin(value).count("1")


def per_device(
    tokens,
    row_adapter_index,
    adapter_storage_slot,
    key_value_base_weight,
    adapter_down_weight,
    adapter_up_weight,
):
    row_count, width = tokens.shape
    local = adapter_down_weight.shape[0]
    groups = lax.axis_size("dp")
    blocks = lax.axis_size("tensor")
    experts = local * groups
    chips = groups // 2
    capacity = max(2, 2 * row_count // experts)
    chip_slots = 2 * local
    full = chip_slots * capacity

    me = lax.axis_index("dp").astype(jnp.int32)
    chip, core = (me // 2).reshape(1), (me % 2).reshape(1)
    adapters = row_adapter_index.reshape(1, row_count)
    slots = adapter_storage_slot.reshape(1, experts)
    flag_lane = width // 4 - 1

    down_sibling = exchange(adapter_down_weight, "dp", 1)

    near = [m for m in range(chips) if bits(m) <= 1]
    far = [m for m in range(chips) if bits(m) > 1]
    message = round_up(full + 1, 16)
    sizes, first_rows = (message,) * chips, (0,) * chips

    packed = pack(chip, adapters, slots, tokens, sizes, first_rows, chip_slots)
    sent, spread = list(packed[:-1]), packed[-1]
    arrived, returned = {0: sent[0]}, {}
    for m in near[1:]:
        arrived[m] = exchange(sent[m], "dp", 2 * m)

    t = lax.axis_index("tensor").astype(jnp.int32)
    parts = base_parts(t, after(tokens, *sent), key_value_base_weight, blocks)
    came = {}

    def arrived_for(r):
        return [came[key] for key in sorted(came) if key[1] == r]

    for m in far:
        arrived[m] = exchange(after(sent[m], parts[0], down_sibling), "dp", 2 * m)
    for r in sorted(range(1, blocks), key=lambda r: (r & -r, -r)):
        low = r & -r
        part = parts[r]
        for one in arrived_for(r):
            part = part + one.astype(F32)
        came[(low, r ^ low)] = exchange(part.astype(BF), "tensor", low)

    own = after(sent[0], came[(1, blocks - 2)])
    carry = shrink(core, [own], adapter_down_weight, down_sibling, flag_lane)
    up_sibling = exchange(after(adapter_up_weight, down_sibling), "dp", 1)
    for part in (near, far):
        if not part:
            continue
        group = [arrived[m] for m in part if m]
        share, place, flag = shrink(
            core, group, adapter_down_weight, after(down_sibling, up_sibling), flag_lane, carry if part is near else ()
        )
        other = came[(1, 0)] if part is near else came[(blocks // 2, 0)]
        shares = [after(share, other)] + [exchange(share, "tensor", z) for z in range(1, blocks)]
        grown = grow(core, shares, place, adapter_up_weight, up_sibling, tuple(sizes[m] for m in part))
        for m, update in zip(part, grown):
            returned[m] = update if m == 0 else exchange(update, "dp", 2 * m)
    return finish([parts[0]] + arrived_for(0), spread, [returned[m] for m in range(chips)])


def solution(mesh):
    placed = (
        P("dp", "tensor"),
        P("dp", None),
        P(),
        P("tensor", None, None),
        P("dp", "tensor", None),
        P("dp", None, None, "tensor"),
    )
    return jax.shard_map(
        per_device, mesh=mesh, in_specs=placed, out_specs=P("dp", None, "tensor"), check_vma=False
    )
```

```python
import functools

import jax
import jax.numpy as jnp
from jax import lax
from jax.experimental import pallas as pl
from jax.experimental.pallas import tpu as pltpu
from jax.sharding import PartitionSpec as P

adapter_scale = 0.5
BF = jnp.bfloat16
F32 = jnp.float32
VMEM_LIMIT = 60 * 1024 * 1024
COST = pl.CostEstimate(flops=1000, bytes_accessed=1000, transcendentals=0)


def round_up(value, unit):
    return (value + unit - 1) // unit * unit


def dot(a, b, contract=((1,), (0,))):
    return lax.dot_general(a, b, (contract, ((), ())), preferred_element_type=F32)


def pack_kernel(shape, place_ref, adapter_ref, slot_ref, tokens_ref, *refs):
    sizes, first_rows, chip_slots, flag_lane = shape
    messages = len(sizes)
    outs, spread_ref, pick = refs[:messages], refs[messages], refs[messages + 1]
    rows, width = tokens_ref.shape
    experts = slot_ref.shape[1]
    offsets = [sum(round_up(s, 128) for s in sizes[:m]) for m in range(messages)]

    @pl.when(pl.program_id(0) == 0)
    def _():
        named = (lax.broadcasted_iota(jnp.int32, (experts, rows), 0) == adapter_ref[...]).astype(BF)
        slots = jnp.broadcast_to(slot_ref[...].astype(F32), (16, experts)).astype(BF)
        slot = dot(slots, named)[0:1, :].astype(jnp.int32)
        shift = (slot // chip_slots) ^ place_ref[0]
        within = (slot % chip_slots + 1).astype(F32)
        lanes = round_up(messages, 16)
        goes = lax.broadcasted_iota(jnp.int32, (lanes, rows), 0) == shift
        earlier = lax.broadcasted_iota(jnp.int32, (rows, rows), 0) < lax.broadcasted_iota(jnp.int32, (rows, rows), 1)
        goes_f = goes.astype(F32)
        rank = dot(goes_f.astype(BF), earlier.astype(F32).astype(BF))
        position = jnp.sum(rank * goes_f, axis=0, keepdims=True).astype(jnp.int32)
        counts = jnp.sum(goes_f, axis=1, keepdims=True)
        sub = lax.broadcasted_iota(jnp.int32, (lanes, 1), 0)
        limit = jnp.zeros((lanes, 1), F32)
        for m in range(messages):
            limit = jnp.where(sub == m, F32(first_rows[m] + sizes[m] - 1), limit)
        over = jnp.max(jnp.where((sub < messages) & (counts > limit), 1.0, 0.0), axis=0, keepdims=True)
        key = jnp.broadcast_to(position + shift * 65536, (8, rows))
        key_column = key.astype(F32).T[:, 0:1].astype(jnp.int32)
        within8 = jnp.broadcast_to(within, (16, rows)).astype(BF)
        for m in range(messages):
            padded = round_up(sizes[m], 128)
            target = lax.broadcasted_iota(jnp.int32, (padded, rows), 0)
            hit = (target + first_rows[m] == position) & (shift == m) & (target < sizes[m] - 1)
            chosen = hit.astype(F32).astype(BF)
            pick[offsets[m]:offsets[m] + padded, :] = chosen
            lane_target = lax.broadcasted_iota(jnp.int32, (rows, padded), 1)
            back = (lane_target == key_column - first_rows[m] - m * 65536) & (lane_target < sizes[m] - 1)
            spread_ref[:, offsets[m]:offsets[m] + padded] = back.astype(F32).astype(BF)
            places = dot(within8, chosen, ((1,), (1,)))[0:1, :]
            if padded < width:
                places = jnp.concatenate([places, jnp.zeros((1, width - padded), F32)], axis=1)
            lane = lax.broadcasted_iota(jnp.int32, (1, width), 1)
            places = jnp.where(lane == flag_lane, over, places)
            body = dot(chosen, tokens_ref[...])[:sizes[m], :]
            row = lax.broadcasted_iota(jnp.int32, (sizes[m], 1), 0)
            outs[m][...] = jnp.where(row == sizes[m] - 1, places, body).astype(BF)

    @pl.when(pl.program_id(0) > 0)
    def _():
        for m in range(messages):
            outs[m][...] = dot(pick[offsets[m]:offsets[m] + sizes[m], :], tokens_ref[...]).astype(BF)


def pack(chip, adapters, slots, tokens, sizes, first_rows, chip_slots, steps=4):
    rows, width = tokens.shape
    block = width // steps
    spread = sum(round_up(s, 128) for s in sizes)
    return pl.pallas_call(
        functools.partial(pack_kernel, (sizes, first_rows, chip_slots, block - 1)),
        grid=(steps,),
        in_specs=[
            pl.BlockSpec(memory_space=pltpu.SMEM),
            pl.BlockSpec((1, rows), lambda i: (0, 0)),
            pl.BlockSpec((1, slots.shape[1]), lambda i: (0, 0)),
            pl.BlockSpec((rows, block), lambda i: (0, i)),
        ],
        out_specs=[pl.BlockSpec((s, block), lambda i: (0, i)) for s in sizes]
        + [pl.BlockSpec((rows, spread), lambda i: (0, 0))],
        out_shape=[jax.ShapeDtypeStruct((s, width), BF) for s in sizes] + [jax.ShapeDtypeStruct((rows, spread), BF)],
        scratch_shapes=[pltpu.VMEM((spread, rows), BF)],
        cost_estimate=COST,
        compiler_params=pltpu.CompilerParams(vmem_limit_bytes=VMEM_LIMIT),
        name="pack_rows",
    )(chip, adapters, slots, tokens)


def shrink_kernel(count, carried, flag_lane, core_ref, *refs):
    messages, (mine, sibling) = refs[:count], refs[count:count + 2]
    carry, refs = refs[count + 2:count + 2 + carried], refs[count + 2 + carried:]
    out, place_out, flag_out, total, places = refs
    kept = carry[0].shape[0] if carried else 0
    step = pl.program_id(0)
    local = 2 * pl.num_programs(0)
    sizes = [m.shape[0] for m in messages]

    @pl.when(step == 0)
    def _():
        flag = jnp.zeros((1, 1), F32)
        start = 0
        for m, size in zip(messages, sizes):
            padded = round_up(size, 128)
            tail = m[size - 16:size, 0:padded].astype(F32)[15:16, :]
            same = lax.broadcasted_iota(jnp.int32, (size, padded), 0) == lax.broadcasted_iota(jnp.int32, (size, padded), 1)
            column = jnp.sum(jnp.where(same, tail, 0.0), axis=1, keepdims=True)
            places[start:start + size, :] = jnp.broadcast_to(column, (size, 128))
            block = m[size - 16:size, flag_lane - 127:flag_lane + 1].astype(F32)[15:16, :]
            last = lax.broadcasted_iota(jnp.int32, (1, 128), 1) == 127
            flag = jnp.maximum(flag, jnp.max(jnp.where(last, block, 0.0), axis=1, keepdims=True))
            start += size
        place_out[kept:, :] = places[...].astype(BF)
        if carried:
            out[:kept, :] = carry[0][...]
            place_out[:kept, :] = carry[1][...]
            flag = jnp.maximum(flag, carry[2][0:1, 0:1])
        flag_out[...] = jnp.broadcast_to(flag, (8, 128))
        total[...] = jnp.zeros_like(total)

    rows = messages[0][...] if count == 1 else jnp.concatenate([m[...] for m in messages], axis=0)
    place = places[...]
    core = core_ref[0]
    for weights, side in ((mine, core), (sibling, 1 - core)):
        product = dot(rows, jnp.concatenate([weights[0], weights[1]], axis=1))
        first = (side * local + 2 * step + 1).astype(F32)
        total[...] += jnp.where(place == first, product[:, :128], 0.0) + jnp.where(
            place == first + 1.0, product[:, 128:], 0.0
        )

    @pl.when(step == pl.num_programs(0) - 1)
    def _():
        out[kept:, :] = total[...].astype(BF)


def shrink(core, messages, mine, sibling, flag_lane, carry=()):
    local, width, both = mine.shape
    rows = sum(m.shape[0] for m in messages)
    whole = [pl.BlockSpec(m.shape, lambda i: (0, 0)) for m in messages]
    pair = pl.BlockSpec((2, width, both), lambda i: (i, 0, 0))
    every = rows + (carry[0].shape[0] if carry else 0)
    keep = pl.BlockSpec((every, both), lambda i: (0, 0))
    whole_carry = [pl.BlockSpec(c.shape, lambda i: (0, 0)) for c in carry]
    return pl.pallas_call(
        functools.partial(shrink_kernel, len(messages), len(carry), flag_lane),
        grid=(local // 2,),
        in_specs=[pl.BlockSpec(memory_space=pltpu.SMEM)] + whole + [pair, pair] + whole_carry,
        out_specs=[keep, keep, pl.BlockSpec((8, 128), lambda i: (0, 0))],
        out_shape=[
            jax.ShapeDtypeStruct((every, both), BF),
            jax.ShapeDtypeStruct((every, both), BF),
            jax.ShapeDtypeStruct((8, 128), F32),
        ],
        scratch_shapes=[pltpu.VMEM((rows, both), F32), pltpu.VMEM((rows, both), F32)],
        cost_estimate=COST,
        compiler_params=pltpu.CompilerParams(vmem_limit_bytes=VMEM_LIMIT),
        name="shrink_rows",
    )(core, *messages, mine, sibling, *carry)


def grow_kernel(shares, sizes, core_ref, *refs):
    parts, place_ref, mine, sibling = refs[:shares], refs[shares], refs[shares + 1], refs[shares + 2]
    outs = refs[shares + 3:]
    summed = parts[0][...].astype(F32)
    for part in parts[1:]:
        summed = summed + part[...].astype(F32)
    shrunk = summed.astype(BF).astype(F32)
    place = place_ref[...].astype(F32)
    local, _, rank, columns = mine.shape
    core = core_ref[0]
    low = lax.broadcasted_iota(jnp.int32, shrunk.shape, 1) < rank
    turned = pltpu.roll(shrunk, rank, 1)
    result = []
    for j in range(2):
        twice = jnp.where(low, shrunk, turned) if j == 0 else jnp.where(low, turned, shrunk)
        total = None
        for weights, side in ((mine, core), (sibling, 1 - core)):
            left = []
            for e in range(0, local, 2):
                first = (side * local + e + 1).astype(F32)
                wanted = jnp.where(low, first, first + 1.0)
                left.append(jnp.where(place == wanted, twice, 0.0).astype(BF))
            right = weights[:, j].reshape(local * rank, columns)
            product = dot(jnp.concatenate(left, axis=1), right)
            total = product if total is None else total + product
        result.append((adapter_scale * total).astype(BF))
    start = 0
    for out, size in zip(outs, sizes):
        out[:, :columns] = result[0][start:start + size, :]
        out[:, columns:] = result[1][start:start + size, :]
        start += size


def grow(core, parts, place, mine, sibling, sizes):
    columns = mine.shape[3]
    vmem = pl.BlockSpec(memory_space=pltpu.VMEM)
    return pl.pallas_call(
        functools.partial(grow_kernel, len(parts), sizes),
        in_specs=[pl.BlockSpec(memory_space=pltpu.SMEM)] + [vmem] * (len(parts) + 3),
        out_specs=[vmem] * len(sizes),
        out_shape=[jax.ShapeDtypeStruct((s, 2 * columns), BF) for s in sizes],
        cost_estimate=COST,
        compiler_params=pltpu.CompilerParams(vmem_limit_bytes=VMEM_LIMIT),
        name="grow_rows",
    )(core, *parts, place, mine, sibling)


def base_kernel(steps, blocks, place_ref, tokens_ref, weight_ref, *refs):
    outs, total = refs[:blocks], refs[blocks]
    step = pl.program_id(0)
    weight = jnp.swapaxes(weight_ref[...], 0, 1)
    columns = total.shape[2] // blocks
    for j in range(2):
        product = dot(tokens_ref[...], weight[j])

        @pl.when(step == 0)
        def _():
            total[j] = product

        @pl.when(step > 0)
        def _():
            total[j] += product

    @pl.when(step == steps - 1)
    def _():
        for r, out in enumerate(outs):
            start = pl.multiple_of((place_ref[0] ^ r) * columns, columns)
            for j in range(2):
                out[:, j * columns:(j + 1) * columns] = total[j, :, pl.ds(start, columns)].astype(out.dtype)


def base_parts(t, tokens, weight, blocks, steps=4):
    rows, width = tokens.shape
    columns = weight.shape[2] // blocks
    types = [BF if r % 2 else F32 for r in range(blocks)]
    if columns % 128:
        total = jnp.einsum("rd,djn->rjn", tokens, weight, preferred_element_type=F32)
        cut = [lax.dynamic_slice_in_dim(total, (t ^ r) * columns, columns, 2) for r in range(blocks)]
        return [c.reshape(rows, 2 * columns).astype(k) for c, k in zip(cut, types)]
    deep = width // steps
    return pl.pallas_call(
        functools.partial(base_kernel, steps, blocks),
        grid=(steps,),
        in_specs=[
            pl.BlockSpec(memory_space=pltpu.SMEM),
            pl.BlockSpec((rows, deep), lambda i: (0, i)),
            pl.BlockSpec((deep, 2, weight.shape[2]), lambda i: (i, 0, 0)),
        ],
        out_specs=[pl.BlockSpec((rows, 2 * columns), lambda i: (0, 0))] * blocks,
        out_shape=[jax.ShapeDtypeStruct((rows, 2 * columns), k) for k in types],
        scratch_shapes=[pltpu.VMEM((2, rows, weight.shape[2]), F32)],
        cost_estimate=COST,
        compiler_params=pltpu.CompilerParams(vmem_limit_bytes=VMEM_LIMIT),
        name="base_parts",
    )(t.reshape(1), tokens, weight)


def finish_kernel(sizes, count, *refs):
    bases, spreads, out = refs[:count], refs[count:count + len(sizes)], refs[-1]
    updates = refs[count + len(sizes):-1]
    total = bases[0][...]
    for base in bases[1:]:
        total = total + base[...].astype(F32)
    update_rows = jnp.zeros(total.shape, F32)
    done = 0
    for spread, group in zip(spreads, sizes):
        start = 0
        for size in group:
            padded = round_up(size, 128)
            rows = updates[done][...]
            if padded > size:
                rows = jnp.concatenate([rows, jnp.zeros((padded - size, rows.shape[1]), rows.dtype)], axis=0)
            update_rows = update_rows + dot(spread[:, start:start + padded], rows)
            start += padded
            done += 1
    total = total + update_rows
    columns = out.shape[2]
    if columns % 128:
        out[:, 0, :] = total[:, :columns].astype(BF)
        out[:, 1, :] = total[:, columns:].astype(BF)
    else:
        both = jnp.stack([total[:, :columns], total[:, columns:]], axis=0).astype(BF)
        out[...] = jnp.swapaxes(both, 0, 1)


def finish(bases, spreads, groups):
    sizes = tuple(tuple(u.shape[0] for u in group) for group in groups)
    rows, both = bases[0].shape
    updates = [u for group in groups for u in group]
    vmem = pl.BlockSpec(memory_space=pltpu.VMEM)
    return pl.pallas_call(
        functools.partial(finish_kernel, sizes, len(bases)),
        in_specs=[vmem] * (len(bases) + len(spreads) + len(updates)),
        out_specs=vmem,
        out_shape=jax.ShapeDtypeStruct((rows, 2, both // 2), BF),
        cost_estimate=COST,
        compiler_params=pltpu.CompilerParams(vmem_limit_bytes=VMEM_LIMIT),
        name="finish_rows",
    )(*bases, *spreads, *updates)


def exchange(array, axis, shift):
    size = lax.axis_size(axis)
    return lax.ppermute(array, axis, [(i, i ^ shift) for i in range(size)])


def after(array, *others):
    return lax.optimization_barrier((array,) + others)[0]


def bits(value):
    return bin(value).count("1")


def per_device(
    tokens,
    row_adapter_index,
    adapter_storage_slot,
    key_value_base_weight,
    adapter_down_weight,
    adapter_up_weight,
):
    row_count, width = tokens.shape
    local = adapter_down_weight.shape[0]
    groups = lax.axis_size("dp")
    blocks = lax.axis_size("tensor")
    experts = local * groups
    chips = groups // 2
    capacity = max(2, 2 * row_count // experts)
    chip_slots = 2 * local
    full = chip_slots * capacity

    me = lax.axis_index("dp").astype(jnp.int32)
    chip, core = (me // 2).reshape(1), (me % 2).reshape(1)
    adapters = row_adapter_index.reshape(1, row_count)
    slots = adapter_storage_slot.reshape(1, experts)
    flag_lane = width // 4 - 1

    down_sibling = exchange(adapter_down_weight, "dp", 1)

    near = [m for m in range(chips) if bits(m) <= 1]
    far = [m for m in range(chips) if bits(m) > 1]
    whole, message = round_up(full + 1, 16), round_up(full * 11 // 16, 16)
    rest = round_up(full - message + 2, 16)
    sizes, first_rows = (whole,) + (message,) * (chips - 1), (0,) * chips

    packed = pack(chip, adapters, slots, tokens, sizes, first_rows, chip_slots)
    sent, spread = list(packed[:-1]), packed[-1]
    arrived, returned = {0: sent[0]}, {}
    for m in near[1:]:
        arrived[m] = exchange(sent[m], "dp", 2 * m)

    t = lax.axis_index("tensor").astype(jnp.int32)
    parts = base_parts(t, after(tokens, *sent), key_value_base_weight, blocks)
    came = {}

    def arrived_for(r):
        return [came[key] for key in sorted(came) if key[1] == r]

    carry = shrink(core, [after(sent[0], parts[0])], adapter_down_weight, down_sibling, flag_lane)
    up_sibling = exchange(after(adapter_up_weight, down_sibling), "dp", 1)
    near_done = [arrived[m] for m in near[1:]] + [carry[0]]
    for r in sorted(range(1, blocks), key=lambda r: (r & -r, -r)):
        low = r & -r
        part = parts[r]
        for one in arrived_for(r):
            part = part + one.astype(F32)
        if r == 1:
            part = after(part, *near_done)
        came[(low, r ^ low)] = exchange(part.astype(BF), "tensor", low)
    for m in far:
        arrived[m] = exchange(after(sent[m], *near_done), "dp", 2 * m)

    flags = []
    for part in (near, far):
        if not part:
            continue
        group = [arrived[m] for m in part if m]
        share, place, flag = shrink(
            core, group, adapter_down_weight, after(down_sibling, up_sibling), flag_lane, carry if part is near else ()
        )
        flags.append(flag)
        other = came[(1, 0)] if part is near else came[(blocks // 2, 0)]
        shares = [after(share, other)] + [exchange(share, "tensor", z) for z in range(1, blocks)]
        grown = grow(core, shares, place, adapter_up_weight, up_sibling, tuple(sizes[m] for m in part))
        for m, update in zip(part, grown):
            returned[m] = update if m == 0 else exchange(update, "dp", 2 * m)
    flag = functools.reduce(jnp.maximum, flags)
    flag = jnp.maximum(flag, exchange(flag, "dp", 1))
    bases = [parts[0]] + arrived_for(0)
    updates = [returned[m] for m in range(chips)]

    def as_is():
        return finish(bases, [spread], [updates])

    def second_round():
        later_sizes, later_rows = (16,) + (rest,) * (chips - 1), (full,) + (message - 1,) * (chips - 1)
        packed = pack(chip, adapters, slots, tokens, later_sizes, later_rows, chip_slots)
        group = [packed[0]] + [exchange(packed[m], "dp", 2 * m) for m in range(1, chips)]
        share, place, _ = shrink(core, group, adapter_down_weight, down_sibling, flag_lane)
        shares = [share] + [exchange(share, "tensor", z) for z in range(1, blocks)]
        grown = grow(core, shares, place, adapter_up_weight, up_sibling, later_sizes)
        back = [grown[0]] + [exchange(grown[m], "dp", 2 * m) for m in range(1, chips)]
        return finish(bases, [spread, packed[-1]], [updates, back])

    return lax.cond(flag[0, 0] > 0.0, second_round, as_is)


def solution(mesh):
    placed = (
        P("dp", "tensor"),
        P("dp", None),
        P(),
        P("tensor", None, None),
        P("dp", "tensor", None),
        P("dp", None, None, "tensor"),
    )
    return jax.shard_map(
        per_device, mesh=mesh, in_specs=placed, out_specs=P("dp", None, "tensor"), check_vma=False
    )
```

```python
import functools

import jax
import jax.numpy as jnp
from jax import lax
from jax.experimental import pallas as pl
from jax.experimental.pallas import tpu as pltpu
from jax.sharding import PartitionSpec as P

adapter_scale = 0.5
BF = jnp.bfloat16
F32 = jnp.float32
VMEM_LIMIT = 28 * 1024 * 1024
VMEM_MOST = 57 * 1024 * 1024
COST = pl.CostEstimate(flops=1000, bytes_accessed=1000, transcendentals=0)


def round_up(value, unit):
    return (value + unit - 1) // unit * unit


def dot(a, b, contract=((1,), (0,))):
    return lax.dot_general(a, b, (contract, ((), ())), preferred_element_type=F32)


def pack_kernel(shape, place_ref, adapter_ref, slot_ref, tokens_ref, *refs):
    sizes, first_rows, chip_slots, flag_lane = shape
    messages = len(sizes)
    outs, spread_ref, pick = refs[:messages], refs[messages], refs[messages + 1]
    rows, width = tokens_ref.shape
    experts = slot_ref.shape[1]
    offsets = [sum(round_up(s, 128) for s in sizes[:m]) for m in range(messages)]

    @pl.when(pl.program_id(0) == 0)
    def _():
        named = (lax.broadcasted_iota(jnp.int32, (experts, rows), 0) == adapter_ref[...]).astype(BF)
        slots = jnp.broadcast_to(slot_ref[...].astype(F32), (16, experts)).astype(BF)
        slot = dot(slots, named)[0:1, :].astype(jnp.int32)
        shift = (slot // chip_slots) ^ place_ref[0]
        within = (slot % chip_slots + 1).astype(F32)
        lanes = round_up(messages, 16)
        goes = lax.broadcasted_iota(jnp.int32, (lanes, rows), 0) == shift
        earlier = lax.broadcasted_iota(jnp.int32, (rows, rows), 0) < lax.broadcasted_iota(jnp.int32, (rows, rows), 1)
        goes_f = goes.astype(F32)
        rank = dot(goes_f.astype(BF), earlier.astype(F32).astype(BF))
        position = jnp.sum(rank * goes_f, axis=0, keepdims=True).astype(jnp.int32)
        counts = jnp.sum(goes_f, axis=1, keepdims=True)
        sub = lax.broadcasted_iota(jnp.int32, (lanes, 1), 0)
        limit = jnp.zeros((lanes, 1), F32)
        for m in range(messages):
            limit = jnp.where(sub == m, F32(first_rows[m] + sizes[m] - 1), limit)
        over = jnp.max(jnp.where((sub < messages) & (counts > limit), 1.0, 0.0), axis=0, keepdims=True)
        key = jnp.broadcast_to(position + shift * 65536, (8, rows))
        key_column = key.astype(F32).T[:, 0:1].astype(jnp.int32)
        within8 = jnp.broadcast_to(within, (16, rows)).astype(BF)
        for m in range(messages):
            padded = round_up(sizes[m], 128)
            target = lax.broadcasted_iota(jnp.int32, (padded, rows), 0)
            hit = (target + first_rows[m] == position) & (shift == m) & (target < sizes[m] - 1)
            chosen = hit.astype(F32).astype(BF)
            pick[offsets[m]:offsets[m] + padded, :] = chosen
            lane_target = lax.broadcasted_iota(jnp.int32, (rows, padded), 1)
            back = (lane_target == key_column - first_rows[m] - m * 65536) & (lane_target < sizes[m] - 1)
            spread_ref[:, offsets[m]:offsets[m] + padded] = back.astype(F32).astype(BF)
            places = dot(within8, chosen, ((1,), (1,)))[0:1, :]
            if padded < width:
                places = jnp.concatenate([places, jnp.zeros((1, width - padded), F32)], axis=1)
            lane = lax.broadcasted_iota(jnp.int32, (1, width), 1)
            places = jnp.where(lane == flag_lane, over, places)
            body = dot(chosen, tokens_ref[...])[:sizes[m], :]
            row = lax.broadcasted_iota(jnp.int32, (sizes[m], 1), 0)
            outs[m][...] = jnp.where(row == sizes[m] - 1, places, body).astype(BF)

    @pl.when(pl.program_id(0) > 0)
    def _():
        for m in range(messages):
            outs[m][...] = dot(pick[offsets[m]:offsets[m] + sizes[m], :], tokens_ref[...]).astype(BF)


def pack(chip, adapters, slots, tokens, sizes, first_rows, chip_slots, steps=4):
    rows, width = tokens.shape
    block = width // steps
    spread = sum(round_up(s, 128) for s in sizes)
    return pl.pallas_call(
        functools.partial(pack_kernel, (sizes, first_rows, chip_slots, block - 1)),
        grid=(steps,),
        in_specs=[
            pl.BlockSpec(memory_space=pltpu.SMEM),
            pl.BlockSpec((1, rows), lambda i: (0, 0)),
            pl.BlockSpec((1, slots.shape[1]), lambda i: (0, 0)),
            pl.BlockSpec((rows, block), lambda i: (0, i)),
        ],
        out_specs=[pl.BlockSpec((s, block), lambda i: (0, i)) for s in sizes]
        + [pl.BlockSpec((rows, spread), lambda i: (0, 0))],
        out_shape=[jax.ShapeDtypeStruct((s, width), BF) for s in sizes] + [jax.ShapeDtypeStruct((rows, spread), BF)],
        scratch_shapes=[pltpu.VMEM((spread, rows), BF)],
        cost_estimate=COST,
        compiler_params=pltpu.CompilerParams(vmem_limit_bytes=VMEM_LIMIT),
        name="pack_rows",
    )(chip, adapters, slots, tokens)


def shrink_kernel(count, carried, flag_lane, core_ref, *refs):
    messages, (mine, sibling) = refs[:count], refs[count:count + 2]
    carry, refs = refs[count + 2:count + 2 + carried], refs[count + 2 + carried:]
    out, place_out, flag_out, total, places = refs
    kept = carry[0].shape[0] if carried else 0
    step = pl.program_id(0)
    local = 2 * pl.num_programs(0)
    sizes = [m.shape[0] for m in messages]

    @pl.when(step == 0)
    def _():
        flag = jnp.zeros((1, 1), F32)
        start = 0
        for m, size in zip(messages, sizes):
            padded = round_up(size, 128)
            tail = m[size - 16:size, 0:padded].astype(F32)[15:16, :]
            same = lax.broadcasted_iota(jnp.int32, (size, padded), 0) == lax.broadcasted_iota(jnp.int32, (size, padded), 1)
            column = jnp.sum(jnp.where(same, tail, 0.0), axis=1, keepdims=True)
            places[start:start + size, :] = jnp.broadcast_to(column, (size, 128))
            block = m[size - 16:size, flag_lane - 127:flag_lane + 1].astype(F32)[15:16, :]
            last = lax.broadcasted_iota(jnp.int32, (1, 128), 1) == 127
            flag = jnp.maximum(flag, jnp.max(jnp.where(last, block, 0.0), axis=1, keepdims=True))
            start += size
        place_out[kept:, :] = places[...].astype(BF)
        if carried:
            out[:kept, :] = carry[0][...]
            place_out[:kept, :] = carry[1][...]
            flag = jnp.maximum(flag, carry[2][0:1, 0:1])
        flag_out[...] = jnp.broadcast_to(flag, (8, 128))
        total[...] = jnp.zeros_like(total)

    rows = messages[0][...] if count == 1 else jnp.concatenate([m[...] for m in messages], axis=0)
    place = places[...]
    core = core_ref[0]
    for weights, side in ((mine, core), (sibling, 1 - core)):
        product = dot(rows, jnp.concatenate([weights[0], weights[1]], axis=1))
        first = (side * local + 2 * step + 1).astype(F32)
        total[...] += jnp.where(place == first, product[:, :128], 0.0) + jnp.where(
            place == first + 1.0, product[:, 128:], 0.0
        )

    @pl.when(step == pl.num_programs(0) - 1)
    def _():
        out[kept:, :] = total[...].astype(BF)


def shrink(core, messages, mine, sibling, flag_lane, carry=()):
    local, width, both = mine.shape
    rows = sum(m.shape[0] for m in messages)
    whole = [pl.BlockSpec(m.shape, lambda i: (0, 0)) for m in messages]
    pair = pl.BlockSpec((2, width, both), lambda i: (i, 0, 0))
    every = rows + (carry[0].shape[0] if carry else 0)
    keep = pl.BlockSpec((every, both), lambda i: (0, 0))
    whole_carry = [pl.BlockSpec(c.shape, lambda i: (0, 0)) for c in carry]
    return pl.pallas_call(
        functools.partial(shrink_kernel, len(messages), len(carry), flag_lane),
        grid=(local // 2,),
        in_specs=[pl.BlockSpec(memory_space=pltpu.SMEM)] + whole + [pair, pair] + whole_carry,
        out_specs=[keep, keep, pl.BlockSpec((8, 128), lambda i: (0, 0))],
        out_shape=[
            jax.ShapeDtypeStruct((every, both), BF),
            jax.ShapeDtypeStruct((every, both), BF),
            jax.ShapeDtypeStruct((8, 128), F32),
        ],
        scratch_shapes=[pltpu.VMEM((rows, both), F32), pltpu.VMEM((rows, both), F32)],
        cost_estimate=pl.CostEstimate(
            flops=8 * rows * width * local * both, bytes_accessed=8 * width * local * both, transcendentals=0
        ),
        compiler_params=pltpu.CompilerParams(vmem_limit_bytes=VMEM_LIMIT),
        name="shrink_rows",
    )(core, *messages, mine, sibling, *carry)


def grow_kernel(shares, sizes, core_ref, *refs):
    parts, place_ref, mine, sibling = refs[:shares], refs[shares], refs[shares + 1], refs[shares + 2]
    outs = refs[shares + 3:]
    summed = parts[0][...].astype(F32)
    for part in parts[1:]:
        summed = summed + part[...].astype(F32)
    shrunk = summed.astype(BF).astype(F32)
    place = place_ref[...].astype(F32)
    local, _, rank, columns = mine.shape
    core = core_ref[0]
    low = lax.broadcasted_iota(jnp.int32, shrunk.shape, 1) < rank
    turned = pltpu.roll(shrunk, rank, 1)
    result = []
    for j in range(2):
        twice = jnp.where(low, shrunk, turned) if j == 0 else jnp.where(low, turned, shrunk)
        total = None
        for weights, side in ((mine, core), (sibling, 1 - core)):
            left = []
            for e in range(0, local, 2):
                first = (side * local + e + 1).astype(F32)
                wanted = jnp.where(low, first, first + 1.0)
                left.append(jnp.where(place == wanted, twice, 0.0).astype(BF))
            right = weights[:, j].reshape(local * rank, columns)
            product = dot(jnp.concatenate(left, axis=1), right)
            total = product if total is None else total + product
        result.append((adapter_scale * total).astype(BF))
    start = 0
    for out, size in zip(outs, sizes):
        out[:, :columns] = result[0][start:start + size, :]
        out[:, columns:] = result[1][start:start + size, :]
        start += size


def grow(core, parts, place, mine, sibling, sizes):
    columns = mine.shape[3]
    vmem = pl.BlockSpec(memory_space=pltpu.VMEM)
    return pl.pallas_call(
        functools.partial(grow_kernel, len(parts), sizes),
        in_specs=[pl.BlockSpec(memory_space=pltpu.SMEM)] + [vmem] * (len(parts) + 3),
        out_specs=[vmem] * len(sizes),
        out_shape=[jax.ShapeDtypeStruct((s, 2 * columns), BF) for s in sizes],
        cost_estimate=COST,
        compiler_params=pltpu.CompilerParams(vmem_limit_bytes=VMEM_LIMIT),
        name="grow_rows",
    )(core, *parts, place, mine, sibling)


def base_kernel(steps, shifts, count, place_ref, weight_ref, tokens_ref, *refs):
    arrived, outs, total = refs[:count], refs[count:-1], refs[-1]
    columns = outs[0].shape[1] // 2
    rows, width = tokens_ref.shape
    deep = width // steps
    read = total.shape[2]
    chosen = (place_ref[0] ^ shifts[0]) if len(shifts) == 1 else 0
    total[...] = jnp.zeros(total.shape, F32)

    def body(tokens, weight):
        turned = jnp.swapaxes(weight[...], 0, 1)
        for j in range(2):
            total[j] += dot(tokens[...], turned[j])

    pltpu.emit_pipeline(
        body,
        grid=(steps,),
        in_specs=[
            pl.BlockSpec((rows, deep), lambda i: (0, i)),
            pl.BlockSpec((deep, 2, read), lambda i: (i, 0, chosen)),
        ],
    )(tokens_ref, weight_ref)
    for r, out in zip(shifts, outs):
        start = 0 if len(shifts) == 1 else pl.multiple_of((place_ref[0] ^ r) * columns, columns)
        for j in range(2):
            part = total[j, :, pl.ds(start, columns)]
            for one in arrived:
                part = part + one[:, j * columns:(j + 1) * columns].astype(F32)
            out[:, j * columns:(j + 1) * columns] = part.astype(out.dtype)


def base_parts(t, tokens, weight, blocks, shifts, steps, arrived=(), dtype=None):
    rows, width = tokens.shape
    columns = weight.shape[2] // blocks
    types = [dtype or (BF if r % 2 else F32) for r in shifts]
    if columns % 128:
        cut = [lax.dynamic_slice_in_dim(weight, (t ^ r) * columns, columns, 2) for r in shifts]
        cut = [dot(tokens, c.reshape(width, 2 * columns)) for c in cut]
        for one in arrived:
            cut = [c + one.astype(F32) for c in cut]
        return [c.astype(k) for c, k in zip(cut, types)]
    read = columns if len(shifts) == 1 else columns * blocks
    vmem = pl.BlockSpec(memory_space=pltpu.VMEM)
    hbm = pl.BlockSpec(memory_space=pltpu.HBM)
    return pl.pallas_call(
        functools.partial(base_kernel, steps, shifts, len(arrived)),
        in_specs=[pl.BlockSpec(memory_space=pltpu.SMEM), hbm, hbm] + [vmem] * len(arrived),
        out_specs=[vmem] * len(shifts),
        scratch_shapes=[pltpu.VMEM((2, rows, read), F32)],
        out_shape=[jax.ShapeDtypeStruct((rows, 2 * columns), k) for k in types],
        cost_estimate=pl.CostEstimate(
            flops=16 * rows * width * read, bytes_accessed=8 * width * read, transcendentals=0
        ),
        compiler_params=pltpu.CompilerParams(vmem_limit_bytes=VMEM_MOST),
        name="base_parts",
    )(t.reshape(1), weight, tokens, *arrived)


def finish_kernel(sizes, count, *refs):
    bases, spreads, out = refs[:count], refs[count:count + len(sizes)], refs[-1]
    updates = refs[count + len(sizes):-1]
    total = bases[0][...]
    for base in bases[1:]:
        total = total + base[...].astype(F32)
    update_rows = jnp.zeros(total.shape, F32)
    done = 0
    for spread, group in zip(spreads, sizes):
        start = 0
        for size in group:
            padded = round_up(size, 128)
            rows = updates[done][...]
            if padded > size:
                rows = jnp.concatenate([rows, jnp.zeros((padded - size, rows.shape[1]), rows.dtype)], axis=0)
            update_rows = update_rows + dot(spread[:, start:start + padded], rows)
            start += padded
            done += 1
    total = total + update_rows
    columns = out.shape[2]
    if columns % 128:
        out[:, 0, :] = total[:, :columns].astype(BF)
        out[:, 1, :] = total[:, columns:].astype(BF)
    else:
        both = jnp.stack([total[:, :columns], total[:, columns:]], axis=0).astype(BF)
        out[...] = jnp.swapaxes(both, 0, 1)


def finish(bases, spreads, groups):
    sizes = tuple(tuple(u.shape[0] for u in group) for group in groups)
    rows, both = bases[0].shape
    updates = [u for group in groups for u in group]
    block = rows // 4
    return pl.pallas_call(
        functools.partial(finish_kernel, sizes, len(bases)),
        grid=(4,),
        in_specs=[pl.BlockSpec((block, x.shape[1]), lambda i: (i, 0)) for x in bases + spreads]
        + [pl.BlockSpec(u.shape, lambda i: (0, 0)) for u in updates],
        out_specs=pl.BlockSpec((block, 2, both // 2), lambda i: (i, 0, 0)),
        out_shape=jax.ShapeDtypeStruct((rows, 2, both // 2), BF),
        cost_estimate=COST,
        compiler_params=pltpu.CompilerParams(vmem_limit_bytes=VMEM_LIMIT),
        name="finish_rows",
    )(*bases, *spreads, *updates)


def exchange(array, axis, shift):
    size = lax.axis_size(axis)
    return lax.ppermute(array, axis, [(i, i ^ shift) for i in range(size)])


def after(array, *others):
    return lax.optimization_barrier((array,) + others)[0]


def bits(value):
    return bin(value).count("1")


def per_device(
    tokens,
    row_adapter_index,
    adapter_storage_slot,
    key_value_base_weight,
    adapter_down_weight,
    adapter_up_weight,
):
    row_count, width = tokens.shape
    local = adapter_down_weight.shape[0]
    groups = lax.axis_size("dp")
    blocks = lax.axis_size("tensor")
    experts = local * groups
    chips = groups // 2
    capacity = max(2, 2 * row_count // experts)
    chip_slots = 2 * local
    full = chip_slots * capacity

    me = lax.axis_index("dp").astype(jnp.int32)
    chip, core = (me // 2).reshape(1), (me % 2).reshape(1)
    adapters = row_adapter_index.reshape(1, row_count)
    slots = adapter_storage_slot.reshape(1, experts)
    flag_lane = width // 4 - 1

    down_sibling = exchange(adapter_down_weight, "dp", 1)

    near = [m for m in range(chips) if bits(m) <= 1]
    far = [m for m in range(chips) if bits(m) > 1]
    message = round_up(full * 11 // 16, 16)
    rest = round_up(full - message + 2, 16)
    sizes, first_rows = (message,) * chips, (0,) * chips

    t = lax.axis_index("tensor").astype(jnp.int32)
    first_shift = blocks - 1
    parts = {first_shift: base_parts(t, tokens, key_value_base_weight, blocks, [first_shift], 2)[0]}
    came = {}
    came[(1, first_shift ^ 1)] = exchange(parts[first_shift], "tensor", 1)

    packed = pack(chip, adapters, slots, after(tokens, parts[first_shift]), sizes, first_rows, chip_slots)
    sent, spread = list(packed[:-1]), packed[-1]
    arrived, returned = {0: sent[0]}, {}
    for m in near[1:]:
        arrived[m] = exchange(sent[m], "dp", 2 * m)

    plain = [r for r in range(blocks - 1) if r % 2 or r == 0]
    late_tokens = after(tokens, *sent)
    parts.update(zip(plain, base_parts(t, late_tokens, key_value_base_weight, blocks, plain, 4)))

    def arrived_for(r):
        return [came[key] for key in sorted(came) if key[1] == r]

    up_sibling = exchange(after(adapter_up_weight, down_sibling), "dp", 1)
    near_done = [arrived[m] for m in near[1:]]
    for r in sorted(range(1, blocks - 1), key=lambda r: (r & -r, -r)):
        low = r & -r
        if r % 2:
            part = after(parts[r], came[(1, first_shift ^ 1)]) if r == 1 else parts[r]
        else:
            part = base_parts(t, late_tokens, key_value_base_weight, blocks, [r], 2, arrived_for(r), BF)[0]
        came[(low, r ^ low)] = exchange(part, "tensor", low)
    carry = shrink(core, [after(sent[0], parts[0], part)], adapter_down_weight, down_sibling, flag_lane)
    for m in far:
        arrived[m] = exchange(after(sent[m], *near_done, carry[0]), "dp", 2 * m)

    flags = []
    for part in (near, far):
        if not part:
            continue
        group = [arrived[m] for m in part if m]
        if part is far:
            group[0] = after(group[0], base)
        share, place, flag = shrink(
            core, group, adapter_down_weight, after(down_sibling, up_sibling), flag_lane, carry if part is near else ()
        )
        flags.append(flag)
        if part is near:
            base = after(parts[0], share)
            for one in arrived_for(0):
                base = base + one.astype(F32)
        shares = [after(share, came[(1, 0)])] + [exchange(share, "tensor", z) for z in range(1, blocks)]
        grown = grow(core, shares, place, adapter_up_weight, up_sibling, tuple(sizes[m] for m in part))
        for m, update in zip(part, grown):
            returned[m] = update if m == 0 else exchange(update, "dp", 2 * m)
    flag = functools.reduce(jnp.maximum, flags)
    flag = jnp.maximum(flag, exchange(flag, "dp", 1))
    bases = [base]
    updates = [returned[m] for m in range(chips)]

    def as_is():
        return finish(bases, [spread], [updates])

    def second_round():
        later_sizes, later_rows = (rest,) * chips, (message - 1,) * chips
        packed = pack(chip, adapters, slots, tokens, later_sizes, later_rows, chip_slots)
        group = [packed[0]] + [exchange(packed[m], "dp", 2 * m) for m in range(1, chips)]
        share, place, _ = shrink(core, group, adapter_down_weight, down_sibling, flag_lane)
        shares = [share] + [exchange(share, "tensor", z) for z in range(1, blocks)]
        grown = grow(core, shares, place, adapter_up_weight, up_sibling, later_sizes)
        back = [grown[0]] + [exchange(grown[m], "dp", 2 * m) for m in range(1, chips)]
        return finish(bases, [spread, packed[-1]], [updates, back])

    return lax.cond(flag[0, 0] > 0.0, second_round, as_is)


def solution(mesh):
    placed = (
        P("dp", "tensor"),
        P("dp", None),
        P(),
        P("tensor", None, None),
        P("dp", "tensor", None),
        P("dp", None, None, "tensor"),
    )
    return jax.shard_map(
        per_device, mesh=mesh, in_specs=placed, out_specs=P("dp", None, "tensor"), check_vma=False
    )
```

```python
import functools

import jax
import jax.numpy as jnp
from jax import lax
from jax.experimental import pallas as pl
from jax.experimental.pallas import tpu as pltpu
from jax.sharding import PartitionSpec as P

adapter_scale = 0.5
BF = jnp.bfloat16
F32 = jnp.float32
VMEM_LIMIT = 28 * 1024 * 1024
VMEM_MOST = 57 * 1024 * 1024
COST = pl.CostEstimate(flops=1000, bytes_accessed=1000, transcendentals=0)


def round_up(value, unit):
    return (value + unit - 1) // unit * unit


def dot(a, b, contract=((1,), (0,))):
    return lax.dot_general(a, b, (contract, ((), ())), preferred_element_type=F32)


def pack_kernel(shape, place_ref, adapter_ref, slot_ref, tokens_ref, *refs):
    sizes, first_rows, chip_slots, flag_lane = shape
    messages = len(sizes)
    outs, key_ref, pick = refs[:messages], refs[messages], refs[messages + 1]
    rows, width = tokens_ref.shape
    experts = slot_ref.shape[1]
    offsets = [sum(round_up(s, 128) for s in sizes[:m]) for m in range(messages)]

    @pl.when(pl.program_id(0) == 0)
    def _():
        named = (lax.broadcasted_iota(jnp.int32, (experts, rows), 0) == adapter_ref[...]).astype(BF)
        slots = jnp.broadcast_to(slot_ref[...].astype(F32), (16, experts)).astype(BF)
        slot = dot(slots, named)[0:1, :].astype(jnp.int32)
        shift = (slot // chip_slots) ^ place_ref[0]
        within = (slot % chip_slots + 1).astype(F32)
        lanes = round_up(messages, 16)
        goes = lax.broadcasted_iota(jnp.int32, (lanes, rows), 0) == shift
        earlier = lax.broadcasted_iota(jnp.int32, (rows, rows), 0) < lax.broadcasted_iota(jnp.int32, (rows, rows), 1)
        goes_f = goes.astype(F32)
        rank = dot(goes_f.astype(BF), earlier.astype(F32).astype(BF))
        position = jnp.sum(rank * goes_f, axis=0, keepdims=True).astype(jnp.int32)
        counts = jnp.sum(goes_f, axis=1, keepdims=True)
        sub = lax.broadcasted_iota(jnp.int32, (lanes, 1), 0)
        limit = jnp.zeros((lanes, 1), F32)
        for m in range(messages):
            limit = jnp.where(sub == m, F32(first_rows[m] + sizes[m] - 1), limit)
        over = jnp.max(jnp.where((sub < messages) & (counts > limit), 1.0, 0.0), axis=0, keepdims=True)
        key = jnp.broadcast_to(position + shift * 65536, (8, rows))
        key_ref[...] = jnp.broadcast_to(key.astype(F32).T[:, 0:1].astype(jnp.int32), key_ref.shape)
        within8 = jnp.broadcast_to(within, (16, rows)).astype(BF)
        for m in range(messages):
            padded = round_up(sizes[m], 128)
            target = lax.broadcasted_iota(jnp.int32, (padded, rows), 0)
            hit = (target + first_rows[m] == position) & (shift == m) & (target < sizes[m] - 1)
            chosen = hit.astype(F32).astype(BF)
            pick[offsets[m]:offsets[m] + padded, :] = chosen
            places = dot(within8, chosen, ((1,), (1,)))[0:1, :]
            if padded < width:
                places = jnp.concatenate([places, jnp.zeros((1, width - padded), F32)], axis=1)
            lane = lax.broadcasted_iota(jnp.int32, (1, width), 1)
            places = jnp.where(lane == flag_lane, over, places)
            body = dot(chosen, tokens_ref[...])[:sizes[m], :]
            row = lax.broadcasted_iota(jnp.int32, (sizes[m], 1), 0)
            outs[m][...] = jnp.where(row == sizes[m] - 1, places, body).astype(BF)

    @pl.when(pl.program_id(0) > 0)
    def _():
        for m in range(messages):
            outs[m][...] = dot(pick[offsets[m]:offsets[m] + sizes[m], :], tokens_ref[...]).astype(BF)


def pack(chip, adapters, slots, tokens, sizes, first_rows, chip_slots, steps=4):
    rows, width = tokens.shape
    block = width // steps
    spread = sum(round_up(s, 128) for s in sizes)
    return pl.pallas_call(
        functools.partial(pack_kernel, (sizes, first_rows, chip_slots, block - 1)),
        grid=(steps,),
        in_specs=[
            pl.BlockSpec(memory_space=pltpu.SMEM),
            pl.BlockSpec((1, rows), lambda i: (0, 0)),
            pl.BlockSpec((1, slots.shape[1]), lambda i: (0, 0)),
            pl.BlockSpec((rows, block), lambda i: (0, i)),
        ],
        out_specs=[pl.BlockSpec((s, block), lambda i: (0, i)) for s in sizes]
        + [pl.BlockSpec((rows, 128), lambda i: (0, 0))],
        out_shape=[jax.ShapeDtypeStruct((s, width), BF) for s in sizes] + [jax.ShapeDtypeStruct((rows, 128), jnp.int32)],
        scratch_shapes=[pltpu.VMEM((spread, rows), BF)],
        cost_estimate=COST,
        compiler_params=pltpu.CompilerParams(vmem_limit_bytes=VMEM_LIMIT),
        name="pack_rows",
    )(chip, adapters, slots, tokens)


def shrink_kernel(count, carried, flag_lane, core_ref, *refs):
    messages, (mine, sibling) = refs[:count], refs[count:count + 2]
    carry, refs = refs[count + 2:count + 2 + carried], refs[count + 2 + carried:]
    out, place_out, flag_out, total, places = refs
    kept = carry[0].shape[0] if carried else 0
    step = pl.program_id(0)
    local = 2 * pl.num_programs(0)
    sizes = [m.shape[0] for m in messages]

    @pl.when(step == 0)
    def _():
        flag = jnp.zeros((1, 1), F32)
        start = 0
        for m, size in zip(messages, sizes):
            padded = round_up(size, 128)
            tail = m[size - 16:size, 0:padded].astype(F32)[15:16, :]
            same = lax.broadcasted_iota(jnp.int32, (size, padded), 0) == lax.broadcasted_iota(jnp.int32, (size, padded), 1)
            column = jnp.sum(jnp.where(same, tail, 0.0), axis=1, keepdims=True)
            places[start:start + size, :] = jnp.broadcast_to(column, (size, 128))
            block = m[size - 16:size, flag_lane - 127:flag_lane + 1].astype(F32)[15:16, :]
            last = lax.broadcasted_iota(jnp.int32, (1, 128), 1) == 127
            flag = jnp.maximum(flag, jnp.max(jnp.where(last, block, 0.0), axis=1, keepdims=True))
            start += size
        place_out[kept:, :] = places[...].astype(BF)
        if carried:
            out[:kept, :] = carry[0][...]
            place_out[:kept, :] = carry[1][...]
            flag = jnp.maximum(flag, carry[2][0:1, 0:1])
        flag_out[...] = jnp.broadcast_to(flag, (8, 128))
        total[...] = jnp.zeros_like(total)

    rows = messages[0][...] if count == 1 else jnp.concatenate([m[...] for m in messages], axis=0)
    place = places[...]
    core = core_ref[0]
    for weights, side in ((mine, core), (sibling, 1 - core)):
        product = dot(rows, jnp.concatenate([weights[0], weights[1]], axis=1))
        first = (side * local + 2 * step + 1).astype(F32)
        total[...] += jnp.where(place == first, product[:, :128], 0.0) + jnp.where(
            place == first + 1.0, product[:, 128:], 0.0
        )

    @pl.when(step == pl.num_programs(0) - 1)
    def _():
        out[kept:, :] = total[...].astype(out.dtype)


def shrink(core, messages, mine, sibling, flag_lane, carry=(), dtype=BF):
    local, width, both = mine.shape
    rows = sum(m.shape[0] for m in messages)
    whole = [pl.BlockSpec(m.shape, lambda i: (0, 0)) for m in messages]
    pair = pl.BlockSpec((2, width, both), lambda i: (i, 0, 0))
    every = rows + (carry[0].shape[0] if carry else 0)
    keep = pl.BlockSpec((every, both), lambda i: (0, 0))
    whole_carry = [pl.BlockSpec(c.shape, lambda i: (0, 0)) for c in carry]
    return pl.pallas_call(
        functools.partial(shrink_kernel, len(messages), len(carry), flag_lane),
        grid=(local // 2,),
        in_specs=[pl.BlockSpec(memory_space=pltpu.SMEM)] + whole + [pair, pair] + whole_carry,
        out_specs=[keep, keep, pl.BlockSpec((8, 128), lambda i: (0, 0))],
        out_shape=[
            jax.ShapeDtypeStruct((every, both), dtype),
            jax.ShapeDtypeStruct((every, both), BF),
            jax.ShapeDtypeStruct((8, 128), F32),
        ],
        scratch_shapes=[pltpu.VMEM((rows, both), F32), pltpu.VMEM((rows, both), F32)],
        cost_estimate=pl.CostEstimate(
            flops=8 * rows * width * local * both, bytes_accessed=8 * width * local * both, transcendentals=0
        ),
        compiler_params=pltpu.CompilerParams(vmem_limit_bytes=VMEM_LIMIT),
        name="shrink_rows",
    )(core, *messages, mine, sibling, *carry)


def grow_kernel(shares, sizes, core_ref, *refs):
    parts, place_ref, mine, sibling = refs[:shares], refs[shares], refs[shares + 1], refs[shares + 2]
    outs = refs[shares + 3:]
    summed = parts[0][...].astype(F32)
    for part in parts[1:]:
        summed = summed + part[...].astype(F32)
    shrunk = summed.astype(BF).astype(F32)
    place = place_ref[...].astype(F32)
    local, _, rank, columns = mine.shape
    core = core_ref[0]
    low = lax.broadcasted_iota(jnp.int32, shrunk.shape, 1) < rank
    turned = pltpu.roll(shrunk, rank, 1)
    result = []
    for j in range(2):
        twice = jnp.where(low, shrunk, turned) if j == 0 else jnp.where(low, turned, shrunk)
        total = None
        for weights, side in ((mine, core), (sibling, 1 - core)):
            left = []
            for e in range(0, local, 2):
                first = (side * local + e + 1).astype(F32)
                wanted = jnp.where(low, first, first + 1.0)
                left.append(jnp.where(place == wanted, twice, 0.0).astype(BF))
            right = weights[:, j].reshape(local * rank, columns)
            product = dot(jnp.concatenate(left, axis=1), right)
            total = product if total is None else total + product
        result.append((adapter_scale * total).astype(BF))
    start = 0
    for out, size in zip(outs, sizes):
        out[:, :columns] = result[0][start:start + size, :]
        out[:, columns:] = result[1][start:start + size, :]
        start += size


def grow(core, parts, place, mine, sibling, sizes):
    columns = mine.shape[3]
    vmem = pl.BlockSpec(memory_space=pltpu.VMEM)
    return pl.pallas_call(
        functools.partial(grow_kernel, len(parts), sizes),
        in_specs=[pl.BlockSpec(memory_space=pltpu.SMEM)] + [vmem] * (len(parts) + 3),
        out_specs=[vmem] * len(sizes),
        out_shape=[jax.ShapeDtypeStruct((s, 2 * columns), BF) for s in sizes],
        cost_estimate=COST,
        compiler_params=pltpu.CompilerParams(vmem_limit_bytes=VMEM_LIMIT),
        name="grow_rows",
    )(core, *parts, place, mine, sibling)


def base_kernel(shifts, place_ref, tokens_ref, weight_ref, *outs):
    step = pl.program_id(0)
    weight = jnp.swapaxes(weight_ref[...], 0, 1)
    columns = weight.shape[2]
    both = [dot(tokens_ref[...], weight[j]) for j in range(2)]
    for i, out in enumerate(outs):

        @pl.when(step == i)
        def _():
            for j in range(2):
                out[:, j * columns:(j + 1) * columns] = both[j].astype(out.dtype)


def base_parts(t, tokens, weight, blocks, shifts):
    rows, width = tokens.shape
    columns = weight.shape[2] // blocks
    types = [BF if r % 2 else F32 for r in shifts]
    if columns % 128:
        cut = [lax.dynamic_slice_in_dim(weight, (t ^ r) * columns, columns, 2) for r in shifts]
        return [dot(tokens, c.reshape(width, 2 * columns)).astype(k) for c, k in zip(cut, types)]
    order = jnp.stack([t ^ r for r in shifts])
    return pl.pallas_call(
        functools.partial(base_kernel, shifts),
        grid_spec=pltpu.PrefetchScalarGridSpec(
            num_scalar_prefetch=1,
            grid=(len(shifts),),
            in_specs=[
                pl.BlockSpec((rows, width), lambda i, p: (0, 0)),
                pl.BlockSpec((width, 2, columns), lambda i, p: (0, 0, p[i])),
            ],
            out_specs=[pl.BlockSpec((rows, 2 * columns), lambda i, p: (0, 0))] * len(shifts),
        ),
        out_shape=[jax.ShapeDtypeStruct((rows, 2 * columns), k) for k in types],
        cost_estimate=pl.CostEstimate(
            flops=16 * len(shifts) * rows * width * columns, bytes_accessed=8 * width * columns, transcendentals=0
        ),
        compiler_params=pltpu.CompilerParams(vmem_limit_bytes=VMEM_MOST),
        name="base_parts",
    )(order, tokens, weight)


def spread_kernel(sizes, first_rows, key_ref, out):
    start = 0
    for m, size in enumerate(sizes):
        padded = round_up(size, 128)
        lane = lax.broadcasted_iota(jnp.int32, (key_ref.shape[0], padded), 1)
        hit = (lane == key_ref[:, 0:1] - first_rows[m] - m * 65536) & (lane < size - 1)
        out[:, start:start + padded] = hit.astype(F32).astype(BF)
        start += padded


def spread_of(key, sizes, first_rows):
    vmem = pl.BlockSpec(memory_space=pltpu.VMEM)
    total = sum(round_up(size, 128) for size in sizes)
    return pl.pallas_call(
        functools.partial(spread_kernel, sizes, first_rows),
        in_specs=[vmem],
        out_specs=vmem,
        out_shape=jax.ShapeDtypeStruct((key.shape[0], total), BF),
        cost_estimate=COST,
        compiler_params=pltpu.CompilerParams(vmem_limit_bytes=VMEM_LIMIT),
        name="spread_rows",
    )(key)


def finish_kernel(sizes, count, *refs):
    bases, spreads, out = refs[:count], refs[count:count + len(sizes)], refs[-1]
    updates = refs[count + len(sizes):-1]
    total = bases[0][...]
    for base in bases[1:]:
        total = total + base[...].astype(F32)
    update_rows = jnp.zeros(total.shape, F32)
    done = 0
    for spread, group in zip(spreads, sizes):
        start = 0
        for size in group:
            padded = round_up(size, 128)
            rows = updates[done][...]
            if padded > size:
                rows = jnp.concatenate([rows, jnp.zeros((padded - size, rows.shape[1]), rows.dtype)], axis=0)
            update_rows = update_rows + dot(spread[:, start:start + padded], rows)
            start += padded
            done += 1
    total = total + update_rows
    columns = out.shape[2]
    if columns % 128:
        out[:, 0, :] = total[:, :columns].astype(BF)
        out[:, 1, :] = total[:, columns:].astype(BF)
    else:
        both = jnp.stack([total[:, :columns], total[:, columns:]], axis=0).astype(BF)
        out[...] = jnp.swapaxes(both, 0, 1)


def finish(bases, spreads, groups):
    sizes = tuple(tuple(u.shape[0] for u in group) for group in groups)
    rows, both = bases[0].shape
    updates = [u for group in groups for u in group]
    block = rows // 4
    return pl.pallas_call(
        functools.partial(finish_kernel, sizes, len(bases)),
        grid=(4,),
        in_specs=[pl.BlockSpec((block, x.shape[1]), lambda i: (i, 0)) for x in bases + spreads]
        + [pl.BlockSpec(u.shape, lambda i: (0, 0)) for u in updates],
        out_specs=pl.BlockSpec((block, 2, both // 2), lambda i: (i, 0, 0)),
        out_shape=jax.ShapeDtypeStruct((rows, 2, both // 2), BF),
        cost_estimate=COST,
        compiler_params=pltpu.CompilerParams(vmem_limit_bytes=VMEM_LIMIT),
        name="finish_rows",
    )(*bases, *spreads, *updates)


def exchange(array, axis, shift):
    size = lax.axis_size(axis)
    return lax.ppermute(array, axis, [(i, i ^ shift) for i in range(size)])


def after(array, *others):
    return lax.optimization_barrier((array,) + others)[0]


def bits(value):
    return bin(value).count("1")


def per_device(
    tokens,
    row_adapter_index,
    adapter_storage_slot,
    key_value_base_weight,
    adapter_down_weight,
    adapter_up_weight,
):
    row_count, width = tokens.shape
    local = adapter_down_weight.shape[0]
    groups = lax.axis_size("dp")
    blocks = lax.axis_size("tensor")
    experts = local * groups
    chips = groups // 2
    capacity = max(2, 2 * row_count // experts)
    chip_slots = 2 * local
    full = chip_slots * capacity

    me = lax.axis_index("dp").astype(jnp.int32)
    chip, core = (me // 2).reshape(1), (me % 2).reshape(1)
    adapters = row_adapter_index.reshape(1, row_count)
    slots = adapter_storage_slot.reshape(1, experts)
    flag_lane = width // 4 - 1

    down_sibling = exchange(adapter_down_weight, "dp", 1)

    near = [m for m in range(chips) if bits(m) <= 1]
    far = [m for m in range(chips) if bits(m) > 1]
    message = round_up(full * 11 // 16, 16)
    rest = round_up(full - message + 2, 16)
    sizes, first_rows = (message,) * chips, (0,) * chips

    packed = pack(chip, adapters, slots, tokens, sizes, first_rows, chip_slots)
    sent, key = list(packed[:-1]), packed[-1]
    arrived, returned = {0: sent[0]}, {}
    for m in near[1:]:
        arrived[m] = exchange(sent[m], "dp", 2 * m)

    t = lax.axis_index("tensor").astype(jnp.int32)
    late_tokens = after(tokens, *sent)
    first_shift = blocks - 1
    parts = {first_shift: base_parts(t, late_tokens, key_value_base_weight, blocks, [first_shift])[0]}
    came = {(1, first_shift ^ 1): exchange(parts[first_shift], "tensor", 1)}
    others = list(range(first_shift - 1, -1, -1))
    late_tokens = after(tokens, parts[first_shift])
    parts.update(zip(others, base_parts(t, late_tokens, key_value_base_weight, blocks, others)))

    def arrived_for(r):
        return [came[key] for key in sorted(came) if key[1] == r]

    up_sibling = exchange(after(adapter_up_weight, down_sibling), "dp", 1)
    carry = shrink(core, [after(sent[0], parts[0])], adapter_down_weight, down_sibling, flag_lane, dtype=F32)
    near_done = [arrived[m] for m in near[1:]]
    for m in far:
        arrived[m] = exchange(after(sent[m], *near_done, carry[0]), "dp", 2 * m)
    for r in sorted(range(1, first_shift), key=lambda r: (r & -r, -r)):
        low = r & -r
        part = parts[r]
        for one in arrived_for(r):
            part = part + after(one, *near_done, carry[0]).astype(F32)
        if r == 1:
            part = after(part, came[(1, first_shift ^ 1)])
        came[(low, r ^ low)] = exchange(part.astype(BF), "tensor", low)

    both_down = after(down_sibling, up_sibling)
    flags, updates = [], {}
    for part in (near, far):
        if not part:
            continue
        group = [arrived[m] for m in part if m]
        if part is near:
            share, place, flag = shrink(core, group, adapter_down_weight, both_down, flag_lane, carry, F32)
            step = 1
            while 2 * step < blocks:
                share = share + exchange(share.astype(BF), "tensor", step).astype(F32)
                step *= 2
            shares = [share, exchange(share.astype(BF), "tensor", step)]
            base = after(parts[0], share)
            for one in arrived_for(0):
                base = base + one.astype(F32)
        else:
            group[0] = after(group[0], base)
            share, place, flag = shrink(core, group, adapter_down_weight, both_down, flag_lane)
            shares = [after(share, returned[0])] + [exchange(share, "tensor", z) for z in range(1, blocks)]
        flags.append(flag)
        grown = grow(core, shares, place, adapter_up_weight, up_sibling, tuple(sizes[m] for m in part))
        for m, update in zip(part, grown):
            returned[m] = update if m == 0 else exchange(update, "dp", 2 * m)
    spread = spread_of(after(key, base), sizes, first_rows)
    flag = functools.reduce(jnp.maximum, flags)
    flag = jnp.maximum(flag, exchange(flag, "dp", 1))
    updates = [returned[m] for m in range(chips)]

    def as_is():
        return finish([base], [spread], [updates])

    def second_round():
        later_sizes, later_rows = (rest,) * chips, (message - 1,) * chips
        packed = pack(chip, adapters, slots, tokens, later_sizes, later_rows, chip_slots)
        group = [packed[0]] + [exchange(packed[m], "dp", 2 * m) for m in range(1, chips)]
        share, place, _ = shrink(core, group, adapter_down_weight, down_sibling, flag_lane)
        shares = [share] + [exchange(share, "tensor", z) for z in range(1, blocks)]
        grown = grow(core, shares, place, adapter_up_weight, up_sibling, later_sizes)
        back = [grown[0]] + [exchange(grown[m], "dp", 2 * m) for m in range(1, chips)]
        return finish([base], [spread, spread_of(packed[-1], later_sizes, later_rows)], [updates, back])

    return lax.cond(flag[0, 0] > 0.0, second_round, as_is)


def solution(mesh):
    placed = (
        P("dp", "tensor"),
        P("dp", None),
        P(),
        P("tensor", None, None),
        P("dp", "tensor", None),
        P("dp", None, None, "tensor"),
    )
    return jax.shard_map(
        per_device, mesh=mesh, in_specs=placed, out_specs=P("dp", None, "tensor"), check_vma=False
    )
```

```python
import functools

import jax
import jax.numpy as jnp
from jax import lax
from jax.experimental import pallas as pl
from jax.experimental.pallas import tpu as pltpu
from jax.sharding import PartitionSpec as P

adapter_scale = 0.5
BF = jnp.bfloat16
F32 = jnp.float32
VMEM_LIMIT = 28 * 1024 * 1024
VMEM_MOST = 57 * 1024 * 1024
COST = pl.CostEstimate(flops=1000, bytes_accessed=1000, transcendentals=0)


def round_up(value, unit):
    return (value + unit - 1) // unit * unit


def dot(a, b, contract=((1,), (0,))):
    return lax.dot_general(a, b, (contract, ((), ())), preferred_element_type=F32)


def pack_kernel(shape, place_ref, adapter_ref, slot_ref, tokens_ref, *refs):
    sizes, first_rows, chip_slots, flag_lane = shape
    messages = len(sizes)
    outs, key_ref, pick = refs[:messages], refs[messages], refs[messages + 1]
    rows, width = tokens_ref.shape
    experts = slot_ref.shape[1]
    offsets = [sum(round_up(s, 128) for s in sizes[:m]) for m in range(messages)]

    @pl.when(pl.program_id(0) == 0)
    def _():
        named = (lax.broadcasted_iota(jnp.int32, (experts, rows), 0) == adapter_ref[...]).astype(BF)
        slots = jnp.broadcast_to(slot_ref[...].astype(F32), (16, experts)).astype(BF)
        slot = dot(slots, named)[0:1, :].astype(jnp.int32)
        shift = (slot // chip_slots) ^ place_ref[0]
        within = (slot % chip_slots + 1).astype(F32)
        lanes = round_up(messages, 16)
        goes = lax.broadcasted_iota(jnp.int32, (lanes, rows), 0) == shift
        earlier = lax.broadcasted_iota(jnp.int32, (rows, rows), 0) < lax.broadcasted_iota(jnp.int32, (rows, rows), 1)
        goes_f = goes.astype(F32)
        rank = dot(goes_f.astype(BF), earlier.astype(F32).astype(BF))
        position = jnp.sum(rank * goes_f, axis=0, keepdims=True).astype(jnp.int32)
        counts = jnp.sum(goes_f, axis=1, keepdims=True)
        sub = lax.broadcasted_iota(jnp.int32, (lanes, 1), 0)
        limit = jnp.zeros((lanes, 1), F32)
        for m in range(messages):
            limit = jnp.where(sub == m, F32(first_rows[m] + sizes[m] - 1), limit)
        over = jnp.max(jnp.where((sub < messages) & (counts > limit), 1.0, 0.0), axis=0, keepdims=True)
        key = jnp.broadcast_to(position + shift * 65536, (8, rows))
        key_ref[...] = jnp.broadcast_to(key.astype(F32).T[:, 0:1].astype(jnp.int32), key_ref.shape)
        within8 = jnp.broadcast_to(within, (16, rows)).astype(BF)
        for m in range(messages):
            padded = round_up(sizes[m], 128)
            target = lax.broadcasted_iota(jnp.int32, (padded, rows), 0)
            hit = (target + first_rows[m] == position) & (shift == m) & (target < sizes[m] - 1)
            chosen = hit.astype(F32).astype(BF)
            pick[offsets[m]:offsets[m] + padded, :] = chosen
            places = dot(within8, chosen, ((1,), (1,)))[0:1, :]
            if padded < width:
                places = jnp.concatenate([places, jnp.zeros((1, width - padded), F32)], axis=1)
            lane = lax.broadcasted_iota(jnp.int32, (1, width), 1)
            places = jnp.where(lane == flag_lane, over, places)
            body = dot(chosen, tokens_ref[...])[:sizes[m], :]
            row = lax.broadcasted_iota(jnp.int32, (sizes[m], 1), 0)
            outs[m][...] = jnp.where(row == sizes[m] - 1, places, body).astype(BF)

    @pl.when(pl.program_id(0) > 0)
    def _():
        for m in range(messages):
            outs[m][...] = dot(pick[offsets[m]:offsets[m] + sizes[m], :], tokens_ref[...]).astype(BF)


def pack(chip, adapters, slots, tokens, sizes, first_rows, chip_slots, steps=4):
    rows, width = tokens.shape
    block = width // steps
    spread = sum(round_up(s, 128) for s in sizes)
    return pl.pallas_call(
        functools.partial(pack_kernel, (sizes, first_rows, chip_slots, block - 1)),
        grid=(steps,),
        in_specs=[
            pl.BlockSpec(memory_space=pltpu.SMEM),
            pl.BlockSpec((1, rows), lambda i: (0, 0)),
            pl.BlockSpec((1, slots.shape[1]), lambda i: (0, 0)),
            pl.BlockSpec((rows, block), lambda i: (0, i)),
        ],
        out_specs=[pl.BlockSpec((s, block), lambda i: (0, i)) for s in sizes]
        + [pl.BlockSpec((rows, 128), lambda i: (0, 0))],
        out_shape=[jax.ShapeDtypeStruct((s, width), BF) for s in sizes] + [jax.ShapeDtypeStruct((rows, 128), jnp.int32)],
        scratch_shapes=[pltpu.VMEM((spread, rows), BF)],
        cost_estimate=COST,
        compiler_params=pltpu.CompilerParams(vmem_limit_bytes=VMEM_LIMIT),
        name="pack_rows",
    )(chip, adapters, slots, tokens)


def shrink_kernel(count, flag_lane, core_ref, *refs):
    messages, (mine, sibling) = refs[:count], refs[count:count + 2]
    out, place_out, flag_out, total, places = refs[count + 2:]
    step = pl.program_id(0)
    local = 2 * pl.num_programs(0)
    sizes = [m.shape[0] for m in messages]

    @pl.when(step == 0)
    def _():
        flag = jnp.zeros((1, 1), F32)
        start = 0
        for m, size in zip(messages, sizes):
            padded = round_up(size, 128)
            tail = m[size - 16:size, 0:padded].astype(F32)[15:16, :]
            same = lax.broadcasted_iota(jnp.int32, (size, padded), 0) == lax.broadcasted_iota(jnp.int32, (size, padded), 1)
            column = jnp.sum(jnp.where(same, tail, 0.0), axis=1, keepdims=True)
            places[start:start + size, :] = jnp.broadcast_to(column, (size, 128))
            block = m[size - 16:size, flag_lane - 127:flag_lane + 1].astype(F32)[15:16, :]
            last = lax.broadcasted_iota(jnp.int32, (1, 128), 1) == 127
            flag = jnp.maximum(flag, jnp.max(jnp.where(last, block, 0.0), axis=1, keepdims=True))
            start += size
        place_out[...] = places[...].astype(BF)
        flag_out[...] = jnp.broadcast_to(flag, (8, 128))
        total[...] = jnp.zeros_like(total)

    rows = messages[0][...] if count == 1 else jnp.concatenate([m[...] for m in messages], axis=0)
    place = places[...]
    core = core_ref[0]
    for weights, side in ((mine, core), (sibling, 1 - core)):
        product = dot(rows, jnp.concatenate([weights[0], weights[1]], axis=1))
        first = (side * local + 2 * step + 1).astype(F32)
        total[...] += jnp.where(place == first, product[:, :128], 0.0) + jnp.where(
            place == first + 1.0, product[:, 128:], 0.0
        )

    @pl.when(step == pl.num_programs(0) - 1)
    def _():
        out[...] = total[...].astype(out.dtype)


def shrink(core, messages, mine, sibling, flag_lane, dtype=BF):
    local, width, both = mine.shape
    rows = sum(m.shape[0] for m in messages)
    whole = [pl.BlockSpec(m.shape, lambda i: (0, 0)) for m in messages]
    pair = pl.BlockSpec((2, width, both), lambda i: (i, 0, 0))
    keep = pl.BlockSpec((rows, both), lambda i: (0, 0))
    return pl.pallas_call(
        functools.partial(shrink_kernel, len(messages), flag_lane),
        grid=(local // 2,),
        in_specs=[pl.BlockSpec(memory_space=pltpu.SMEM)] + whole + [pair, pair],
        out_specs=[keep, keep, pl.BlockSpec((8, 128), lambda i: (0, 0))],
        out_shape=[
            jax.ShapeDtypeStruct((rows, both), dtype),
            jax.ShapeDtypeStruct((rows, both), BF),
            jax.ShapeDtypeStruct((8, 128), F32),
        ],
        scratch_shapes=[pltpu.VMEM((rows, both), F32), pltpu.VMEM((rows, both), F32)],
        cost_estimate=pl.CostEstimate(
            flops=8 * rows * width * local * both, bytes_accessed=8 * width * local * both, transcendentals=0
        ),
        compiler_params=pltpu.CompilerParams(vmem_limit_bytes=VMEM_LIMIT),
        name="shrink_rows",
    )(core, *messages, mine, sibling)


def grow_kernel(shares, sizes, core_ref, *refs):
    parts, place_ref, mine, sibling = refs[:shares], refs[shares], refs[shares + 1], refs[shares + 2]
    outs = refs[shares + 3:]
    summed = parts[0][...].astype(F32)
    for part in parts[1:]:
        summed = summed + part[...].astype(F32)
    shrunk = summed.astype(BF).astype(F32)
    place = place_ref[...].astype(F32)
    local, _, rank, columns = mine.shape
    core = core_ref[0]
    low = lax.broadcasted_iota(jnp.int32, shrunk.shape, 1) < rank
    turned = pltpu.roll(shrunk, rank, 1)
    result = []
    for j in range(2):
        twice = jnp.where(low, shrunk, turned) if j == 0 else jnp.where(low, turned, shrunk)
        total = None
        for weights, side in ((mine, core), (sibling, 1 - core)):
            left = []
            for e in range(0, local, 2):
                first = (side * local + e + 1).astype(F32)
                wanted = jnp.where(low, first, first + 1.0)
                left.append(jnp.where(place == wanted, twice, 0.0).astype(BF))
            right = weights[:, j].reshape(local * rank, columns)
            product = dot(jnp.concatenate(left, axis=1), right)
            total = product if total is None else total + product
        result.append((adapter_scale * total).astype(BF))
    start = 0
    for out, size in zip(outs, sizes):
        out[:, :columns] = result[0][start:start + size, :]
        out[:, columns:] = result[1][start:start + size, :]
        start += size


def grow(core, parts, place, mine, sibling, sizes):
    columns = mine.shape[3]
    vmem = pl.BlockSpec(memory_space=pltpu.VMEM)
    return pl.pallas_call(
        functools.partial(grow_kernel, len(parts), sizes),
        in_specs=[pl.BlockSpec(memory_space=pltpu.SMEM)] + [vmem] * (len(parts) + 3),
        out_specs=[vmem] * len(sizes),
        out_shape=[jax.ShapeDtypeStruct((s, 2 * columns), BF) for s in sizes],
        cost_estimate=COST,
        compiler_params=pltpu.CompilerParams(vmem_limit_bytes=VMEM_LIMIT),
        name="grow_rows",
    )(core, *parts, place, mine, sibling)


def base_kernel(shifts, place_ref, tokens_ref, weight_ref, *outs):
    step = pl.program_id(0)
    weight = jnp.swapaxes(weight_ref[...], 0, 1)
    columns = weight.shape[2]
    both = [dot(tokens_ref[...], weight[j]) for j in range(2)]
    for i, out in enumerate(outs):

        @pl.when(step == i)
        def _():
            for j in range(2):
                out[:, j * columns:(j + 1) * columns] = both[j].astype(out.dtype)


def base_parts(t, tokens, weight, blocks, shifts):
    rows, width = tokens.shape
    columns = weight.shape[2] // blocks
    types = [BF if r % 2 else F32 for r in shifts]
    if columns % 128:
        cut = [lax.dynamic_slice_in_dim(weight, (t ^ r) * columns, columns, 2) for r in shifts]
        return [dot(tokens, c.reshape(width, 2 * columns)).astype(k) for c, k in zip(cut, types)]
    order = jnp.stack([t ^ r for r in shifts])
    return pl.pallas_call(
        functools.partial(base_kernel, shifts),
        grid_spec=pltpu.PrefetchScalarGridSpec(
            num_scalar_prefetch=1,
            grid=(len(shifts),),
            in_specs=[
                pl.BlockSpec((rows, width), lambda i, p: (0, 0)),
                pl.BlockSpec((width, 2, columns), lambda i, p: (0, 0, p[i])),
            ],
            out_specs=[pl.BlockSpec((rows, 2 * columns), lambda i, p: (0, 0))] * len(shifts),
        ),
        out_shape=[jax.ShapeDtypeStruct((rows, 2 * columns), k) for k in types],
        cost_estimate=pl.CostEstimate(
            flops=16 * len(shifts) * rows * width * columns, bytes_accessed=8 * width * columns, transcendentals=0
        ),
        compiler_params=pltpu.CompilerParams(vmem_limit_bytes=VMEM_MOST),
        name="base_parts",
    )(order, tokens, weight)


def spread_kernel(sizes, first_rows, key_ref, out):
    start = 0
    for m, size in enumerate(sizes):
        padded = round_up(size, 128)
        lane = lax.broadcasted_iota(jnp.int32, (key_ref.shape[0], padded), 1)
        hit = (lane == key_ref[:, 0:1] - first_rows[m] - m * 65536) & (lane < size - 1)
        out[:, start:start + padded] = hit.astype(F32).astype(BF)
        start += padded


def spread_of(key, sizes, first_rows):
    vmem = pl.BlockSpec(memory_space=pltpu.VMEM)
    total = sum(round_up(size, 128) for size in sizes)
    return pl.pallas_call(
        functools.partial(spread_kernel, sizes, first_rows),
        in_specs=[vmem],
        out_specs=vmem,
        out_shape=jax.ShapeDtypeStruct((key.shape[0], total), BF),
        cost_estimate=COST,
        compiler_params=pltpu.CompilerParams(vmem_limit_bytes=VMEM_LIMIT),
        name="spread_rows",
    )(key)


def finish_kernel(sizes, count, *refs):
    bases, spreads, out = refs[:count], refs[count:count + len(sizes)], refs[-1]
    updates = refs[count + len(sizes):-1]
    total = bases[0][...]
    for base in bases[1:]:
        total = total + base[...].astype(F32)
    update_rows = jnp.zeros(total.shape, F32)
    done = 0
    for spread, group in zip(spreads, sizes):
        start = 0
        for size in group:
            padded = round_up(size, 128)
            rows = updates[done][...]
            if padded > size:
                rows = jnp.concatenate([rows, jnp.zeros((padded - size, rows.shape[1]), rows.dtype)], axis=0)
            update_rows = update_rows + dot(spread[:, start:start + padded], rows)
            start += padded
            done += 1
    total = total + update_rows
    columns = out.shape[2]
    if columns % 128:
        out[:, 0, :] = total[:, :columns].astype(BF)
        out[:, 1, :] = total[:, columns:].astype(BF)
    else:
        both = jnp.stack([total[:, :columns], total[:, columns:]], axis=0).astype(BF)
        out[...] = jnp.swapaxes(both, 0, 1)


def finish(bases, spreads, groups):
    sizes = tuple(tuple(u.shape[0] for u in group) for group in groups)
    rows, both = bases[0].shape
    updates = [u for group in groups for u in group]
    block = rows // 4
    return pl.pallas_call(
        functools.partial(finish_kernel, sizes, len(bases)),
        grid=(4,),
        in_specs=[pl.BlockSpec((block, x.shape[1]), lambda i: (i, 0)) for x in bases + spreads]
        + [pl.BlockSpec(u.shape, lambda i: (0, 0)) for u in updates],
        out_specs=pl.BlockSpec((block, 2, both // 2), lambda i: (i, 0, 0)),
        out_shape=jax.ShapeDtypeStruct((rows, 2, both // 2), BF),
        cost_estimate=COST,
        compiler_params=pltpu.CompilerParams(vmem_limit_bytes=VMEM_LIMIT),
        name="finish_rows",
    )(*bases, *spreads, *updates)


def exchange(array, axis, shift):
    size = lax.axis_size(axis)
    return lax.ppermute(array, axis, [(i, i ^ shift) for i in range(size)])


def after(array, *others):
    return lax.optimization_barrier((array,) + others)[0]


def bits(value):
    return bin(value).count("1")


def per_device(
    tokens,
    row_adapter_index,
    adapter_storage_slot,
    key_value_base_weight,
    adapter_down_weight,
    adapter_up_weight,
):
    row_count, width = tokens.shape
    local = adapter_down_weight.shape[0]
    groups = lax.axis_size("dp")
    blocks = lax.axis_size("tensor")
    experts = local * groups
    chips = groups // 2
    capacity = max(2, 2 * row_count // experts)
    chip_slots = 2 * local
    full = chip_slots * capacity

    me = lax.axis_index("dp").astype(jnp.int32)
    chip, core = (me // 2).reshape(1), (me % 2).reshape(1)
    adapters = row_adapter_index.reshape(1, row_count)
    slots = adapter_storage_slot.reshape(1, experts)
    flag_lane = width // 4 - 1

    down_sibling = exchange(adapter_down_weight, "dp", 1)

    near = [m for m in range(chips) if bits(m) <= 1]
    far = [m for m in range(chips) if bits(m) > 1]
    message = round_up(full * 11 // 16, 16)
    rest = round_up(full - message + 2, 16)
    sizes, first_rows = (message,) * chips, (0,) * chips

    t = lax.axis_index("tensor").astype(jnp.int32)
    first_shift = blocks - 1
    parts, came = {}, {}

    def compute(shifts, ready):
        parts.update(zip(shifts, base_parts(t, ready, key_value_base_weight, blocks, shifts)))

    def arrived_for(r):
        return [came[key] for key in sorted(came) if key[1] == r]

    def send(r):
        part = parts[r]
        for one in arrived_for(r):
            part = part + one.astype(F32)
        part = part.astype(BF)
        came[(r & -r, r ^ (r & -r))] = exchange(part, "tensor", r & -r)
        return part

    compute([first_shift], tokens)
    send(first_shift)
    packed = pack(chip, adapters, slots, after(tokens, parts[first_shift]), sizes, first_rows, chip_slots)
    sent, key = list(packed[:-1]), packed[-1]
    arrived, returned = {0: sent[0]}, {}
    for m in near[1:]:
        arrived[m] = exchange(sent[m], "dp", 2 * m)
    middle = [r for r in range(first_shift - 1, 1, -1)]
    compute(middle, after(tokens, *sent))
    for r in sorted(middle, key=lambda r: (r & -r, -r)):
        last_sent = send(r)
    compute([1, 0], after(tokens, last_sent))
    send(1)

    up_sibling = exchange(after(adapter_up_weight, down_sibling), "dp", 1)
    near_done = [arrived[m] for m in near[1:]]
    for m in far:
        arrived[m] = exchange(after(sent[m], *near_done, parts[0]), "dp", 2 * m)

    both_down = after(down_sibling, up_sibling)
    flags, updates = [], {}
    for part in (near, far):
        if not part:
            continue
        group = [arrived[m] for m in part]
        if part is near:
            share, place, flag = shrink(core, group, adapter_down_weight, both_down, flag_lane, F32)
            step = 1
            while 2 * step < blocks:
                share = share + exchange(share.astype(BF), "tensor", step).astype(F32)
                step *= 2
            shares = [share, exchange(share.astype(BF), "tensor", step)]
            base = after(parts[0], share)
            for one in arrived_for(0):
                base = base + one.astype(F32)
        else:
            group[0] = after(group[0], base, shares[-1])
            share, place, flag = shrink(core, group, adapter_down_weight, both_down, flag_lane)
            shares = [after(share, returned[0])] + [exchange(share, "tensor", z) for z in range(1, blocks)]
        flags.append(flag)
        grown = grow(core, shares, place, adapter_up_weight, up_sibling, tuple(sizes[m] for m in part))
        for m, update in zip(part, grown):
            returned[m] = update if m == 0 else exchange(update, "dp", 2 * m)
    spread = spread_of(after(key, base), sizes, first_rows)
    flag = functools.reduce(jnp.maximum, flags)
    flag = jnp.maximum(flag, exchange(flag, "dp", 1))
    updates = [returned[m] for m in range(chips)]

    def as_is():
        return finish([base], [spread], [updates])

    def second_round():
        later_sizes, later_rows = (rest,) * chips, (message - 1,) * chips
        packed = pack(chip, adapters, slots, tokens, later_sizes, later_rows, chip_slots)
        group = [packed[0]] + [exchange(packed[m], "dp", 2 * m) for m in range(1, chips)]
        share, place, _ = shrink(core, group, adapter_down_weight, down_sibling, flag_lane)
        shares = [share] + [exchange(share, "tensor", z) for z in range(1, blocks)]
        grown = grow(core, shares, place, adapter_up_weight, up_sibling, later_sizes)
        back = [grown[0]] + [exchange(grown[m], "dp", 2 * m) for m in range(1, chips)]
        return finish([base], [spread, spread_of(packed[-1], later_sizes, later_rows)], [updates, back])

    return lax.cond(flag[0, 0] > 0.0, second_round, as_is)


def solution(mesh):
    placed = (
        P("dp", "tensor"),
        P("dp", None),
        P(),
        P("tensor", None, None),
        P("dp", "tensor", None),
        P("dp", None, None, "tensor"),
    )
    return jax.shard_map(
        per_device, mesh=mesh, in_specs=placed, out_specs=P("dp", None, "tensor"), check_vma=False
    )
```

```python
import functools

import jax
import jax.numpy as jnp
from jax import lax
from jax.experimental import pallas as pl
from jax.experimental.pallas import tpu as pltpu
from jax.sharding import PartitionSpec as P

adapter_scale = 0.5
BF = jnp.bfloat16
F32 = jnp.float32
VMEM_LIMIT = 28 * 1024 * 1024
VMEM_MOST = 57 * 1024 * 1024
COST = pl.CostEstimate(flops=1000, bytes_accessed=1000, transcendentals=0)


def round_up(value, unit):
    return (value + unit - 1) // unit * unit


def dot(a, b, contract=((1,), (0,))):
    return lax.dot_general(a, b, (contract, ((), ())), preferred_element_type=F32)


def pack_kernel(shape, place_ref, adapter_ref, slot_ref, tokens_ref, *refs):
    sizes, first_rows, chip_slots, flag_lane = shape
    messages = len(sizes)
    outs, key_ref, pick = refs[:messages], refs[messages], refs[messages + 1]
    rows, width = tokens_ref.shape
    experts = slot_ref.shape[1]
    offsets = [sum(round_up(s, 128) for s in sizes[:m]) for m in range(messages)]

    @pl.when(pl.program_id(0) == 0)
    def _():
        named = (lax.broadcasted_iota(jnp.int32, (experts, rows), 0) == adapter_ref[...]).astype(BF)
        slots = jnp.broadcast_to(slot_ref[...].astype(F32), (16, experts)).astype(BF)
        slot = dot(slots, named)[0:1, :].astype(jnp.int32)
        shift = (slot // chip_slots) ^ place_ref[0]
        within = (slot % chip_slots + 1).astype(F32)
        lanes = round_up(messages, 16)
        goes = lax.broadcasted_iota(jnp.int32, (lanes, rows), 0) == shift
        earlier = lax.broadcasted_iota(jnp.int32, (rows, rows), 0) < lax.broadcasted_iota(jnp.int32, (rows, rows), 1)
        goes_f = goes.astype(F32)
        rank = dot(goes_f.astype(BF), earlier.astype(F32).astype(BF))
        position = jnp.sum(rank * goes_f, axis=0, keepdims=True).astype(jnp.int32)
        counts = jnp.sum(goes_f, axis=1, keepdims=True)
        sub = lax.broadcasted_iota(jnp.int32, (lanes, 1), 0)
        limit = jnp.zeros((lanes, 1), F32)
        for m in range(messages):
            limit = jnp.where(sub == m, F32(first_rows[m] + sizes[m] - 1), limit)
        over = jnp.max(jnp.where((sub < messages) & (counts > limit), 1.0, 0.0), axis=0, keepdims=True)
        key = jnp.broadcast_to(position + shift * 65536, (8, rows))
        key_ref[...] = jnp.broadcast_to(key.astype(F32).T[:, 0:1].astype(jnp.int32), key_ref.shape)
        within8 = jnp.broadcast_to(within, (16, rows)).astype(BF)
        for m in range(messages):
            padded = round_up(sizes[m], 128)
            target = lax.broadcasted_iota(jnp.int32, (padded, rows), 0)
            hit = (target + first_rows[m] == position) & (shift == m) & (target < sizes[m] - 1)
            chosen = hit.astype(F32).astype(BF)
            pick[offsets[m]:offsets[m] + padded, :] = chosen
            places = dot(within8, chosen, ((1,), (1,)))[0:1, :]
            if padded < width:
                places = jnp.concatenate([places, jnp.zeros((1, width - padded), F32)], axis=1)
            lane = lax.broadcasted_iota(jnp.int32, (1, width), 1)
            places = jnp.where(lane == flag_lane, over, places)
            body = dot(chosen, tokens_ref[...])[:sizes[m], :]
            row = lax.broadcasted_iota(jnp.int32, (sizes[m], 1), 0)
            outs[m][...] = jnp.where(row == sizes[m] - 1, places, body).astype(BF)

    @pl.when(pl.program_id(0) > 0)
    def _():
        for m in range(messages):
            outs[m][...] = dot(pick[offsets[m]:offsets[m] + sizes[m], :], tokens_ref[...]).astype(BF)


def pack(chip, adapters, slots, tokens, sizes, first_rows, chip_slots, steps=4):
    rows, width = tokens.shape
    block = width // steps
    spread = sum(round_up(s, 128) for s in sizes)
    return pl.pallas_call(
        functools.partial(pack_kernel, (sizes, first_rows, chip_slots, block - 1)),
        grid=(steps,),
        in_specs=[
            pl.BlockSpec(memory_space=pltpu.SMEM),
            pl.BlockSpec((1, rows), lambda i: (0, 0)),
            pl.BlockSpec((1, slots.shape[1]), lambda i: (0, 0)),
            pl.BlockSpec((rows, block), lambda i: (0, i)),
        ],
        out_specs=[pl.BlockSpec((s, block), lambda i: (0, i)) for s in sizes]
        + [pl.BlockSpec((rows, 128), lambda i: (0, 0))],
        out_shape=[jax.ShapeDtypeStruct((s, width), BF) for s in sizes] + [jax.ShapeDtypeStruct((rows, 128), jnp.int32)],
        scratch_shapes=[pltpu.VMEM((spread, rows), BF)],
        cost_estimate=COST,
        compiler_params=pltpu.CompilerParams(vmem_limit_bytes=VMEM_LIMIT),
        name="pack_rows",
    )(chip, adapters, slots, tokens)


def shrink_kernel(count, flag_lane, core_ref, *refs):
    messages, (mine, sibling) = refs[:count], refs[count:count + 2]
    out, place_out, flag_out, total, places = refs[count + 2:]
    step = pl.program_id(0)
    local = 2 * pl.num_programs(0)
    sizes = [m.shape[0] for m in messages]

    @pl.when(step == 0)
    def _():
        flag = jnp.zeros((1, 1), F32)
        start = 0
        for m, size in zip(messages, sizes):
            padded = round_up(size, 128)
            tail = m[size - 16:size, 0:padded].astype(F32)[15:16, :]
            same = lax.broadcasted_iota(jnp.int32, (size, padded), 0) == lax.broadcasted_iota(jnp.int32, (size, padded), 1)
            column = jnp.sum(jnp.where(same, tail, 0.0), axis=1, keepdims=True)
            places[start:start + size, :] = jnp.broadcast_to(column, (size, 128))
            block = m[size - 16:size, flag_lane - 127:flag_lane + 1].astype(F32)[15:16, :]
            last = lax.broadcasted_iota(jnp.int32, (1, 128), 1) == 127
            flag = jnp.maximum(flag, jnp.max(jnp.where(last, block, 0.0), axis=1, keepdims=True))
            start += size
        place_out[...] = places[...].astype(BF)
        flag_out[...] = jnp.broadcast_to(flag, (8, 128))
        total[...] = jnp.zeros_like(total)

    rows = messages[0][...] if count == 1 else jnp.concatenate([m[...] for m in messages], axis=0)
    place = places[...]
    core = core_ref[0]
    for weights, side in ((mine, core), (sibling, 1 - core)):
        product = dot(rows, jnp.concatenate([weights[0], weights[1]], axis=1))
        first = (side * local + 2 * step + 1).astype(F32)
        total[...] += jnp.where(place == first, product[:, :128], 0.0) + jnp.where(
            place == first + 1.0, product[:, 128:], 0.0
        )

    @pl.when(step == pl.num_programs(0) - 1)
    def _():
        out[...] = total[...].astype(out.dtype)


def shrink(core, messages, mine, sibling, flag_lane, dtype=BF):
    local, width, both = mine.shape
    rows = sum(m.shape[0] for m in messages)
    whole = [pl.BlockSpec(m.shape, lambda i: (0, 0)) for m in messages]
    pair = pl.BlockSpec((2, width, both), lambda i: (i, 0, 0))
    keep = pl.BlockSpec((rows, both), lambda i: (0, 0))
    return pl.pallas_call(
        functools.partial(shrink_kernel, len(messages), flag_lane),
        grid=(local // 2,),
        in_specs=[pl.BlockSpec(memory_space=pltpu.SMEM)] + whole + [pair, pair],
        out_specs=[keep, keep, pl.BlockSpec((8, 128), lambda i: (0, 0))],
        out_shape=[
            jax.ShapeDtypeStruct((rows, both), dtype),
            jax.ShapeDtypeStruct((rows, both), BF),
            jax.ShapeDtypeStruct((8, 128), F32),
        ],
        scratch_shapes=[pltpu.VMEM((rows, both), F32), pltpu.VMEM((rows, both), F32)],
        cost_estimate=pl.CostEstimate(
            flops=8 * rows * width * local * both, bytes_accessed=8 * width * local * both, transcendentals=0
        ),
        compiler_params=pltpu.CompilerParams(vmem_limit_bytes=VMEM_LIMIT),
        name="shrink_rows",
    )(core, *messages, mine, sibling)


def grow_kernel(shares, sizes, core_ref, *refs):
    parts, place_ref, mine, sibling = refs[:shares], refs[shares], refs[shares + 1], refs[shares + 2]
    outs = refs[shares + 3:]
    summed = parts[0][...].astype(F32)
    for part in parts[1:]:
        summed = summed + part[...].astype(F32)
    shrunk = summed.astype(BF).astype(F32)
    place = place_ref[...].astype(F32)
    local, _, rank, columns = mine.shape
    core = core_ref[0]
    low = lax.broadcasted_iota(jnp.int32, shrunk.shape, 1) < rank
    turned = pltpu.roll(shrunk, rank, 1)
    result = []
    for j in range(2):
        twice = jnp.where(low, shrunk, turned) if j == 0 else jnp.where(low, turned, shrunk)
        total = None
        for weights, side in ((mine, core), (sibling, 1 - core)):
            left = []
            for e in range(0, local, 2):
                first = (side * local + e + 1).astype(F32)
                wanted = jnp.where(low, first, first + 1.0)
                left.append(jnp.where(place == wanted, twice, 0.0).astype(BF))
            right = weights[:, j].reshape(local * rank, columns)
            product = dot(jnp.concatenate(left, axis=1), right)
            total = product if total is None else total + product
        result.append((adapter_scale * total).astype(BF))
    start = 0
    for out, size in zip(outs, sizes):
        out[:, :columns] = result[0][start:start + size, :]
        out[:, columns:] = result[1][start:start + size, :]
        start += size


def grow(core, parts, place, mine, sibling, sizes):
    columns = mine.shape[3]
    vmem = pl.BlockSpec(memory_space=pltpu.VMEM)
    return pl.pallas_call(
        functools.partial(grow_kernel, len(parts), sizes),
        in_specs=[pl.BlockSpec(memory_space=pltpu.SMEM)] + [vmem] * (len(parts) + 3),
        out_specs=[vmem] * len(sizes),
        out_shape=[jax.ShapeDtypeStruct((s, 2 * columns), BF) for s in sizes],
        cost_estimate=COST,
        compiler_params=pltpu.CompilerParams(vmem_limit_bytes=VMEM_LIMIT),
        name="grow_rows",
    )(core, *parts, place, mine, sibling)


def base_kernel(shifts, place_ref, tokens_ref, weight_ref, *outs):
    step = pl.program_id(0)
    weight = jnp.swapaxes(weight_ref[...], 0, 1)
    columns = weight.shape[2]
    both = [dot(tokens_ref[...], weight[j]) for j in range(2)]
    for i, out in enumerate(outs):

        @pl.when(step == i)
        def _():
            for j in range(2):
                out[:, j * columns:(j + 1) * columns] = both[j].astype(out.dtype)


def base_parts(t, tokens, weight, blocks, shifts):
    rows, width = tokens.shape
    columns = weight.shape[2] // blocks
    types = [BF if r % 2 else F32 for r in shifts]
    if columns % 128:
        cut = [lax.dynamic_slice_in_dim(weight, (t ^ r) * columns, columns, 2) for r in shifts]
        return [dot(tokens, c.reshape(width, 2 * columns)).astype(k) for c, k in zip(cut, types)]

    def block(i, place):
        shift = shifts[0]
        for k, r in enumerate(shifts[1:], 1):
            shift = jnp.where(i == k, r, shift)
        return 0, 0, place[0] ^ shift

    return pl.pallas_call(
        functools.partial(base_kernel, shifts),
        grid_spec=pltpu.PrefetchScalarGridSpec(
            num_scalar_prefetch=1,
            grid=(len(shifts),),
            in_specs=[
                pl.BlockSpec((rows, width), lambda i, p: (0, 0)),
                pl.BlockSpec((width, 2, columns), block),
            ],
            out_specs=[pl.BlockSpec((rows, 2 * columns), lambda i, p: (0, 0))] * len(shifts),
        ),
        out_shape=[jax.ShapeDtypeStruct((rows, 2 * columns), k) for k in types],
        cost_estimate=pl.CostEstimate(
            flops=16 * len(shifts) * rows * width * columns, bytes_accessed=8 * width * columns, transcendentals=0
        ),
        compiler_params=pltpu.CompilerParams(vmem_limit_bytes=VMEM_MOST),
        name="base_parts",
    )(t.reshape(1), tokens, weight)


def spread_kernel(sizes, first_rows, key_ref, out):
    start = 0
    for m, size in enumerate(sizes):
        padded = round_up(size, 128)
        lane = lax.broadcasted_iota(jnp.int32, (key_ref.shape[0], padded), 1)
        hit = (lane == key_ref[:, 0:1] - first_rows[m] - m * 65536) & (lane < size - 1)
        out[:, start:start + padded] = hit.astype(F32).astype(BF)
        start += padded


def spread_of(key, sizes, first_rows):
    vmem = pl.BlockSpec(memory_space=pltpu.VMEM)
    total = sum(round_up(size, 128) for size in sizes)
    return pl.pallas_call(
        functools.partial(spread_kernel, sizes, first_rows),
        in_specs=[vmem],
        out_specs=vmem,
        out_shape=jax.ShapeDtypeStruct((key.shape[0], total), BF),
        cost_estimate=COST,
        compiler_params=pltpu.CompilerParams(vmem_limit_bytes=VMEM_LIMIT),
        name="spread_rows",
    )(key)


def finish_kernel(sizes, count, *refs):
    bases, spreads, out = refs[:count], refs[count:count + len(sizes)], refs[-1]
    updates = refs[count + len(sizes):-1]
    total = bases[0][...]
    for base in bases[1:]:
        total = total + base[...].astype(F32)
    update_rows = jnp.zeros(total.shape, F32)
    done = 0
    for spread, group in zip(spreads, sizes):
        start = 0
        for size in group:
            padded = round_up(size, 128)
            rows = updates[done][...]
            if padded > size:
                rows = jnp.concatenate([rows, jnp.zeros((padded - size, rows.shape[1]), rows.dtype)], axis=0)
            update_rows = update_rows + dot(spread[:, start:start + padded], rows)
            start += padded
            done += 1
    total = total + update_rows
    columns = out.shape[2]
    if columns % 128:
        out[:, 0, :] = total[:, :columns].astype(BF)
        out[:, 1, :] = total[:, columns:].astype(BF)
    else:
        both = jnp.stack([total[:, :columns], total[:, columns:]], axis=0).astype(BF)
        out[...] = jnp.swapaxes(both, 0, 1)


def finish(bases, spreads, groups):
    sizes = tuple(tuple(u.shape[0] for u in group) for group in groups)
    rows, both = bases[0].shape
    updates = [u for group in groups for u in group]
    block = rows // 4
    return pl.pallas_call(
        functools.partial(finish_kernel, sizes, len(bases)),
        grid=(4,),
        in_specs=[pl.BlockSpec((block, x.shape[1]), lambda i: (i, 0)) for x in bases + spreads]
        + [pl.BlockSpec(u.shape, lambda i: (0, 0)) for u in updates],
        out_specs=pl.BlockSpec((block, 2, both // 2), lambda i: (i, 0, 0)),
        out_shape=jax.ShapeDtypeStruct((rows, 2, both // 2), BF),
        cost_estimate=COST,
        compiler_params=pltpu.CompilerParams(vmem_limit_bytes=VMEM_LIMIT),
        name="finish_rows",
    )(*bases, *spreads, *updates)


def exchange(array, axis, shift):
    size = lax.axis_size(axis)
    return lax.ppermute(array, axis, [(i, i ^ shift) for i in range(size)])


def after(array, *others):
    return lax.optimization_barrier((array,) + others)[0]


def bits(value):
    return bin(value).count("1")


def per_device(
    tokens,
    row_adapter_index,
    adapter_storage_slot,
    key_value_base_weight,
    adapter_down_weight,
    adapter_up_weight,
):
    row_count, width = tokens.shape
    local = adapter_down_weight.shape[0]
    groups = lax.axis_size("dp")
    blocks = lax.axis_size("tensor")
    experts = local * groups
    chips = groups // 2
    capacity = max(2, 2 * row_count // experts)
    chip_slots = 2 * local
    full = chip_slots * capacity

    me = lax.axis_index("dp").astype(jnp.int32)
    chip, core = (me // 2).reshape(1), (me % 2).reshape(1)
    adapters = row_adapter_index.reshape(1, row_count)
    slots = adapter_storage_slot.reshape(1, experts)
    flag_lane = width // 4 - 1

    down_sibling = exchange(adapter_down_weight, "dp", 1)

    near = [m for m in range(chips) if bits(m) <= 1]
    far = [m for m in range(chips) if bits(m) > 1]
    message = round_up(full * 11 // 16, 16)
    rest = round_up(full - message + 2, 16)
    sizes, first_rows = (message,) * chips, (0,) * chips

    t = lax.axis_index("tensor").astype(jnp.int32)
    first_shift = blocks - 1
    parts, came = {}, {}

    def compute(shifts, ready):
        parts.update(zip(shifts, base_parts(t, ready, key_value_base_weight, blocks, shifts)))

    def arrived_for(r):
        return [came[key] for key in sorted(came) if key[1] == r]

    def send(r):
        part = parts[r]
        for one in arrived_for(r):
            part = part + one.astype(F32)
        part = part.astype(BF)
        came[(r & -r, r ^ (r & -r))] = exchange(part, "tensor", r & -r)
        return part

    compute([first_shift], tokens)
    send(first_shift)
    packed = pack(chip, adapters, slots, after(tokens, parts[first_shift]), sizes, first_rows, chip_slots)
    sent, key = list(packed[:-1]), packed[-1]
    arrived, returned = {0: sent[0]}, {}
    for m in near[1:]:
        arrived[m] = exchange(sent[m], "dp", 2 * m)
    middle = list(range(1, first_shift))
    compute(middle, after(tokens, *sent))
    for r in sorted(middle, key=lambda r: (r & -r, -r)):
        last_sent = send(r)

    up_sibling = exchange(after(adapter_up_weight, down_sibling), "dp", 1)
    near_done = [arrived[m] for m in near[1:]]
    for m in far:
        arrived[m] = exchange(after(sent[m], *near_done, last_sent), "dp", 2 * m)

    both_down = after(down_sibling, up_sibling)
    flags, updates = [], {}
    for part in (near, far):
        if not part:
            continue
        group = [arrived[m] for m in part]
        if part is near:
            share, place, flag = shrink(core, group, adapter_down_weight, both_down, flag_lane, F32)
            compute([0], after(tokens, share))
            step = 1
            while 2 * step < blocks:
                share = share + exchange(share.astype(BF), "tensor", step).astype(F32)
                step *= 2
            shares = [share, exchange(share.astype(BF), "tensor", step)]
            base = after(parts[0], share)
            for one in arrived_for(0):
                base = base + one.astype(F32)
        else:
            group[0] = after(group[0], base, shares[-1])
            share, place, flag = shrink(core, group, adapter_down_weight, both_down, flag_lane)
            shares = [after(share, returned[0])] + [exchange(share, "tensor", z) for z in range(1, blocks)]
        flags.append(flag)
        grown = grow(core, shares, place, adapter_up_weight, up_sibling, tuple(sizes[m] for m in part))
        for m, update in zip(part, grown):
            returned[m] = update if m == 0 else exchange(update, "dp", 2 * m)
    spread = spread_of(after(key, base), sizes, first_rows)
    flag = functools.reduce(jnp.maximum, flags)
    flag = jnp.maximum(flag, exchange(flag, "dp", 1))
    updates = [returned[m] for m in range(chips)]

    def as_is():
        return finish([base], [spread], [updates])

    def second_round():
        later_sizes, later_rows = (rest,) * chips, (message - 1,) * chips
        packed = pack(chip, adapters, slots, tokens, later_sizes, later_rows, chip_slots)
        group = [packed[0]] + [exchange(packed[m], "dp", 2 * m) for m in range(1, chips)]
        share, place, _ = shrink(core, group, adapter_down_weight, down_sibling, flag_lane)
        shares = [share] + [exchange(share, "tensor", z) for z in range(1, blocks)]
        grown = grow(core, shares, place, adapter_up_weight, up_sibling, later_sizes)
        back = [grown[0]] + [exchange(grown[m], "dp", 2 * m) for m in range(1, chips)]
        return finish([base], [spread, spread_of(packed[-1], later_sizes, later_rows)], [updates, back])

    return lax.cond(flag[0, 0] > 0.0, second_round, as_is)


def solution(mesh):
    placed = (
        P("dp", "tensor"),
        P("dp", None),
        P(),
        P("tensor", None, None),
        P("dp", "tensor", None),
        P("dp", None, None, "tensor"),
    )
    return jax.shard_map(
        per_device, mesh=mesh, in_specs=placed, out_specs=P("dp", None, "tensor"), check_vma=False
    )
```

```python
import functools

import jax
import jax.numpy as jnp
from jax import lax
from jax.experimental import pallas as pl
from jax.experimental.pallas import tpu as pltpu
from jax.sharding import PartitionSpec as P

adapter_scale = 0.5
BF = jnp.bfloat16
F32 = jnp.float32
VMEM_LIMIT = 28 * 1024 * 1024
VMEM_MOST = 57 * 1024 * 1024
COST = pl.CostEstimate(flops=1000, bytes_accessed=1000, transcendentals=0)


def round_up(value, unit):
    return (value + unit - 1) // unit * unit


def dot(a, b, contract=((1,), (0,))):
    return lax.dot_general(a, b, (contract, ((), ())), preferred_element_type=F32)


def pack_kernel(shape, place_ref, adapter_ref, slot_ref, tokens_ref, *refs):
    sizes, first_rows, chip_slots, flag_lane = shape
    messages = len(sizes)
    outs, key_ref, pick = refs[:messages], refs[messages], refs[messages + 1]
    rows, width = tokens_ref.shape
    experts = slot_ref.shape[1]
    offsets = [sum(round_up(s, 128) for s in sizes[:m]) for m in range(messages)]

    @pl.when(pl.program_id(0) == 0)
    def _():
        named = (lax.broadcasted_iota(jnp.int32, (experts, rows), 0) == adapter_ref[...]).astype(BF)
        slots = jnp.broadcast_to(slot_ref[...].astype(F32), (16, experts)).astype(BF)
        slot = dot(slots, named)[0:1, :].astype(jnp.int32)
        shift = (slot // chip_slots) ^ place_ref[0]
        within = (slot % chip_slots + 1).astype(F32)
        lanes = round_up(messages, 16)
        goes = lax.broadcasted_iota(jnp.int32, (lanes, rows), 0) == shift
        earlier = lax.broadcasted_iota(jnp.int32, (rows, rows), 0) < lax.broadcasted_iota(jnp.int32, (rows, rows), 1)
        goes_f = goes.astype(F32)
        rank = dot(goes_f.astype(BF), earlier.astype(F32).astype(BF))
        position = jnp.sum(rank * goes_f, axis=0, keepdims=True).astype(jnp.int32)
        counts = jnp.sum(goes_f, axis=1, keepdims=True)
        sub = lax.broadcasted_iota(jnp.int32, (lanes, 1), 0)
        limit = jnp.zeros((lanes, 1), F32)
        for m in range(messages):
            limit = jnp.where(sub == m, F32(first_rows[m] + sizes[m] - 1), limit)
        over = jnp.max(jnp.where((sub < messages) & (counts > limit), 1.0, 0.0), axis=0, keepdims=True)
        key = jnp.broadcast_to(position + shift * 65536, (8, rows))
        key_ref[...] = jnp.broadcast_to(key.astype(F32).T[:, 0:1].astype(jnp.int32), key_ref.shape)
        within8 = jnp.broadcast_to(within, (16, rows)).astype(BF)
        for m in range(messages):
            padded = round_up(sizes[m], 128)
            target = lax.broadcasted_iota(jnp.int32, (padded, rows), 0)
            hit = (target + first_rows[m] == position) & (shift == m) & (target < sizes[m] - 1)
            chosen = hit.astype(F32).astype(BF)
            pick[offsets[m]:offsets[m] + padded, :] = chosen
            places = dot(within8, chosen, ((1,), (1,)))[0:1, :]
            if padded < width:
                places = jnp.concatenate([places, jnp.zeros((1, width - padded), F32)], axis=1)
            lane = lax.broadcasted_iota(jnp.int32, (1, width), 1)
            places = jnp.where(lane == flag_lane, over, places)
            body = dot(chosen, tokens_ref[...])[:sizes[m], :]
            row = lax.broadcasted_iota(jnp.int32, (sizes[m], 1), 0)
            outs[m][...] = jnp.where(row == sizes[m] - 1, places, body).astype(BF)

    @pl.when(pl.program_id(0) > 0)
    def _():
        for m in range(messages):
            outs[m][...] = dot(pick[offsets[m]:offsets[m] + sizes[m], :], tokens_ref[...]).astype(BF)


def pack(chip, adapters, slots, tokens, sizes, first_rows, chip_slots, steps=4):
    rows, width = tokens.shape
    block = width // steps
    spread = sum(round_up(s, 128) for s in sizes)
    return pl.pallas_call(
        functools.partial(pack_kernel, (sizes, first_rows, chip_slots, block - 1)),
        grid=(steps,),
        in_specs=[
            pl.BlockSpec(memory_space=pltpu.SMEM),
            pl.BlockSpec((1, rows), lambda i: (0, 0)),
            pl.BlockSpec((1, slots.shape[1]), lambda i: (0, 0)),
            pl.BlockSpec((rows, block), lambda i: (0, i)),
        ],
        out_specs=[pl.BlockSpec((s, block), lambda i: (0, i)) for s in sizes]
        + [pl.BlockSpec((rows, 128), lambda i: (0, 0))],
        out_shape=[jax.ShapeDtypeStruct((s, width), BF) for s in sizes] + [jax.ShapeDtypeStruct((rows, 128), jnp.int32)],
        scratch_shapes=[pltpu.VMEM((spread, rows), BF)],
        cost_estimate=COST,
        compiler_params=pltpu.CompilerParams(vmem_limit_bytes=VMEM_LIMIT),
        name="pack_rows",
    )(chip, adapters, slots, tokens)


def shrink_kernel(count, flag_lane, core_ref, *refs):
    messages, (mine, sibling) = refs[:count], refs[count:count + 2]
    out, place_out, flag_out, total, places = refs[count + 2:]
    step = pl.program_id(0)
    local = 2 * pl.num_programs(0)
    sizes = [m.shape[0] for m in messages]

    @pl.when(step == 0)
    def _():
        flag = jnp.zeros((1, 1), F32)
        start = 0
        for m, size in zip(messages, sizes):
            padded = round_up(size, 128)
            tail = m[size - 16:size, 0:padded].astype(F32)[15:16, :]
            same = lax.broadcasted_iota(jnp.int32, (size, padded), 0) == lax.broadcasted_iota(jnp.int32, (size, padded), 1)
            column = jnp.sum(jnp.where(same, tail, 0.0), axis=1, keepdims=True)
            places[start:start + size, :] = jnp.broadcast_to(column, (size, 128))
            block = m[size - 16:size, flag_lane - 127:flag_lane + 1].astype(F32)[15:16, :]
            last = lax.broadcasted_iota(jnp.int32, (1, 128), 1) == 127
            flag = jnp.maximum(flag, jnp.max(jnp.where(last, block, 0.0), axis=1, keepdims=True))
            start += size
        place_out[...] = places[...].astype(BF)
        flag_out[...] = jnp.broadcast_to(flag, (8, 128))
        total[...] = jnp.zeros_like(total)

    rows = messages[0][...] if count == 1 else jnp.concatenate([m[...] for m in messages], axis=0)
    place = places[...]
    core = core_ref[0]
    for weights, side in ((mine, core), (sibling, 1 - core)):
        product = dot(rows, jnp.concatenate([weights[0], weights[1]], axis=1))
        first = (side * local + 2 * step + 1).astype(F32)
        total[...] += jnp.where(place == first, product[:, :128], 0.0) + jnp.where(
            place == first + 1.0, product[:, 128:], 0.0
        )

    @pl.when(step == pl.num_programs(0) - 1)
    def _():
        out[...] = total[...].astype(out.dtype)


def shrink(core, messages, mine, sibling, flag_lane, dtype=BF):
    local, width, both = mine.shape
    rows = sum(m.shape[0] for m in messages)
    whole = [pl.BlockSpec(m.shape, lambda i: (0, 0)) for m in messages]
    pair = pl.BlockSpec((2, width, both), lambda i: (i, 0, 0))
    keep = pl.BlockSpec((rows, both), lambda i: (0, 0))
    return pl.pallas_call(
        functools.partial(shrink_kernel, len(messages), flag_lane),
        grid=(local // 2,),
        in_specs=[pl.BlockSpec(memory_space=pltpu.SMEM)] + whole + [pair, pair],
        out_specs=[keep, keep, pl.BlockSpec((8, 128), lambda i: (0, 0))],
        out_shape=[
            jax.ShapeDtypeStruct((rows, both), dtype),
            jax.ShapeDtypeStruct((rows, both), BF),
            jax.ShapeDtypeStruct((8, 128), F32),
        ],
        scratch_shapes=[pltpu.VMEM((rows, both), F32), pltpu.VMEM((rows, both), F32)],
        cost_estimate=pl.CostEstimate(
            flops=1000, bytes_accessed=1000, transcendentals=0
        ),
        compiler_params=pltpu.CompilerParams(vmem_limit_bytes=VMEM_LIMIT),
        name="shrink_rows",
    )(core, *messages, mine, sibling)


def grow_kernel(shares, sizes, core_ref, *refs):
    parts, place_ref, mine, sibling = refs[:shares], refs[shares], refs[shares + 1], refs[shares + 2]
    outs = refs[shares + 3:]
    summed = parts[0][...].astype(F32)
    for part in parts[1:]:
        summed = summed + part[...].astype(F32)
    shrunk = summed.astype(BF).astype(F32)
    place = place_ref[...].astype(F32)
    local, _, rank, columns = mine.shape
    core = core_ref[0]
    low = lax.broadcasted_iota(jnp.int32, shrunk.shape, 1) < rank
    turned = pltpu.roll(shrunk, rank, 1)
    result = []
    for j in range(2):
        twice = jnp.where(low, shrunk, turned) if j == 0 else jnp.where(low, turned, shrunk)
        total = None
        for weights, side in ((mine, core), (sibling, 1 - core)):
            left = []
            for e in range(0, local, 2):
                first = (side * local + e + 1).astype(F32)
                wanted = jnp.where(low, first, first + 1.0)
                left.append(jnp.where(place == wanted, twice, 0.0).astype(BF))
            right = weights[:, j].reshape(local * rank, columns)
            product = dot(jnp.concatenate(left, axis=1), right)
            total = product if total is None else total + product
        result.append((adapter_scale * total).astype(BF))
    start = 0
    for out, size in zip(outs, sizes):
        out[:, :columns] = result[0][start:start + size, :]
        out[:, columns:] = result[1][start:start + size, :]
        start += size


def grow(core, parts, place, mine, sibling, sizes):
    columns = mine.shape[3]
    vmem = pl.BlockSpec(memory_space=pltpu.VMEM)
    return pl.pallas_call(
        functools.partial(grow_kernel, len(parts), sizes),
        in_specs=[pl.BlockSpec(memory_space=pltpu.SMEM)] + [vmem] * (len(parts) + 3),
        out_specs=[vmem] * len(sizes),
        out_shape=[jax.ShapeDtypeStruct((s, 2 * columns), BF) for s in sizes],
        cost_estimate=COST,
        compiler_params=pltpu.CompilerParams(vmem_limit_bytes=VMEM_LIMIT),
        name="grow_rows",
    )(core, *parts, place, mine, sibling)


def base_kernel(shifts, place_ref, tokens_ref, weight_ref, *outs):
    step = pl.program_id(0)
    weight = jnp.swapaxes(weight_ref[...], 0, 1)
    columns = weight.shape[2]
    both = [dot(tokens_ref[...], weight[j]) for j in range(2)]
    for i, out in enumerate(outs):

        @pl.when(step == i)
        def _():
            for j in range(2):
                out[:, j * columns:(j + 1) * columns] = both[j].astype(out.dtype)


def base_parts(t, tokens, weight, blocks, shifts):
    rows, width = tokens.shape
    columns = weight.shape[2] // blocks
    types = [BF if r % 2 else F32 for r in shifts]
    if columns % 128:
        cut = [lax.dynamic_slice_in_dim(weight, (t ^ r) * columns, columns, 2) for r in shifts]
        return [dot(tokens, c.reshape(width, 2 * columns)).astype(k) for c, k in zip(cut, types)]

    def block(i, place):
        shift = shifts[0]
        for k, r in enumerate(shifts[1:], 1):
            shift = jnp.where(i == k, r, shift)
        return 0, 0, place[0] ^ shift

    return pl.pallas_call(
        functools.partial(base_kernel, shifts),
        grid_spec=pltpu.PrefetchScalarGridSpec(
            num_scalar_prefetch=1,
            grid=(len(shifts),),
            in_specs=[
                pl.BlockSpec((rows, width), lambda i, p: (0, 0)),
                pl.BlockSpec((width, 2, columns), block),
            ],
            out_specs=[pl.BlockSpec((rows, 2 * columns), lambda i, p: (0, 0))] * len(shifts),
        ),
        out_shape=[jax.ShapeDtypeStruct((rows, 2 * columns), k) for k in types],
        cost_estimate=pl.CostEstimate(
            flops=16 * len(shifts) * rows * width * columns, bytes_accessed=8 * width * columns, transcendentals=0
        ),
        compiler_params=pltpu.CompilerParams(vmem_limit_bytes=VMEM_MOST),
        name="base_parts",
    )(t.reshape(1), tokens, weight)


def spread_kernel(sizes, first_rows, key_ref, out):
    start = 0
    for m, size in enumerate(sizes):
        padded = round_up(size, 128)
        lane = lax.broadcasted_iota(jnp.int32, (key_ref.shape[0], padded), 1)
        hit = (lane == key_ref[:, 0:1] - first_rows[m] - m * 65536) & (lane < size - 1)
        out[:, start:start + padded] = hit.astype(F32).astype(BF)
        start += padded


def spread_of(key, sizes, first_rows):
    vmem = pl.BlockSpec(memory_space=pltpu.VMEM)
    total = sum(round_up(size, 128) for size in sizes)
    return pl.pallas_call(
        functools.partial(spread_kernel, sizes, first_rows),
        in_specs=[vmem],
        out_specs=vmem,
        out_shape=jax.ShapeDtypeStruct((key.shape[0], total), BF),
        cost_estimate=COST,
        compiler_params=pltpu.CompilerParams(vmem_limit_bytes=VMEM_LIMIT),
        name="spread_rows",
    )(key)


def finish_kernel(sizes, count, *refs):
    bases, spreads, out = refs[:count], refs[count:count + len(sizes)], refs[-1]
    updates = refs[count + len(sizes):-1]
    total = bases[0][...]
    for base in bases[1:]:
        total = total + base[...].astype(F32)
    update_rows = jnp.zeros(total.shape, F32)
    done = 0
    for spread, group in zip(spreads, sizes):
        start = 0
        for size in group:
            padded = round_up(size, 128)
            rows = updates[done][...]
            if padded > size:
                rows = jnp.concatenate([rows, jnp.zeros((padded - size, rows.shape[1]), rows.dtype)], axis=0)
            update_rows = update_rows + dot(spread[:, start:start + padded], rows)
            start += padded
            done += 1
    total = total + update_rows
    columns = out.shape[2]
    if columns % 128:
        out[:, 0, :] = total[:, :columns].astype(BF)
        out[:, 1, :] = total[:, columns:].astype(BF)
    else:
        both = jnp.stack([total[:, :columns], total[:, columns:]], axis=0).astype(BF)
        out[...] = jnp.swapaxes(both, 0, 1)


def finish(bases, spreads, groups):
    sizes = tuple(tuple(u.shape[0] for u in group) for group in groups)
    rows, both = bases[0].shape
    updates = [u for group in groups for u in group]
    block = rows // 4
    return pl.pallas_call(
        functools.partial(finish_kernel, sizes, len(bases)),
        grid=(4,),
        in_specs=[pl.BlockSpec((block, x.shape[1]), lambda i: (i, 0)) for x in bases + spreads]
        + [pl.BlockSpec(u.shape, lambda i: (0, 0)) for u in updates],
        out_specs=pl.BlockSpec((block, 2, both // 2), lambda i: (i, 0, 0)),
        out_shape=jax.ShapeDtypeStruct((rows, 2, both // 2), BF),
        cost_estimate=COST,
        compiler_params=pltpu.CompilerParams(vmem_limit_bytes=VMEM_LIMIT),
        name="finish_rows",
    )(*bases, *spreads, *updates)


def exchange(array, axis, shift):
    size = lax.axis_size(axis)
    return lax.ppermute(array, axis, [(i, i ^ shift) for i in range(size)])


def after(array, *others):
    return lax.optimization_barrier((array,) + others)[0]


def bits(value):
    return bin(value).count("1")


def per_device(
    tokens,
    row_adapter_index,
    adapter_storage_slot,
    key_value_base_weight,
    adapter_down_weight,
    adapter_up_weight,
):
    row_count, width = tokens.shape
    local = adapter_down_weight.shape[0]
    groups = lax.axis_size("dp")
    blocks = lax.axis_size("tensor")
    experts = local * groups
    chips = groups // 2
    capacity = max(2, 2 * row_count // experts)
    chip_slots = 2 * local
    full = chip_slots * capacity

    me = lax.axis_index("dp").astype(jnp.int32)
    chip, core = (me // 2).reshape(1), (me % 2).reshape(1)
    adapters = row_adapter_index.reshape(1, row_count)
    slots = adapter_storage_slot.reshape(1, experts)
    flag_lane = width // 4 - 1

    down_sibling = exchange(adapter_down_weight, "dp", 1)

    near = [m for m in range(chips) if bits(m) <= 1]
    far = [m for m in range(chips) if bits(m) > 1]
    message = round_up(full * 11 // 16, 16)
    rest = round_up(full - message + 2, 16)
    sizes, first_rows = (message,) * chips, (0,) * chips

    t = lax.axis_index("tensor").astype(jnp.int32)
    first_shift = blocks - 1
    parts, came = {}, {}

    def compute(shifts, ready):
        parts.update(zip(shifts, base_parts(t, ready, key_value_base_weight, blocks, shifts)))

    def arrived_for(r):
        return [came[key] for key in sorted(came) if key[1] == r]

    def send(r):
        part = parts[r]
        for one in arrived_for(r):
            part = part + one.astype(F32)
        part = part.astype(BF)
        came[(r & -r, r ^ (r & -r))] = exchange(part, "tensor", r & -r)
        return part

    compute([first_shift], tokens)
    send(first_shift)
    packed = pack(chip, adapters, slots, after(tokens, parts[first_shift]), sizes, first_rows, chip_slots)
    sent, key = list(packed[:-1]), packed[-1]
    arrived, returned = {0: sent[0]}, {}
    for m in near[1:]:
        arrived[m] = exchange(sent[m], "dp", 2 * m)
    middle = list(range(1, first_shift))
    compute(middle, after(tokens, *sent))
    for r in sorted(middle, key=lambda r: (r & -r, -r)):
        last_sent = send(r)

    up_sibling = exchange(after(adapter_up_weight, down_sibling), "dp", 1)
    near_done = [arrived[m] for m in near[1:]]
    for m in far:
        arrived[m] = exchange(after(sent[m], last_sent), "dp", 2 * m)

    both_down = after(down_sibling, up_sibling)
    flags, updates = [], {}
    for part in (near, far):
        if not part:
            continue
        group = [arrived[m] for m in part]
        if part is near:
            share, place, flag = shrink(core, group, adapter_down_weight, both_down, flag_lane, F32)
            compute([0], after(tokens, share))
            step = 1
            while 2 * step < blocks:
                share = share + exchange(share.astype(BF), "tensor", step).astype(F32)
                step *= 2
            shares = [share, exchange(share.astype(BF), "tensor", step)]
            base = after(parts[0], share)
            for one in arrived_for(0):
                base = base + one.astype(F32)
        else:
            group[0] = after(group[0], base)
            share, place, flag = shrink(core, group, adapter_down_weight, both_down, flag_lane)
            shares = [after(share, returned[0])] + [exchange(share, "tensor", z) for z in range(1, blocks)]
        flags.append(flag)
        grown = grow(core, shares, place, adapter_up_weight, up_sibling, tuple(sizes[m] for m in part))
        for m, update in zip(part, grown):
            returned[m] = update if m == 0 else exchange(update, "dp", 2 * m)
    spread = spread_of(after(key, base), sizes, first_rows)
    flag = functools.reduce(jnp.maximum, flags)
    flag = jnp.maximum(flag, exchange(flag, "dp", 1))
    updates = [returned[m] for m in range(chips)]

    def as_is():
        return finish([base], [spread], [updates])

    def second_round():
        later_sizes, later_rows = (rest,) * chips, (message - 1,) * chips
        packed = pack(chip, adapters, slots, tokens, later_sizes, later_rows, chip_slots)
        group = [packed[0]] + [exchange(packed[m], "dp", 2 * m) for m in range(1, chips)]
        share, place, _ = shrink(core, group, adapter_down_weight, down_sibling, flag_lane)
        shares = [share] + [exchange(share, "tensor", z) for z in range(1, blocks)]
        grown = grow(core, shares, place, adapter_up_weight, up_sibling, later_sizes)
        back = [grown[0]] + [exchange(grown[m], "dp", 2 * m) for m in range(1, chips)]
        return finish([base], [spread, spread_of(packed[-1], later_sizes, later_rows)], [updates, back])

    return lax.cond(flag[0, 0] > 0.0, second_round, as_is)


def solution(mesh):
    placed = (
        P("dp", "tensor"),
        P("dp", None),
        P(),
        P("tensor", None, None),
        P("dp", "tensor", None),
        P("dp", None, None, "tensor"),
    )
    return jax.shard_map(
        per_device, mesh=mesh, in_specs=placed, out_specs=P("dp", None, "tensor"), check_vma=False
    )
```

```python
import functools

import jax
import jax.numpy as jnp
from jax import lax
from jax.experimental import pallas as pl
from jax.experimental.pallas import tpu as pltpu
from jax.sharding import PartitionSpec as P

adapter_scale = 0.5
BF = jnp.bfloat16
F32 = jnp.float32
VMEM_LIMIT = 28 * 1024 * 1024
VMEM_MOST = 57 * 1024 * 1024
COST = pl.CostEstimate(flops=1000, bytes_accessed=1000, transcendentals=0)


def round_up(value, unit):
    return (value + unit - 1) // unit * unit


def dot(a, b, contract=((1,), (0,))):
    return lax.dot_general(a, b, (contract, ((), ())), preferred_element_type=F32)


def pack_kernel(shape, place_ref, adapter_ref, slot_ref, tokens_ref, *refs):
    sizes, first_rows, chip_slots, flag_lane = shape
    messages = len(sizes)
    outs, key_ref, pick = refs[:messages], refs[messages], refs[messages + 1]
    rows, width = tokens_ref.shape
    experts = slot_ref.shape[1]
    offsets = [sum(round_up(s, 128) for s in sizes[:m]) for m in range(messages)]

    @pl.when(pl.program_id(0) == 0)
    def _():
        named = (lax.broadcasted_iota(jnp.int32, (experts, rows), 0) == adapter_ref[...]).astype(BF)
        slots = jnp.broadcast_to(slot_ref[...].astype(F32), (16, experts)).astype(BF)
        slot = dot(slots, named)[0:1, :].astype(jnp.int32)
        shift = (slot // chip_slots) ^ place_ref[0]
        within = (slot % chip_slots + 1).astype(F32)
        lanes = round_up(messages, 16)
        goes = lax.broadcasted_iota(jnp.int32, (lanes, rows), 0) == shift
        earlier = lax.broadcasted_iota(jnp.int32, (rows, rows), 0) < lax.broadcasted_iota(jnp.int32, (rows, rows), 1)
        goes_f = goes.astype(F32)
        rank = dot(goes_f.astype(BF), earlier.astype(F32).astype(BF))
        position = jnp.sum(rank * goes_f, axis=0, keepdims=True).astype(jnp.int32)
        counts = jnp.sum(goes_f, axis=1, keepdims=True)
        sub = lax.broadcasted_iota(jnp.int32, (lanes, 1), 0)
        limit = jnp.zeros((lanes, 1), F32)
        for m in range(messages):
            limit = jnp.where(sub == m, F32(first_rows[m] + sizes[m] - 1), limit)
        over = jnp.max(jnp.where((sub < messages) & (counts > limit), 1.0, 0.0), axis=0, keepdims=True)
        key = jnp.broadcast_to(position + shift * 65536, (8, rows))
        key_ref[...] = jnp.broadcast_to(key.astype(F32).T[:, 0:1].astype(jnp.int32), key_ref.shape)
        within8 = jnp.broadcast_to(within, (16, rows)).astype(BF)
        for m in range(messages):
            padded = round_up(sizes[m], 128)
            target = lax.broadcasted_iota(jnp.int32, (padded, rows), 0)
            hit = (target + first_rows[m] == position) & (shift == m) & (target < sizes[m] - 1)
            chosen = hit.astype(F32).astype(BF)
            pick[offsets[m]:offsets[m] + padded, :] = chosen
            places = dot(within8, chosen, ((1,), (1,)))[0:1, :]
            if padded < width:
                places = jnp.concatenate([places, jnp.zeros((1, width - padded), F32)], axis=1)
            lane = lax.broadcasted_iota(jnp.int32, (1, width), 1)
            places = jnp.where(lane == flag_lane, over, places)
            body = dot(chosen, tokens_ref[...])[:sizes[m], :]
            row = lax.broadcasted_iota(jnp.int32, (sizes[m], 1), 0)
            outs[m][...] = jnp.where(row == sizes[m] - 1, places, body).astype(BF)

    @pl.when(pl.program_id(0) > 0)
    def _():
        for m in range(messages):
            outs[m][...] = dot(pick[offsets[m]:offsets[m] + sizes[m], :], tokens_ref[...]).astype(BF)


def pack(chip, adapters, slots, tokens, sizes, first_rows, chip_slots, steps=4):
    rows, width = tokens.shape
    block = width // steps
    spread = sum(round_up(s, 128) for s in sizes)
    return pl.pallas_call(
        functools.partial(pack_kernel, (sizes, first_rows, chip_slots, block - 1)),
        grid=(steps,),
        in_specs=[
            pl.BlockSpec(memory_space=pltpu.SMEM),
            pl.BlockSpec((1, rows), lambda i: (0, 0)),
            pl.BlockSpec((1, slots.shape[1]), lambda i: (0, 0)),
            pl.BlockSpec((rows, block), lambda i: (0, i)),
        ],
        out_specs=[pl.BlockSpec((s, block), lambda i: (0, i)) for s in sizes]
        + [pl.BlockSpec((rows, 128), lambda i: (0, 0))],
        out_shape=[jax.ShapeDtypeStruct((s, width), BF) for s in sizes] + [jax.ShapeDtypeStruct((rows, 128), jnp.int32)],
        scratch_shapes=[pltpu.VMEM((spread, rows), BF)],
        cost_estimate=COST,
        compiler_params=pltpu.CompilerParams(vmem_limit_bytes=VMEM_LIMIT),
        name="pack_rows",
    )(chip, adapters, slots, tokens)


def shrink_kernel(count, flag_lane, core_ref, *refs):
    messages, (mine, sibling) = refs[:count], refs[count:count + 2]
    out, place_out, flag_out, total, places = refs[count + 2:]
    step = pl.program_id(0)
    local = 2 * pl.num_programs(0)
    sizes = [m.shape[0] for m in messages]

    @pl.when(step == 0)
    def _():
        flag = jnp.zeros((1, 1), F32)
        start = 0
        for m, size in zip(messages, sizes):
            padded = round_up(size, 128)
            tail = m[size - 16:size, 0:padded].astype(F32)[15:16, :]
            same = lax.broadcasted_iota(jnp.int32, (size, padded), 0) == lax.broadcasted_iota(jnp.int32, (size, padded), 1)
            column = jnp.sum(jnp.where(same, tail, 0.0), axis=1, keepdims=True)
            places[start:start + size, :] = jnp.broadcast_to(column, (size, 128))
            block = m[size - 16:size, flag_lane - 127:flag_lane + 1].astype(F32)[15:16, :]
            last = lax.broadcasted_iota(jnp.int32, (1, 128), 1) == 127
            flag = jnp.maximum(flag, jnp.max(jnp.where(last, block, 0.0), axis=1, keepdims=True))
            start += size
        place_out[...] = places[...].astype(BF)
        flag_out[...] = jnp.broadcast_to(flag, (8, 128))
        total[...] = jnp.zeros_like(total)

    rows = messages[0][...] if count == 1 else jnp.concatenate([m[...] for m in messages], axis=0)
    place = places[...]
    core = core_ref[0]
    for weights, side in ((mine, core), (sibling, 1 - core)):
        product = dot(rows, jnp.concatenate([weights[0], weights[1]], axis=1))
        first = (side * local + 2 * step + 1).astype(F32)
        total[...] += jnp.where(place == first, product[:, :128], 0.0) + jnp.where(
            place == first + 1.0, product[:, 128:], 0.0
        )

    @pl.when(step == pl.num_programs(0) - 1)
    def _():
        out[...] = total[...].astype(out.dtype)


def shrink(core, messages, mine, sibling, flag_lane, dtype=BF):
    local, width, both = mine.shape
    rows = sum(m.shape[0] for m in messages)
    whole = [pl.BlockSpec(m.shape, lambda i: (0, 0)) for m in messages]
    pair = pl.BlockSpec((2, width, both), lambda i: (i, 0, 0))
    keep = pl.BlockSpec((rows, both), lambda i: (0, 0))
    return pl.pallas_call(
        functools.partial(shrink_kernel, len(messages), flag_lane),
        grid=(local // 2,),
        in_specs=[pl.BlockSpec(memory_space=pltpu.SMEM)] + whole + [pair, pair],
        out_specs=[keep, keep, pl.BlockSpec((8, 128), lambda i: (0, 0))],
        out_shape=[
            jax.ShapeDtypeStruct((rows, both), dtype),
            jax.ShapeDtypeStruct((rows, both), BF),
            jax.ShapeDtypeStruct((8, 128), F32),
        ],
        scratch_shapes=[pltpu.VMEM((rows, both), F32), pltpu.VMEM((rows, both), F32)],
        cost_estimate=pl.CostEstimate(
            flops=1000, bytes_accessed=1000, transcendentals=0
        ),
        compiler_params=pltpu.CompilerParams(vmem_limit_bytes=VMEM_LIMIT),
        name="shrink_rows",
    )(core, *messages, mine, sibling)


def grow_kernel(shares, sizes, core_ref, *refs):
    parts, place_ref, mine, sibling = refs[:shares], refs[shares], refs[shares + 1], refs[shares + 2]
    outs = refs[shares + 3:]
    summed = parts[0][...].astype(F32)
    for part in parts[1:]:
        summed = summed + part[...].astype(F32)
    shrunk = summed.astype(BF).astype(F32)
    place = place_ref[...].astype(F32)
    local, _, rank, columns = mine.shape
    core = core_ref[0]
    low = lax.broadcasted_iota(jnp.int32, shrunk.shape, 1) < rank
    turned = pltpu.roll(shrunk, rank, 1)
    result = []
    for j in range(2):
        twice = jnp.where(low, shrunk, turned) if j == 0 else jnp.where(low, turned, shrunk)
        total = None
        for weights, side in ((mine, core), (sibling, 1 - core)):
            left = []
            for e in range(0, local, 2):
                first = (side * local + e + 1).astype(F32)
                wanted = jnp.where(low, first, first + 1.0)
                left.append(jnp.where(place == wanted, twice, 0.0).astype(BF))
            right = weights[:, j].reshape(local * rank, columns)
            product = dot(jnp.concatenate(left, axis=1), right)
            total = product if total is None else total + product
        result.append((adapter_scale * total).astype(BF))
    start = 0
    for out, size in zip(outs, sizes):
        out[:, :columns] = result[0][start:start + size, :]
        out[:, columns:] = result[1][start:start + size, :]
        start += size


def grow(core, parts, place, mine, sibling, sizes):
    columns = mine.shape[3]
    vmem = pl.BlockSpec(memory_space=pltpu.VMEM)
    return pl.pallas_call(
        functools.partial(grow_kernel, len(parts), sizes),
        in_specs=[pl.BlockSpec(memory_space=pltpu.SMEM)] + [vmem] * (len(parts) + 3),
        out_specs=[vmem] * len(sizes),
        out_shape=[jax.ShapeDtypeStruct((s, 2 * columns), BF) for s in sizes],
        cost_estimate=COST,
        compiler_params=pltpu.CompilerParams(vmem_limit_bytes=VMEM_LIMIT),
        name="grow_rows",
    )(core, *parts, place, mine, sibling)


def base_kernel(shifts, place_ref, tokens_ref, weight_ref, *outs):
    step = pl.program_id(0)
    weight = jnp.swapaxes(weight_ref[...], 0, 1)
    columns = weight.shape[2]
    both = [dot(tokens_ref[...], weight[j]) for j in range(2)]
    for i, out in enumerate(outs):

        @pl.when(step == i)
        def _():
            for j in range(2):
                out[:, j * columns:(j + 1) * columns] = both[j].astype(out.dtype)


def base_parts(t, tokens, weight, blocks, shifts):
    rows, width = tokens.shape
    columns = weight.shape[2] // blocks
    types = [BF if r % 2 else F32 for r in shifts]
    if columns % 128:
        cut = [lax.dynamic_slice_in_dim(weight, (t ^ r) * columns, columns, 2) for r in shifts]
        return [dot(tokens, c.reshape(width, 2 * columns)).astype(k) for c, k in zip(cut, types)]

    def block(i, place):
        shift = shifts[0]
        for k, r in enumerate(shifts[1:], 1):
            shift = jnp.where(i == k, r, shift)
        return 0, 0, place[0] ^ shift

    return pl.pallas_call(
        functools.partial(base_kernel, shifts),
        grid_spec=pltpu.PrefetchScalarGridSpec(
            num_scalar_prefetch=1,
            grid=(len(shifts),),
            in_specs=[
                pl.BlockSpec((rows, width), lambda i, p: (0, 0)),
                pl.BlockSpec((width, 2, columns), block),
            ],
            out_specs=[pl.BlockSpec((rows, 2 * columns), lambda i, p: (0, 0))] * len(shifts),
        ),
        out_shape=[jax.ShapeDtypeStruct((rows, 2 * columns), k) for k in types],
        cost_estimate=pl.CostEstimate(
            flops=16 * len(shifts) * rows * width * columns, bytes_accessed=8 * width * columns, transcendentals=0
        ),
        compiler_params=pltpu.CompilerParams(vmem_limit_bytes=VMEM_MOST),
        name="base_parts",
    )(t.reshape(1), tokens, weight)


def spread_kernel(sizes, first_rows, key_ref, out):
    start = 0
    for m, size in enumerate(sizes):
        padded = round_up(size, 128)
        lane = lax.broadcasted_iota(jnp.int32, (key_ref.shape[0], padded), 1)
        hit = (lane == key_ref[:, 0:1] - first_rows[m] - m * 65536) & (lane < size - 1)
        out[:, start:start + padded] = hit.astype(F32).astype(BF)
        start += padded


def spread_of(key, sizes, first_rows):
    vmem = pl.BlockSpec(memory_space=pltpu.VMEM)
    total = sum(round_up(size, 128) for size in sizes)
    return pl.pallas_call(
        functools.partial(spread_kernel, sizes, first_rows),
        in_specs=[vmem],
        out_specs=vmem,
        out_shape=jax.ShapeDtypeStruct((key.shape[0], total), BF),
        cost_estimate=COST,
        compiler_params=pltpu.CompilerParams(vmem_limit_bytes=VMEM_LIMIT),
        name="spread_rows",
    )(key)


def finish_kernel(sizes, count, *refs):
    bases, spreads, out = refs[:count], refs[count:count + len(sizes)], refs[-1]
    updates = refs[count + len(sizes):-1]
    total = bases[0][...]
    for base in bases[1:]:
        total = total + base[...].astype(F32)
    update_rows = jnp.zeros(total.shape, F32)
    done = 0
    for spread, group in zip(spreads, sizes):
        start = 0
        for size in group:
            padded = round_up(size, 128)
            rows = updates[done][...]
            if padded > size:
                rows = jnp.concatenate([rows, jnp.zeros((padded - size, rows.shape[1]), rows.dtype)], axis=0)
            update_rows = update_rows + dot(spread[:, start:start + padded], rows)
            start += padded
            done += 1
    total = total + update_rows
    columns = out.shape[2]
    if columns % 128:
        out[:, 0, :] = total[:, :columns].astype(BF)
        out[:, 1, :] = total[:, columns:].astype(BF)
    else:
        both = jnp.stack([total[:, :columns], total[:, columns:]], axis=0).astype(BF)
        out[...] = jnp.swapaxes(both, 0, 1)


def finish(bases, spreads, groups):
    sizes = tuple(tuple(u.shape[0] for u in group) for group in groups)
    rows, both = bases[0].shape
    updates = [u for group in groups for u in group]
    block = rows // 4
    return pl.pallas_call(
        functools.partial(finish_kernel, sizes, len(bases)),
        grid=(4,),
        in_specs=[pl.BlockSpec((block, x.shape[1]), lambda i: (i, 0)) for x in bases + spreads]
        + [pl.BlockSpec(u.shape, lambda i: (0, 0)) for u in updates],
        out_specs=pl.BlockSpec((block, 2, both // 2), lambda i: (i, 0, 0)),
        out_shape=jax.ShapeDtypeStruct((rows, 2, both // 2), BF),
        cost_estimate=COST,
        compiler_params=pltpu.CompilerParams(vmem_limit_bytes=VMEM_LIMIT),
        name="finish_rows",
    )(*bases, *spreads, *updates)


def exchange(array, axis, shift):
    size = lax.axis_size(axis)
    return lax.ppermute(array, axis, [(i, i ^ shift) for i in range(size)])


def after(array, *others):
    return lax.optimization_barrier((array,) + others)[0]


def bits(value):
    return bin(value).count("1")


def per_device(
    tokens,
    row_adapter_index,
    adapter_storage_slot,
    key_value_base_weight,
    adapter_down_weight,
    adapter_up_weight,
):
    row_count, width = tokens.shape
    local = adapter_down_weight.shape[0]
    groups = lax.axis_size("dp")
    blocks = lax.axis_size("tensor")
    experts = local * groups
    chips = groups // 2
    capacity = max(2, 2 * row_count // experts)
    chip_slots = 2 * local
    full = chip_slots * capacity

    me = lax.axis_index("dp").astype(jnp.int32)
    chip, core = (me // 2).reshape(1), (me % 2).reshape(1)
    adapters = row_adapter_index.reshape(1, row_count)
    slots = adapter_storage_slot.reshape(1, experts)
    flag_lane = width // 4 - 1

    down_sibling = exchange(adapter_down_weight, "dp", 1)

    near = [m for m in range(chips) if bits(m) <= 1]
    far = [m for m in range(chips) if bits(m) > 1]
    message = round_up(full * 11 // 16, 16)
    rest = round_up(full - message + 2, 16)
    sizes, first_rows = (message,) * chips, (0,) * chips

    t = lax.axis_index("tensor").astype(jnp.int32)
    first_shift = blocks - 1
    parts, came = {}, {}

    def compute(shifts, ready):
        parts.update(zip(shifts, base_parts(t, ready, key_value_base_weight, blocks, shifts)))

    def arrived_for(r):
        return [came[key] for key in sorted(came) if key[1] == r]

    def send(r):
        part = parts[r]
        for one in arrived_for(r):
            part = part + one.astype(F32)
        part = part.astype(BF)
        came[(r & -r, r ^ (r & -r))] = exchange(part, "tensor", r & -r)
        return part

    compute([first_shift], tokens)
    send(first_shift)
    packed = pack(chip, adapters, slots, after(tokens, parts[first_shift]), sizes, first_rows, chip_slots)
    sent, key = list(packed[:-1]), packed[-1]
    arrived, returned = {0: sent[0]}, {}
    for m in near[1:]:
        arrived[m] = exchange(sent[m], "dp", 2 * m)
    middle = list(range(1, first_shift))
    compute(middle, after(tokens, *sent))
    for r in sorted(middle, key=lambda r: (r & -r, -r)):
        last_sent = send(r)

    up_sibling = exchange(after(adapter_up_weight, down_sibling), "dp", 1)
    near_done = [arrived[m] for m in near[1:]]
    for m in far:
        arrived[m] = exchange(after(sent[m], *near_done, last_sent), "dp", 2 * m)

    both_down = after(down_sibling, up_sibling)
    flags, updates = [], {}
    for part in (near, far):
        if not part:
            continue
        group = [arrived[m] for m in part]
        if part is near:
            share, place, flag = shrink(core, group, adapter_down_weight, both_down, flag_lane, F32)
            compute([0], after(tokens, share))
            step = 1
            while 2 * step < blocks:
                share = share + exchange(share.astype(BF), "tensor", step).astype(F32)
                step *= 2
            shares = [share, exchange(share.astype(BF), "tensor", step)]
            base = after(parts[0], share)
            for one in arrived_for(0):
                base = base + one.astype(F32)
        else:
            group[0] = after(group[0], base)
            share, place, flag = shrink(core, group, adapter_down_weight, both_down, flag_lane)
            shares = [after(share, returned[0])] + [exchange(share, "tensor", z) for z in range(1, blocks)]
        flags.append(flag)
        grown = grow(core, shares, place, adapter_up_weight, up_sibling, tuple(sizes[m] for m in part))
        for m, update in zip(part, grown):
            returned[m] = update if m == 0 else exchange(update, "dp", 2 * m)
    spread = spread_of(after(key, base), sizes, first_rows)
    flag = functools.reduce(jnp.maximum, flags)
    flag = jnp.maximum(flag, exchange(flag, "dp", 1))
    updates = [returned[m] for m in range(chips)]

    def as_is():
        return finish([base], [spread], [updates])

    def second_round():
        later_sizes, later_rows = (rest,) * chips, (message - 1,) * chips
        packed = pack(chip, adapters, slots, tokens, later_sizes, later_rows, chip_slots)
        group = [packed[0]] + [exchange(packed[m], "dp", 2 * m) for m in range(1, chips)]
        share, place, _ = shrink(core, group, adapter_down_weight, down_sibling, flag_lane)
        shares = [share] + [exchange(share, "tensor", z) for z in range(1, blocks)]
        grown = grow(core, shares, place, adapter_up_weight, up_sibling, later_sizes)
        back = [grown[0]] + [exchange(grown[m], "dp", 2 * m) for m in range(1, chips)]
        return finish([base], [spread, spread_of(packed[-1], later_sizes, later_rows)], [updates, back])

    return lax.cond(flag[0, 0] > 0.0, second_round, as_is)


def solution(mesh):
    placed = (
        P("dp", "tensor"),
        P("dp", None),
        P(),
        P("tensor", None, None),
        P("dp", "tensor", None),
        P("dp", None, None, "tensor"),
    )
    return jax.shard_map(
        per_device, mesh=mesh, in_specs=placed, out_specs=P("dp", None, "tensor"), check_vma=False
    )
```

```python
import functools

import jax
import jax.numpy as jnp
from jax import lax
from jax.experimental import pallas as pl
from jax.experimental.pallas import tpu as pltpu
from jax.sharding import PartitionSpec as P

adapter_scale = 0.5
BF = jnp.bfloat16
F32 = jnp.float32
VMEM_LIMIT = 28 * 1024 * 1024
VMEM_MOST = 57 * 1024 * 1024
COST = pl.CostEstimate(flops=1000, bytes_accessed=1000, transcendentals=0)


def round_up(value, unit):
    return (value + unit - 1) // unit * unit


def dot(a, b, contract=((1,), (0,))):
    return lax.dot_general(a, b, (contract, ((), ())), preferred_element_type=F32)


def pack_kernel(shape, place_ref, adapter_ref, slot_ref, tokens_ref, *refs):
    sizes, first_rows, chip_slots, flag_lane = shape
    messages = len(sizes)
    outs, key_ref, pick, tail = refs[:messages], *refs[messages:]
    rows, width = tokens_ref.shape
    experts = slot_ref.shape[1]
    offsets = [sum(sizes[:m]) for m in range(messages)]

    @pl.when(pl.program_id(0) == 0)
    def _():
        named = (lax.broadcasted_iota(jnp.int32, (experts, rows), 0) == adapter_ref[...]).astype(BF)
        slots = jnp.broadcast_to(slot_ref[...].astype(F32), (16, experts)).astype(BF)
        slot = dot(slots, named)[0:1, :].astype(jnp.int32)
        shift = (slot // chip_slots) ^ place_ref[0]
        within = (slot % chip_slots + 1).astype(F32)
        lanes = round_up(messages, 16)
        goes = lax.broadcasted_iota(jnp.int32, (lanes, rows), 0) == shift
        earlier = lax.broadcasted_iota(jnp.int32, (rows, rows), 0) < lax.broadcasted_iota(jnp.int32, (rows, rows), 1)
        goes_f = goes.astype(F32)
        rank = dot(goes_f.astype(BF), earlier.astype(F32).astype(BF))
        position = jnp.sum(rank * goes_f, axis=0, keepdims=True).astype(jnp.int32)
        counts = jnp.sum(goes_f, axis=1, keepdims=True)
        sub = lax.broadcasted_iota(jnp.int32, (lanes, 1), 0)
        limit = jnp.zeros((lanes, 1), F32)
        for m in range(messages):
            limit = jnp.where(sub == m, F32(first_rows[m] + sizes[m] - 1), limit)
        over = jnp.max(jnp.where((sub < messages) & (counts > limit), 1.0, 0.0), axis=0, keepdims=True)
        key = jnp.broadcast_to(position + shift * 65536, (8, rows))
        key_ref[...] = jnp.broadcast_to(key.astype(F32).T[:, 0:1].astype(jnp.int32), key_ref.shape)
        within8 = jnp.broadcast_to(within, (16, rows)).astype(BF)
        for m in range(messages):
            padded = round_up(sizes[m], 128)
            target = lax.broadcasted_iota(jnp.int32, (padded, rows), 0)
            hit = (target == position - first_rows[m]) & (shift == m) & (target < sizes[m] - 1)
            chosen = hit.astype(F32).astype(BF)
            pick[offsets[m]:offsets[m] + sizes[m], :] = chosen[:sizes[m], :]
            places = dot(within8, chosen, ((1,), (1,)))[0:1, :]
            if padded < width:
                places = jnp.concatenate([places, jnp.zeros((1, width - padded), F32)], axis=1)
            lane = lax.broadcasted_iota(jnp.int32, (1, width), 1)
            tail[m:m + 1, :] = jnp.where(lane == flag_lane, over, places)

    body = dot(pick[...], tokens_ref[...])
    for m in range(messages):
        outs[m][...] = body[offsets[m]:offsets[m] + sizes[m], :].astype(BF)

    @pl.when(pl.program_id(0) == 0)
    def _():
        for m in range(messages):
            end = outs[m][sizes[m] - 16:sizes[m], :].astype(F32)
            row = lax.broadcasted_iota(jnp.int32, (16, 1), 0)
            outs[m][sizes[m] - 16:sizes[m], :] = jnp.where(row == 15, tail[m:m + 1, :], end).astype(BF)


def pack(chip, adapters, slots, tokens, sizes, first_rows, chip_slots, steps=2):
    rows, width = tokens.shape
    block = width // steps
    return pl.pallas_call(
        functools.partial(pack_kernel, (sizes, first_rows, chip_slots, block - 1)),
        grid=(steps,),
        in_specs=[
            pl.BlockSpec(memory_space=pltpu.SMEM),
            pl.BlockSpec((1, rows), lambda i: (0, 0)),
            pl.BlockSpec((1, slots.shape[1]), lambda i: (0, 0)),
            pl.BlockSpec((rows, block), lambda i: (0, i)),
        ],
        out_specs=[pl.BlockSpec((s, block), lambda i: (0, i)) for s in sizes]
        + [pl.BlockSpec((rows, 128), lambda i: (0, 0))],
        out_shape=[jax.ShapeDtypeStruct((s, width), BF) for s in sizes] + [jax.ShapeDtypeStruct((rows, 128), jnp.int32)],
        scratch_shapes=[
            pltpu.VMEM((sum(sizes), rows), BF),
            pltpu.VMEM((round_up(len(sizes), 8), block), F32),
        ],
        cost_estimate=COST,
        compiler_params=pltpu.CompilerParams(vmem_limit_bytes=VMEM_LIMIT),
        name="pack_rows",
    )(chip, adapters, slots, tokens)


def shrink_kernel(count, flag_lane, core_ref, *refs):
    messages, (mine, sibling) = refs[:count], refs[count:count + 2]
    out, send_out, place_out, flag_out, places = refs[count + 2:]
    total = out
    step = pl.program_id(0)
    local = 2 * pl.num_programs(0)
    sizes = [m.shape[0] for m in messages]

    @pl.when(step == 0)
    def _():
        flag = jnp.zeros((1, 1), F32)
        start = 0
        for m, size in zip(messages, sizes):
            padded = round_up(size, 128)
            tail = m[size - 16:size, 0:padded].astype(F32)[15:16, :]
            same = lax.broadcasted_iota(jnp.int32, (size, padded), 0) == lax.broadcasted_iota(jnp.int32, (size, padded), 1)
            column = jnp.sum(jnp.where(same, tail, 0.0), axis=1, keepdims=True)
            places[start:start + size, :] = jnp.broadcast_to(column, (size, 128))
            block = m[size - 16:size, flag_lane - 127:flag_lane + 1].astype(F32)[15:16, :]
            last = lax.broadcasted_iota(jnp.int32, (1, 128), 1) == 127
            flag = jnp.maximum(flag, jnp.max(jnp.where(last, block, 0.0), axis=1, keepdims=True))
            start += size
        place_out[...] = places[...].astype(BF)
        flag_out[...] = jnp.broadcast_to(flag, (8, 128))
        total[...] = jnp.zeros_like(total)

    rows = messages[0][...] if count == 1 else jnp.concatenate([m[...] for m in messages], axis=0)
    place = places[...]
    core = core_ref[0]
    for weights, side in ((mine, core), (sibling, 1 - core)):
        product = dot(rows, jnp.concatenate([weights[0], weights[1]], axis=1))
        first = (side * local + 2 * step + 1).astype(F32)
        total[...] += jnp.where(place == first, product[:, :128], 0.0) + jnp.where(
            place == first + 1.0, product[:, 128:], 0.0
        )

    @pl.when(step == pl.num_programs(0) - 1)
    def _():
        send_out[...] = total[...].astype(BF)


def shrink(core, messages, mine, sibling, flag_lane):
    local, width, both = mine.shape
    rows = sum(m.shape[0] for m in messages)
    whole = [pl.BlockSpec(m.shape, lambda i: (0, 0)) for m in messages]
    pair = pl.BlockSpec((2, width, both), lambda i: (i, 0, 0))
    keep = pl.BlockSpec((rows, both), lambda i: (0, 0))
    return pl.pallas_call(
        functools.partial(shrink_kernel, len(messages), flag_lane),
        grid=(local // 2,),
        in_specs=[pl.BlockSpec(memory_space=pltpu.SMEM)] + whole + [pair, pair],
        out_specs=[keep, keep, keep, pl.BlockSpec((8, 128), lambda i: (0, 0))],
        out_shape=[
            jax.ShapeDtypeStruct((rows, both), F32),
            jax.ShapeDtypeStruct((rows, both), BF),
            jax.ShapeDtypeStruct((rows, both), BF),
            jax.ShapeDtypeStruct((8, 128), F32),
        ],
        scratch_shapes=[pltpu.VMEM((rows, both), F32)],
        cost_estimate=pl.CostEstimate(
            flops=1000, bytes_accessed=1000, transcendentals=0
        ),
        compiler_params=pltpu.CompilerParams(vmem_limit_bytes=VMEM_LIMIT),
        name="shrink_rows",
    )(core, *messages, mine, sibling)


def grow_kernel(shares, sizes, core_ref, *refs):
    parts, place_ref, mine, sibling = refs[:shares], refs[shares], refs[shares + 1], refs[shares + 2]
    outs = refs[shares + 3:]
    summed = parts[0][...].astype(F32)
    for part in parts[1:]:
        summed = summed + part[...].astype(F32)
    shrunk = summed.astype(BF).astype(F32)
    place = place_ref[...].astype(F32)
    local, _, rank, columns = mine.shape
    core = core_ref[0]
    low = lax.broadcasted_iota(jnp.int32, shrunk.shape, 1) < rank
    turned = pltpu.roll(shrunk, rank, 1)
    result = []
    for j in range(2):
        twice = jnp.where(low, shrunk, turned) if j == 0 else jnp.where(low, turned, shrunk)
        total = None
        for weights, side in ((mine, core), (sibling, 1 - core)):
            left = []
            for e in range(0, local, 2):
                first = (side * local + e + 1).astype(F32)
                wanted = jnp.where(low, first, first + 1.0)
                left.append(jnp.where(place == wanted, twice, 0.0).astype(BF))
            right = weights[:, j].reshape(local * rank, columns)
            product = dot(jnp.concatenate(left, axis=1), right)
            total = product if total is None else total + product
        result.append((adapter_scale * total).astype(BF))
    start = 0
    for out, size in zip(outs, sizes):
        out[:, :columns] = result[0][start:start + size, :]
        out[:, columns:] = result[1][start:start + size, :]
        start += size


def grow(core, parts, place, mine, sibling, sizes):
    columns = mine.shape[3]
    vmem = pl.BlockSpec(memory_space=pltpu.VMEM)
    return pl.pallas_call(
        functools.partial(grow_kernel, len(parts), sizes),
        in_specs=[pl.BlockSpec(memory_space=pltpu.SMEM)] + [vmem] * (len(parts) + 3),
        out_specs=[vmem] * len(sizes),
        out_shape=[jax.ShapeDtypeStruct((s, 2 * columns), BF) for s in sizes],
        cost_estimate=COST,
        compiler_params=pltpu.CompilerParams(vmem_limit_bytes=VMEM_LIMIT),
        name="grow_rows",
    )(core, *parts, place, mine, sibling)


def base_kernel(shifts, place_ref, tokens_ref, weight_ref, *outs):
    step = pl.program_id(0)
    weight = jnp.swapaxes(weight_ref[...], 0, 1)
    columns = weight.shape[2]
    both = [dot(tokens_ref[...], weight[j]) for j in range(2)]
    for i, out in enumerate(outs):

        @pl.when(step == i)
        def _():
            for j in range(2):
                out[:, j * columns:(j + 1) * columns] = both[j].astype(out.dtype)


def base_parts(t, tokens, weight, blocks, shifts):
    rows, width = tokens.shape
    columns = weight.shape[2] // blocks
    types = [BF if r % 2 else F32 for r in shifts]
    if columns % 128:
        cut = [lax.dynamic_slice_in_dim(weight, (t ^ r) * columns, columns, 2) for r in shifts]
        return [dot(tokens, c.reshape(width, 2 * columns)).astype(k) for c, k in zip(cut, types)]

    def block(i, place):
        shift = shifts[0]
        for k, r in enumerate(shifts[1:], 1):
            shift = jnp.where(i == k, r, shift)
        return 0, 0, place[0] ^ shift

    return pl.pallas_call(
        functools.partial(base_kernel, shifts),
        grid_spec=pltpu.PrefetchScalarGridSpec(
            num_scalar_prefetch=1,
            grid=(len(shifts),),
            in_specs=[
                pl.BlockSpec((rows, width), lambda i, p: (0, 0)),
                pl.BlockSpec((width, 2, columns), block),
            ],
            out_specs=[pl.BlockSpec((rows, 2 * columns), lambda i, p: (0, 0))] * len(shifts),
        ),
        out_shape=[jax.ShapeDtypeStruct((rows, 2 * columns), k) for k in types],
        cost_estimate=pl.CostEstimate(
            flops=16 * len(shifts) * rows * width * columns, bytes_accessed=8 * width * columns, transcendentals=0
        ),
        compiler_params=pltpu.CompilerParams(vmem_limit_bytes=VMEM_MOST),
        name="base_parts",
    )(t.reshape(1), tokens, weight)


def spread_kernel(sizes, first_rows, key_ref, out):
    start = 0
    for m, size in enumerate(sizes):
        padded = round_up(size, 128)
        lane = lax.broadcasted_iota(jnp.int32, (key_ref.shape[0], padded), 1)
        hit = (lane == key_ref[:, 0:1] - first_rows[m] - m * 65536) & (lane < size - 1)
        out[:, start:start + padded] = hit.astype(F32).astype(BF)
        start += padded


def spread_of(key, sizes, first_rows):
    vmem = pl.BlockSpec(memory_space=pltpu.VMEM)
    total = sum(round_up(size, 128) for size in sizes)
    return pl.pallas_call(
        functools.partial(spread_kernel, sizes, first_rows),
        in_specs=[vmem],
        out_specs=vmem,
        out_shape=jax.ShapeDtypeStruct((key.shape[0], total), BF),
        cost_estimate=COST,
        compiler_params=pltpu.CompilerParams(vmem_limit_bytes=VMEM_LIMIT),
        name="spread_rows",
    )(key)


def finish_kernel(sizes, count, *refs):
    bases, spreads, out = refs[:count], refs[count:count + len(sizes)], refs[-1]
    updates = refs[count + len(sizes):-1]
    total = bases[0][...]
    for base in bases[1:]:
        total = total + base[...].astype(F32)
    update_rows = jnp.zeros(total.shape, F32)
    done = 0
    for spread, group in zip(spreads, sizes):
        start = 0
        for size in group:
            padded = round_up(size, 128)
            rows = updates[done][...]
            if padded > size:
                rows = jnp.concatenate([rows, jnp.zeros((padded - size, rows.shape[1]), rows.dtype)], axis=0)
            update_rows = update_rows + dot(spread[:, start:start + padded], rows)
            start += padded
            done += 1
    total = total + update_rows
    columns = out.shape[2]
    if columns % 128:
        out[:, 0, :] = total[:, :columns].astype(BF)
        out[:, 1, :] = total[:, columns:].astype(BF)
    else:
        both = jnp.stack([total[:, :columns], total[:, columns:]], axis=0).astype(BF)
        out[...] = jnp.swapaxes(both, 0, 1)


def finish(bases, spreads, groups):
    sizes = tuple(tuple(u.shape[0] for u in group) for group in groups)
    rows, both = bases[0].shape
    updates = [u for group in groups for u in group]
    block = rows // 4
    return pl.pallas_call(
        functools.partial(finish_kernel, sizes, len(bases)),
        grid=(4,),
        in_specs=[pl.BlockSpec((block, x.shape[1]), lambda i: (i, 0)) for x in bases + spreads]
        + [pl.BlockSpec(u.shape, lambda i: (0, 0)) for u in updates],
        out_specs=pl.BlockSpec((block, 2, both // 2), lambda i: (i, 0, 0)),
        out_shape=jax.ShapeDtypeStruct((rows, 2, both // 2), BF),
        cost_estimate=COST,
        compiler_params=pltpu.CompilerParams(vmem_limit_bytes=VMEM_LIMIT),
        name="finish_rows",
    )(*bases, *spreads, *updates)


def exchange(array, axis, shift):
    size = lax.axis_size(axis)
    return lax.ppermute(array, axis, [(i, i ^ shift) for i in range(size)])


def after(array, *others):
    return lax.optimization_barrier((array,) + others)[0]


def bits(value):
    return bin(value).count("1")


def per_device(
    tokens,
    row_adapter_index,
    adapter_storage_slot,
    key_value_base_weight,
    adapter_down_weight,
    adapter_up_weight,
):
    row_count, width = tokens.shape
    local = adapter_down_weight.shape[0]
    groups = lax.axis_size("dp")
    blocks = lax.axis_size("tensor")
    experts = local * groups
    chips = groups // 2
    capacity = max(2, 2 * row_count // experts)
    chip_slots = 2 * local
    full = chip_slots * capacity

    me = lax.axis_index("dp").astype(jnp.int32)
    chip, core = (me // 2).reshape(1), (me % 2).reshape(1)
    adapters = row_adapter_index.reshape(1, row_count)
    slots = adapter_storage_slot.reshape(1, experts)
    flag_lane = width // 2 - 1

    down_sibling = exchange(adapter_down_weight, "dp", 1)

    near = [m for m in range(chips) if bits(m) <= 1]
    far = [m for m in range(chips) if bits(m) > 1]
    message = round_up(full * 11 // 16, 16)
    rest = round_up(full - message + 2, 16)
    sizes, first_rows = (message,) * chips, (0,) * chips

    t = lax.axis_index("tensor").astype(jnp.int32)
    first_shift = blocks - 1
    parts, came = {}, {}

    def compute(shifts, ready):
        parts.update(zip(shifts, base_parts(t, ready, key_value_base_weight, blocks, shifts)))

    def arrived_for(r):
        return [came[key] for key in sorted(came) if key[1] == r]

    def send(r):
        part = parts[r]
        for one in arrived_for(r):
            part = part + one.astype(F32)
        part = part.astype(BF)
        came[(r & -r, r ^ (r & -r))] = exchange(part, "tensor", r & -r)
        return part

    compute([first_shift], tokens)
    send(first_shift)
    packed = pack(chip, adapters, slots, after(tokens, parts[first_shift]), sizes, first_rows, chip_slots)
    sent, key = list(packed[:-1]), packed[-1]
    arrived, returned = {0: sent[0]}, {}
    for m in near[1:]:
        arrived[m] = exchange(sent[m], "dp", 2 * m)
    middle = list(range(1, first_shift))
    compute(middle, after(tokens, *sent))
    for r in sorted(middle, key=lambda r: (r & -r, -r)):
        last_sent = send(r)

    up_sibling = exchange(after(adapter_up_weight, down_sibling), "dp", 1)
    near_done = [arrived[m] for m in near[1:]]
    for m in far:
        arrived[m] = exchange(after(sent[m], *near_done, last_sent), "dp", 2 * m)

    both_down = after(down_sibling, up_sibling)
    flags, updates = [], {}
    for part in (near, far):
        if not part:
            continue
        group = [arrived[m] for m in part]
        if part is near:
            share, _, place, flag = shrink(core, group, adapter_down_weight, both_down, flag_lane)
            compute([0], after(tokens, share))
            step = 1
            while 2 * step < blocks:
                share = share + exchange(share if step == 1 else share.astype(BF), "tensor", step).astype(F32)
                step *= 2
            shares = [share, exchange(share.astype(BF), "tensor", step)]
            base = after(parts[0], share)
            for one in arrived_for(0):
                base = base + one.astype(F32)
        else:
            group[0] = after(group[0], base)
            share, rounded, place, flag = shrink(core, group, adapter_down_weight, both_down, flag_lane)
            shares = [after(share, returned[0])] + [exchange(rounded, "tensor", z) for z in range(1, blocks)]
        flags.append(flag)
        grown = grow(core, shares, place, adapter_up_weight, up_sibling, tuple(sizes[m] for m in part))
        for m, update in zip(part, grown):
            returned[m] = update if m == 0 else exchange(update, "dp", 2 * m)
    bases = [base]
    spread = spread_of(after(key, base), sizes, first_rows)
    flag = functools.reduce(jnp.maximum, flags)
    flag = jnp.maximum(flag, exchange(flag, "dp", 1))
    updates = [returned[m] for m in range(chips)]

    def as_is():
        return finish(bases, [spread], [updates])

    def second_round():
        later_sizes, later_rows = (rest,) * chips, (message - 1,) * chips
        packed = pack(chip, adapters, slots, tokens, later_sizes, later_rows, chip_slots)
        group = [packed[0]] + [exchange(packed[m], "dp", 2 * m) for m in range(1, chips)]
        share, rounded, place, _ = shrink(core, group, adapter_down_weight, down_sibling, flag_lane)
        shares = [share] + [exchange(rounded, "tensor", z) for z in range(1, blocks)]
        grown = grow(core, shares, place, adapter_up_weight, up_sibling, later_sizes)
        back = [grown[0]] + [exchange(grown[m], "dp", 2 * m) for m in range(1, chips)]
        return finish(bases, [spread, spread_of(packed[-1], later_sizes, later_rows)], [updates, back])

    return lax.cond(flag[0, 0] > 0.0, second_round, as_is)


def solution(mesh):
    placed = (
        P("dp", "tensor"),
        P("dp", None),
        P(),
        P("tensor", None, None),
        P("dp", "tensor", None),
        P("dp", None, None, "tensor"),
    )
    return jax.shard_map(
        per_device, mesh=mesh, in_specs=placed, out_specs=P("dp", None, "tensor"), check_vma=False
    )
```

```python
import functools

import jax
import jax.numpy as jnp
from jax import lax
from jax.experimental import pallas as pl
from jax.experimental.pallas import tpu as pltpu
from jax.sharding import PartitionSpec as P

adapter_scale = 0.5
BF = jnp.bfloat16
F32 = jnp.float32
VMEM_LIMIT = 28 * 1024 * 1024
VMEM_MOST = 57 * 1024 * 1024
COST = pl.CostEstimate(flops=1000, bytes_accessed=1000, transcendentals=0)


def round_up(value, unit):
    return (value + unit - 1) // unit * unit


def dot(a, b, contract=((1,), (0,))):
    return lax.dot_general(a, b, (contract, ((), ())), preferred_element_type=F32)


def pack_kernel(shape, place_ref, adapter_ref, slot_ref, tokens_ref, *refs):
    sizes, first_rows, chip_slots, flag_lane = shape
    messages = len(sizes)
    outs, key_ref, pick, tail = refs[:messages], *refs[messages:]
    rows, width = tokens_ref.shape
    experts = slot_ref.shape[1]
    offsets = [sum(sizes[:m]) for m in range(messages)]

    @pl.when(pl.program_id(0) == 0)
    def _():
        named = (lax.broadcasted_iota(jnp.int32, (experts, rows), 0) == adapter_ref[...]).astype(BF)
        slots = jnp.broadcast_to(slot_ref[...].astype(F32), (16, experts)).astype(BF)
        slot = dot(slots, named)[0:1, :].astype(jnp.int32)
        shift = (slot // chip_slots) ^ place_ref[0]
        within = (slot % chip_slots + 1).astype(F32)
        lanes = round_up(messages, 16)
        goes = lax.broadcasted_iota(jnp.int32, (lanes, rows), 0) == shift
        earlier = lax.broadcasted_iota(jnp.int32, (rows, rows), 0) < lax.broadcasted_iota(jnp.int32, (rows, rows), 1)
        goes_f = goes.astype(F32)
        rank = dot(goes_f.astype(BF), earlier.astype(F32).astype(BF))
        position = jnp.sum(rank * goes_f, axis=0, keepdims=True).astype(jnp.int32)
        counts = jnp.sum(goes_f, axis=1, keepdims=True)
        sub = lax.broadcasted_iota(jnp.int32, (lanes, 1), 0)
        limit = jnp.zeros((lanes, 1), F32)
        for m in range(messages):
            limit = jnp.where(sub == m, F32(first_rows[m] + sizes[m] - 1), limit)
        over = jnp.max(jnp.where((sub < messages) & (counts > limit), 1.0, 0.0), axis=0, keepdims=True)
        key = jnp.broadcast_to(position + shift * 65536, (8, rows))
        key_ref[...] = jnp.broadcast_to(key.astype(F32).T[:, 0:1].astype(jnp.int32), key_ref.shape)
        within8 = jnp.broadcast_to(within, (16, rows)).astype(BF)
        for m in range(messages):
            padded = round_up(sizes[m], 128)
            target = lax.broadcasted_iota(jnp.int32, (padded, rows), 0)
            hit = (target == position - first_rows[m]) & (shift == m) & (target < sizes[m] - 1)
            chosen = hit.astype(F32).astype(BF)
            pick[offsets[m]:offsets[m] + sizes[m], :] = chosen[:sizes[m], :]
            places = dot(within8, chosen, ((1,), (1,)))[0:1, :]
            if padded < width:
                places = jnp.concatenate([places, jnp.zeros((1, width - padded), F32)], axis=1)
            lane = lax.broadcasted_iota(jnp.int32, (1, width), 1)
            tail[m:m + 1, :] = jnp.where(lane == flag_lane, over, places)

    body = dot(pick[...], tokens_ref[...])
    for m in range(messages):
        outs[m][...] = body[offsets[m]:offsets[m] + sizes[m], :].astype(BF)

    @pl.when(pl.program_id(0) == 0)
    def _():
        for m in range(messages):
            end = outs[m][sizes[m] - 16:sizes[m], :].astype(F32)
            row = lax.broadcasted_iota(jnp.int32, (16, 1), 0)
            outs[m][sizes[m] - 16:sizes[m], :] = jnp.where(row == 15, tail[m:m + 1, :], end).astype(BF)


def pack(chip, adapters, slots, tokens, sizes, first_rows, chip_slots, steps=2):
    rows, width = tokens.shape
    block = width // steps
    return pl.pallas_call(
        functools.partial(pack_kernel, (sizes, first_rows, chip_slots, block - 1)),
        grid=(steps,),
        in_specs=[
            pl.BlockSpec(memory_space=pltpu.SMEM),
            pl.BlockSpec((1, rows), lambda i: (0, 0)),
            pl.BlockSpec((1, slots.shape[1]), lambda i: (0, 0)),
            pl.BlockSpec((rows, block), lambda i: (0, i)),
        ],
        out_specs=[pl.BlockSpec((s, block), lambda i: (0, i)) for s in sizes]
        + [pl.BlockSpec((rows, 128), lambda i: (0, 0))],
        out_shape=[jax.ShapeDtypeStruct((s, width), BF) for s in sizes] + [jax.ShapeDtypeStruct((rows, 128), jnp.int32)],
        scratch_shapes=[
            pltpu.VMEM((sum(sizes), rows), BF),
            pltpu.VMEM((round_up(len(sizes), 8), block), F32),
        ],
        cost_estimate=COST,
        compiler_params=pltpu.CompilerParams(vmem_limit_bytes=VMEM_LIMIT),
        name="pack_rows",
    )(chip, adapters, slots, tokens)


def shrink_kernel(count, carried, flag_lane, core_ref, *refs):
    messages, (mine, sibling) = refs[:count], refs[count:count + 2]
    carry, refs = refs[count + 2:count + 2 + carried], refs[count + 2 + carried:]
    out, send_out, place_out, flag_out, places = refs
    kept = carry[0].shape[0] if carried else 0
    total = out.at[kept:, :]
    step = pl.program_id(0)
    local = 2 * pl.num_programs(0)
    sizes = [m.shape[0] for m in messages]

    @pl.when(step == 0)
    def _():
        flag = jnp.zeros((1, 1), F32)
        start = 0
        for m, size in zip(messages, sizes):
            padded = round_up(size, 128)
            tail = m[size - 16:size, 0:padded].astype(F32)[15:16, :]
            same = lax.broadcasted_iota(jnp.int32, (size, padded), 0) == lax.broadcasted_iota(jnp.int32, (size, padded), 1)
            column = jnp.sum(jnp.where(same, tail, 0.0), axis=1, keepdims=True)
            places[start:start + size, :] = jnp.broadcast_to(column, (size, 128))
            block = m[size - 16:size, flag_lane - 127:flag_lane + 1].astype(F32)[15:16, :]
            last = lax.broadcasted_iota(jnp.int32, (1, 128), 1) == 127
            flag = jnp.maximum(flag, jnp.max(jnp.where(last, block, 0.0), axis=1, keepdims=True))
            start += size
        place_out[kept:, :] = places[...].astype(BF)
        if carried:
            out[:kept, :] = carry[0][...]
            place_out[:kept, :] = carry[1][...]
            flag = jnp.maximum(flag, carry[2][0:1, 0:1])
        flag_out[...] = jnp.broadcast_to(flag, (8, 128))
        total[...] = jnp.zeros_like(total)

    rows = messages[0][...] if count == 1 else jnp.concatenate([m[...] for m in messages], axis=0)
    place = places[...]
    core = core_ref[0]
    for weights, side in ((mine, core), (sibling, 1 - core)):
        product = dot(rows, jnp.concatenate([weights[0], weights[1]], axis=1))
        first = (side * local + 2 * step + 1).astype(F32)
        total[...] += jnp.where(place == first, product[:, :128], 0.0) + jnp.where(
            place == first + 1.0, product[:, 128:], 0.0
        )

    @pl.when(step == pl.num_programs(0) - 1)
    def _():
        send_out[...] = out[...].astype(BF)


def shrink(core, messages, mine, sibling, flag_lane, carry=()):
    local, width, both = mine.shape
    rows = sum(m.shape[0] for m in messages)
    whole = [pl.BlockSpec(m.shape, lambda i: (0, 0)) for m in messages]
    pair = pl.BlockSpec((2, width, both), lambda i: (i, 0, 0))
    every = rows + (carry[0].shape[0] if carry else 0)
    keep = pl.BlockSpec((every, both), lambda i: (0, 0))
    kept = [pl.BlockSpec(c.shape, lambda i: (0, 0)) for c in carry]
    return pl.pallas_call(
        functools.partial(shrink_kernel, len(messages), len(carry), flag_lane),
        grid=(local // 2,),
        in_specs=[pl.BlockSpec(memory_space=pltpu.SMEM)] + whole + [pair, pair] + kept,
        out_specs=[keep, keep, keep, pl.BlockSpec((8, 128), lambda i: (0, 0))],
        out_shape=[
            jax.ShapeDtypeStruct((every, both), F32),
            jax.ShapeDtypeStruct((every, both), BF),
            jax.ShapeDtypeStruct((every, both), BF),
            jax.ShapeDtypeStruct((8, 128), F32),
        ],
        scratch_shapes=[pltpu.VMEM((rows, both), F32)],
        cost_estimate=pl.CostEstimate(
            flops=1000, bytes_accessed=1000, transcendentals=0
        ),
        compiler_params=pltpu.CompilerParams(vmem_limit_bytes=VMEM_LIMIT),
        name="shrink_rows",
    )(core, *messages, mine, sibling, *carry)


def hold_kernel(source, out):
    out[...] = source[...]


def hold(array):
    block = pl.BlockSpec((2,) + array.shape[1:], lambda i: (i, 0, 0))
    return pl.pallas_call(
        hold_kernel,
        grid=(array.shape[0] // 2,),
        in_specs=[block],
        out_specs=block,
        out_shape=jax.ShapeDtypeStruct(array.shape, array.dtype),
        cost_estimate=COST,
        compiler_params=pltpu.CompilerParams(vmem_limit_bytes=VMEM_LIMIT),
        name="hold_weights",
    )(array)


def grow_kernel(shares, sizes, core_ref, *refs):
    parts, place_ref, mine, sibling = refs[:shares], refs[shares], refs[shares + 1], refs[shares + 2]
    outs = refs[shares + 3:]
    summed = parts[0][...].astype(F32)
    for part in parts[1:]:
        summed = summed + part[...].astype(F32)
    shrunk = summed.astype(BF).astype(F32)
    place = place_ref[...].astype(F32)
    local, _, rank, columns = mine.shape
    core = core_ref[0]
    low = lax.broadcasted_iota(jnp.int32, shrunk.shape, 1) < rank
    turned = pltpu.roll(shrunk, rank, 1)
    result = []
    for j in range(2):
        twice = jnp.where(low, shrunk, turned) if j == 0 else jnp.where(low, turned, shrunk)
        total = None
        for weights, side in ((mine, core), (sibling, 1 - core)):
            left = []
            for e in range(0, local, 2):
                first = (side * local + e + 1).astype(F32)
                wanted = jnp.where(low, first, first + 1.0)
                left.append(jnp.where(place == wanted, twice, 0.0).astype(BF))
            right = weights[:, j].reshape(local * rank, columns)
            product = dot(jnp.concatenate(left, axis=1), right)
            total = product if total is None else total + product
        result.append((adapter_scale * total).astype(BF))
    start = 0
    for out, size in zip(outs, sizes):
        out[:, :columns] = result[0][start:start + size, :]
        out[:, columns:] = result[1][start:start + size, :]
        start += size


def grow(core, parts, place, mine, sibling, sizes):
    columns = mine.shape[3]
    vmem = pl.BlockSpec(memory_space=pltpu.VMEM)
    return pl.pallas_call(
        functools.partial(grow_kernel, len(parts), sizes),
        in_specs=[pl.BlockSpec(memory_space=pltpu.SMEM)] + [vmem] * (len(parts) + 3),
        out_specs=[vmem] * len(sizes),
        out_shape=[jax.ShapeDtypeStruct((s, 2 * columns), BF) for s in sizes],
        cost_estimate=COST,
        compiler_params=pltpu.CompilerParams(vmem_limit_bytes=VMEM_LIMIT),
        name="grow_rows",
    )(core, *parts, place, mine, sibling)


def base_kernel(shifts, place_ref, tokens_ref, weight_ref, *outs):
    step = pl.program_id(0)
    weight = jnp.swapaxes(weight_ref[...], 0, 1)
    columns = weight.shape[2]
    both = [dot(tokens_ref[...], weight[j]) for j in range(2)]
    for i, out in enumerate(outs):

        @pl.when(step == i)
        def _():
            for j in range(2):
                out[:, j * columns:(j + 1) * columns] = both[j].astype(out.dtype)


def base_parts(t, tokens, weight, blocks, shifts, vmem=VMEM_LIMIT):
    rows, width = tokens.shape
    columns = weight.shape[2] // blocks
    types = [BF if r % 2 else F32 for r in shifts]
    if columns % 128:
        cut = [lax.dynamic_slice_in_dim(weight, (t ^ r) * columns, columns, 2) for r in shifts]
        return [dot(tokens, c.reshape(width, 2 * columns)).astype(k) for c, k in zip(cut, types)]

    def block(i, place):
        shift = shifts[0]
        for k, r in enumerate(shifts[1:], 1):
            shift = jnp.where(i == k, r, shift)
        return 0, 0, place[0] ^ shift

    return pl.pallas_call(
        functools.partial(base_kernel, shifts),
        grid_spec=pltpu.PrefetchScalarGridSpec(
            num_scalar_prefetch=1,
            grid=(len(shifts),),
            in_specs=[
                pl.BlockSpec((rows, width), lambda i, p: (0, 0)),
                pl.BlockSpec((width, 2, columns), block),
            ],
            out_specs=[pl.BlockSpec((rows, 2 * columns), lambda i, p: (0, 0))] * len(shifts),
        ),
        out_shape=[jax.ShapeDtypeStruct((rows, 2 * columns), k) for k in types],
        cost_estimate=pl.CostEstimate(
            flops=16 * len(shifts) * rows * width * columns, bytes_accessed=8 * width * columns, transcendentals=0
        ),
        compiler_params=pltpu.CompilerParams(vmem_limit_bytes=vmem),
        name="base_parts",
    )(t.reshape(1), tokens, weight)


def spread_kernel(sizes, first_rows, key_ref, out):
    start = 0
    for m, size in enumerate(sizes):
        padded = round_up(size, 128)
        lane = lax.broadcasted_iota(jnp.int32, (key_ref.shape[0], padded), 1)
        hit = (lane == key_ref[:, 0:1] - first_rows[m] - m * 65536) & (lane < size - 1)
        out[:, start:start + padded] = hit.astype(F32).astype(BF)
        start += padded


def spread_of(key, sizes, first_rows):
    vmem = pl.BlockSpec(memory_space=pltpu.VMEM)
    total = sum(round_up(size, 128) for size in sizes)
    return pl.pallas_call(
        functools.partial(spread_kernel, sizes, first_rows),
        in_specs=[vmem],
        out_specs=vmem,
        out_shape=jax.ShapeDtypeStruct((key.shape[0], total), BF),
        cost_estimate=COST,
        compiler_params=pltpu.CompilerParams(vmem_limit_bytes=VMEM_LIMIT),
        name="spread_rows",
    )(key)


def finish_kernel(sizes, count, *refs):
    bases, spreads, out = refs[:count], refs[count:count + len(sizes)], refs[-1]
    updates = refs[count + len(sizes):-1]
    total = bases[0][...]
    for base in bases[1:]:
        total = total + base[...].astype(F32)
    update_rows = jnp.zeros(total.shape, F32)
    done = 0
    for spread, group in zip(spreads, sizes):
        start = 0
        for size in group:
            padded = round_up(size, 128)
            rows = updates[done][...]
            if padded > size:
                rows = jnp.concatenate([rows, jnp.zeros((padded - size, rows.shape[1]), rows.dtype)], axis=0)
            update_rows = update_rows + dot(spread[:, start:start + padded], rows)
            start += padded
            done += 1
    total = total + update_rows
    columns = out.shape[2]
    if columns % 128:
        out[:, 0, :] = total[:, :columns].astype(BF)
        out[:, 1, :] = total[:, columns:].astype(BF)
    else:
        both = jnp.stack([total[:, :columns], total[:, columns:]], axis=0).astype(BF)
        out[...] = jnp.swapaxes(both, 0, 1)


def finish(bases, spreads, groups):
    sizes = tuple(tuple(u.shape[0] for u in group) for group in groups)
    rows, both = bases[0].shape
    updates = [u for group in groups for u in group]
    block = rows // 4
    return pl.pallas_call(
        functools.partial(finish_kernel, sizes, len(bases)),
        grid=(4,),
        in_specs=[pl.BlockSpec((block, x.shape[1]), lambda i: (i, 0)) for x in bases + spreads]
        + [pl.BlockSpec(u.shape, lambda i: (0, 0)) for u in updates],
        out_specs=pl.BlockSpec((block, 2, both // 2), lambda i: (i, 0, 0)),
        out_shape=jax.ShapeDtypeStruct((rows, 2, both // 2), BF),
        cost_estimate=COST,
        compiler_params=pltpu.CompilerParams(vmem_limit_bytes=VMEM_LIMIT),
        name="finish_rows",
    )(*bases, *spreads, *updates)


def exchange(array, axis, shift):
    size = lax.axis_size(axis)
    return lax.ppermute(array, axis, [(i, i ^ shift) for i in range(size)])


def after(array, *others):
    return lax.optimization_barrier((array,) + others)[0]


def bits(value):
    return bin(value).count("1")


def per_device(
    tokens,
    row_adapter_index,
    adapter_storage_slot,
    key_value_base_weight,
    adapter_down_weight,
    adapter_up_weight,
):
    row_count, width = tokens.shape
    local = adapter_down_weight.shape[0]
    groups = lax.axis_size("dp")
    blocks = lax.axis_size("tensor")
    experts = local * groups
    chips = groups // 2
    capacity = max(2, 2 * row_count // experts)
    chip_slots = 2 * local
    full = chip_slots * capacity

    me = lax.axis_index("dp").astype(jnp.int32)
    chip, core = (me // 2).reshape(1), (me % 2).reshape(1)
    adapters = row_adapter_index.reshape(1, row_count)
    slots = adapter_storage_slot.reshape(1, experts)
    flag_lane = width // 2 - 1

    down_sibling = exchange(adapter_down_weight, "dp", 1)

    near = [m for m in range(chips) if bits(m) <= 1]
    far = [m for m in range(chips) if bits(m) > 1]
    message = round_up(full * 11 // 16, 16)
    rest = round_up(full - message + 2, 16)
    sizes, first_rows = (message,) * chips, (0,) * chips

    t = lax.axis_index("tensor").astype(jnp.int32)
    first_shift = blocks - 1
    parts, came = {}, {}

    def compute(shifts, ready, vmem=VMEM_LIMIT):
        parts.update(zip(shifts, base_parts(t, ready, key_value_base_weight, blocks, shifts, vmem)))

    def arrived_for(r):
        return [came[key] for key in sorted(came) if key[1] == r]

    def send(r):
        part = parts[r]
        for one in arrived_for(r):
            part = part + one.astype(F32)
        part = part.astype(BF)
        came[(r & -r, r ^ (r & -r))] = exchange(part, "tensor", r & -r)
        return part

    odd, even = list(range(first_shift, 0, -2)), list(range(2, first_shift, 2))
    compute(odd, tokens, VMEM_MOST)
    for r in odd:
        send(r)
    packed = pack(chip, adapters, slots, after(tokens, parts[first_shift]), sizes, first_rows, chip_slots)
    sent, key = list(packed[:-1]), packed[-1]
    arrived, returned = {0: sent[0]}, {}
    for m in near[1:]:
        arrived[m] = exchange(sent[m], "dp", 2 * m)
    compute(even, after(tokens, *sent), VMEM_MOST)
    for r in sorted(even, key=lambda r: (r & -r, -r)):
        last_sent = send(r)

    up_sibling = exchange(after(adapter_up_weight, down_sibling), "dp", 1)
    held = hold(after(down_sibling, last_sent))
    carry = shrink(core, [sent[0]], adapter_down_weight, held, flag_lane)
    carry = (carry[0], carry[2], carry[3])
    near_done = [arrived[m] for m in near[1:]]
    for m in far:
        arrived[m] = exchange(after(sent[m], *near_done, carry[0]), "dp", 2 * m)

    both_down = after(held, up_sibling)
    flags, updates = [], {}
    for part in (near, far):
        if not part:
            continue
        group = [arrived[m] for m in part if m]
        if part is near:
            share, _, place, flag = shrink(core, group, adapter_down_weight, both_down, flag_lane, carry)
            compute([0], after(tokens, share))
            step = 1
            while 2 * step < blocks:
                share = share + exchange(share if step == 1 else share.astype(BF), "tensor", step).astype(F32)
                step *= 2
            shares = [share, exchange(share.astype(BF), "tensor", step)]
            base = after(parts[0], share)
            for one in arrived_for(0):
                base = base + one.astype(F32)
        else:
            group[0] = after(group[0], base)
            share, rounded, place, flag = shrink(core, group, adapter_down_weight, both_down, flag_lane)
            shares = [after(share, returned[0])] + [exchange(rounded, "tensor", z) for z in range(1, blocks)]
        flags.append(flag)
        grown = grow(core, shares, place, adapter_up_weight, up_sibling, tuple(sizes[m] for m in part))
        for m, update in zip(part, grown):
            returned[m] = update if m == 0 else exchange(update, "dp", 2 * m)
    bases = [base]
    spread = spread_of(after(key, base), sizes, first_rows)
    flag = functools.reduce(jnp.maximum, flags)
    flag = jnp.maximum(flag, exchange(flag, "dp", 1))
    updates = [returned[m] for m in range(chips)]

    def as_is():
        return finish(bases, [spread], [updates])

    def second_round():
        later_sizes, later_rows = (rest,) * chips, (message - 1,) * chips
        packed = pack(chip, adapters, slots, tokens, later_sizes, later_rows, chip_slots)
        group = [packed[0]] + [exchange(packed[m], "dp", 2 * m) for m in range(1, chips)]
        share, rounded, place, _ = shrink(core, group, adapter_down_weight, down_sibling, flag_lane)
        shares = [share] + [exchange(rounded, "tensor", z) for z in range(1, blocks)]
        grown = grow(core, shares, place, adapter_up_weight, up_sibling, later_sizes)
        back = [grown[0]] + [exchange(grown[m], "dp", 2 * m) for m in range(1, chips)]
        return finish(bases, [spread, spread_of(packed[-1], later_sizes, later_rows)], [updates, back])

    return lax.cond(flag[0, 0] > 0.0, second_round, as_is)


def solution(mesh):
    placed = (
        P("dp", "tensor"),
        P("dp", None),
        P(),
        P("tensor", None, None),
        P("dp", "tensor", None),
        P("dp", None, None, "tensor"),
    )
    return jax.shard_map(
        per_device, mesh=mesh, in_specs=placed, out_specs=P("dp", None, "tensor"), check_vma=False
    )
```

```python
import functools

import jax
import jax.numpy as jnp
from jax import lax
from jax.experimental import pallas as pl
from jax.experimental.pallas import tpu as pltpu
from jax.sharding import PartitionSpec as P

adapter_scale = 0.5
BF = jnp.bfloat16
F32 = jnp.float32
VMEM_LIMIT = 28 * 1024 * 1024
VMEM_MOST = 57 * 1024 * 1024
COST = pl.CostEstimate(flops=1000, bytes_accessed=1000, transcendentals=0)


def round_up(value, unit):
    return (value + unit - 1) // unit * unit


def dot(a, b, contract=((1,), (0,))):
    return lax.dot_general(a, b, (contract, ((), ())), preferred_element_type=F32)


def pack_kernel(shape, place_ref, adapter_ref, slot_ref, tokens_ref, *refs):
    sizes, first_rows, chip_slots, flag_lane = shape
    messages = len(sizes)
    outs, key_ref, pick, tail = refs[:messages], *refs[messages:]
    rows, width = tokens_ref.shape
    experts = slot_ref.shape[1]
    offsets = [sum(sizes[:m]) for m in range(messages)]

    @pl.when(pl.program_id(0) == 0)
    def _():
        named = (lax.broadcasted_iota(jnp.int32, (experts, rows), 0) == adapter_ref[...]).astype(BF)
        slots = jnp.broadcast_to(slot_ref[...].astype(F32), (16, experts)).astype(BF)
        slot = dot(slots, named)[0:1, :].astype(jnp.int32)
        shift = (slot // chip_slots) ^ place_ref[0]
        within = (slot % chip_slots + 1).astype(F32)
        lanes = round_up(messages, 16)
        goes = lax.broadcasted_iota(jnp.int32, (lanes, rows), 0) == shift
        earlier = lax.broadcasted_iota(jnp.int32, (rows, rows), 0) < lax.broadcasted_iota(jnp.int32, (rows, rows), 1)
        goes_f = goes.astype(F32)
        rank = dot(goes_f.astype(BF), earlier.astype(F32).astype(BF))
        position = jnp.sum(rank * goes_f, axis=0, keepdims=True).astype(jnp.int32)
        counts = jnp.sum(goes_f, axis=1, keepdims=True)
        sub = lax.broadcasted_iota(jnp.int32, (lanes, 1), 0)
        limit = jnp.zeros((lanes, 1), F32)
        for m in range(messages):
            limit = jnp.where(sub == m, F32(first_rows[m] + sizes[m] - 1), limit)
        over = jnp.max(jnp.where((sub < messages) & (counts > limit), 1.0, 0.0), axis=0, keepdims=True)
        key = jnp.broadcast_to(position + shift * 65536, (8, rows))
        key_ref[...] = jnp.broadcast_to(key.astype(F32).T[:, 0:1].astype(jnp.int32), key_ref.shape)
        within8 = jnp.broadcast_to(within, (16, rows)).astype(BF)
        for m in range(messages):
            padded = round_up(sizes[m], 128)
            target = lax.broadcasted_iota(jnp.int32, (padded, rows), 0)
            hit = (target == position - first_rows[m]) & (shift == m) & (target < sizes[m] - 1)
            chosen = hit.astype(F32).astype(BF)
            pick[offsets[m]:offsets[m] + sizes[m], :] = chosen[:sizes[m], :]
            places = dot(within8, chosen, ((1,), (1,)))[0:1, :]
            if padded < width:
                places = jnp.concatenate([places, jnp.zeros((1, width - padded), F32)], axis=1)
            lane = lax.broadcasted_iota(jnp.int32, (1, width), 1)
            tail[m:m + 1, :] = jnp.where(lane == flag_lane, over, places)

    body = dot(pick[...], tokens_ref[...])
    for m in range(messages):
        outs[m][...] = body[offsets[m]:offsets[m] + sizes[m], :].astype(BF)

    @pl.when(pl.program_id(0) == 0)
    def _():
        for m in range(messages):
            end = outs[m][sizes[m] - 16:sizes[m], :].astype(F32)
            row = lax.broadcasted_iota(jnp.int32, (16, 1), 0)
            outs[m][sizes[m] - 16:sizes[m], :] = jnp.where(row == 15, tail[m:m + 1, :], end).astype(BF)


def pack(chip, adapters, slots, tokens, sizes, first_rows, chip_slots, steps=2):
    rows, width = tokens.shape
    block = width // steps
    return pl.pallas_call(
        functools.partial(pack_kernel, (sizes, first_rows, chip_slots, block - 1)),
        grid=(steps,),
        in_specs=[
            pl.BlockSpec(memory_space=pltpu.SMEM),
            pl.BlockSpec((1, rows), lambda i: (0, 0)),
            pl.BlockSpec((1, slots.shape[1]), lambda i: (0, 0)),
            pl.BlockSpec((rows, block), lambda i: (0, i)),
        ],
        out_specs=[pl.BlockSpec((s, block), lambda i: (0, i)) for s in sizes]
        + [pl.BlockSpec((rows, 128), lambda i: (0, 0))],
        out_shape=[jax.ShapeDtypeStruct((s, width), BF) for s in sizes] + [jax.ShapeDtypeStruct((rows, 128), jnp.int32)],
        scratch_shapes=[
            pltpu.VMEM((sum(sizes), rows), BF),
            pltpu.VMEM((round_up(len(sizes), 8), block), F32),
        ],
        cost_estimate=COST,
        compiler_params=pltpu.CompilerParams(vmem_limit_bytes=VMEM_LIMIT),
        name="pack_rows",
    )(chip, adapters, slots, tokens)


def shrink_kernel(count, carried, flag_lane, core_ref, *refs):
    messages, (mine, sibling) = refs[:count], refs[count:count + 2]
    carry, refs = refs[count + 2:count + 2 + carried], refs[count + 2 + carried:]
    out, send_out, place_out, flag_out, places = refs
    kept = carry[0].shape[0] if carried else 0
    total = out.at[kept:, :]
    step = pl.program_id(0)
    local = mine.shape[0] * pl.num_programs(0)
    sizes = [m.shape[0] for m in messages]

    @pl.when(step == 0)
    def _():
        flag = jnp.zeros((1, 1), F32)
        start = 0
        for m, size in zip(messages, sizes):
            padded = round_up(size, 128)
            tail = m[size - 16:size, 0:padded].astype(F32)[15:16, :]
            same = lax.broadcasted_iota(jnp.int32, (size, padded), 0) == lax.broadcasted_iota(jnp.int32, (size, padded), 1)
            column = jnp.sum(jnp.where(same, tail, 0.0), axis=1, keepdims=True)
            places[start:start + size, :] = jnp.broadcast_to(column, (size, 128))
            block = m[size - 16:size, flag_lane - 127:flag_lane + 1].astype(F32)[15:16, :]
            last = lax.broadcasted_iota(jnp.int32, (1, 128), 1) == 127
            flag = jnp.maximum(flag, jnp.max(jnp.where(last, block, 0.0), axis=1, keepdims=True))
            start += size
        place_out[kept:, :] = places[...].astype(BF)
        if carried:
            out[:kept, :] = carry[0][...]
            place_out[:kept, :] = carry[1][...]
            flag = jnp.maximum(flag, carry[2][0:1, 0:1])
        flag_out[...] = jnp.broadcast_to(flag, (8, 128))
        total[...] = jnp.zeros_like(total)

    rows = messages[0][...] if count == 1 else jnp.concatenate([m[...] for m in messages], axis=0)
    place = places[...]
    core = core_ref[0]
    each = mine.shape[0]
    every = [weights[e] for weights in (mine, sibling) for e in range(each)]
    product = dot(rows, jnp.concatenate(every, axis=1))
    picked = total[...]
    for k, side in enumerate((core, 1 - core)):
        first = (side * local + each * step + 1).astype(F32)
        for e in range(each):
            start = 128 * (each * k + e)
            picked = picked + jnp.where(place == first + e, product[:, start:start + 128], 0.0)
    total[...] = picked

    @pl.when(step == pl.num_programs(0) - 1)
    def _():
        send_out[...] = out[...].astype(BF)


def shrink(core, messages, mine, sibling, flag_lane, carry=()):
    local, width, both = mine.shape
    rows = sum(m.shape[0] for m in messages)
    whole = [pl.BlockSpec(m.shape, lambda i: (0, 0)) for m in messages]
    pair = pl.BlockSpec((4, width, both), lambda i: (i, 0, 0))
    every = rows + (carry[0].shape[0] if carry else 0)
    keep = pl.BlockSpec((every, both), lambda i: (0, 0))
    kept = [pl.BlockSpec(c.shape, lambda i: (0, 0)) for c in carry]
    return pl.pallas_call(
        functools.partial(shrink_kernel, len(messages), len(carry), flag_lane),
        grid=(local // 4,),
        in_specs=[pl.BlockSpec(memory_space=pltpu.SMEM)] + whole + [pair, pair] + kept,
        out_specs=[keep, keep, keep, pl.BlockSpec((8, 128), lambda i: (0, 0))],
        out_shape=[
            jax.ShapeDtypeStruct((every, both), F32),
            jax.ShapeDtypeStruct((every, both), BF),
            jax.ShapeDtypeStruct((every, both), BF),
            jax.ShapeDtypeStruct((8, 128), F32),
        ],
        scratch_shapes=[pltpu.VMEM((rows, both), F32)],
        cost_estimate=pl.CostEstimate(
            flops=1000, bytes_accessed=1000, transcendentals=0
        ),
        compiler_params=pltpu.CompilerParams(vmem_limit_bytes=VMEM_LIMIT),
        name="shrink_rows",
    )(core, *messages, mine, sibling, *carry)


def hold_kernel(source, out):
    out[...] = source[...]


def hold(array):
    block = pl.BlockSpec((2,) + array.shape[1:], lambda i: (i, 0, 0))
    return pl.pallas_call(
        hold_kernel,
        grid=(array.shape[0] // 2,),
        in_specs=[block],
        out_specs=block,
        out_shape=jax.ShapeDtypeStruct(array.shape, array.dtype),
        cost_estimate=COST,
        compiler_params=pltpu.CompilerParams(vmem_limit_bytes=VMEM_LIMIT),
        name="hold_weights",
    )(array)


def grow_kernel(shares, sizes, core_ref, *refs):
    parts, place_ref, mine, sibling = refs[:shares], refs[shares], refs[shares + 1], refs[shares + 2]
    outs = refs[shares + 3:]
    summed = parts[0][...].astype(F32)
    for part in parts[1:]:
        summed = summed + part[...].astype(F32)
    shrunk = summed.astype(BF).astype(F32)
    place = place_ref[...].astype(F32)
    local, _, rank, columns = mine.shape
    core = core_ref[0]
    low = lax.broadcasted_iota(jnp.int32, shrunk.shape, 1) < rank
    turned = pltpu.roll(shrunk, rank, 1)
    result = []
    for j in range(2):
        twice = jnp.where(low, shrunk, turned) if j == 0 else jnp.where(low, turned, shrunk)
        total = None
        for weights, side in ((mine, core), (sibling, 1 - core)):
            left = []
            for e in range(0, local, 2):
                first = (side * local + e + 1).astype(F32)
                wanted = jnp.where(low, first, first + 1.0)
                left.append(jnp.where(place == wanted, twice, 0.0).astype(BF))
            right = weights[:, j].reshape(local * rank, columns)
            product = dot(jnp.concatenate(left, axis=1), right)
            total = product if total is None else total + product
        result.append((adapter_scale * total).astype(BF))
    start = 0
    for out, size in zip(outs, sizes):
        out[:, :columns] = result[0][start:start + size, :]
        out[:, columns:] = result[1][start:start + size, :]
        start += size


def grow(core, parts, place, mine, sibling, sizes):
    columns = mine.shape[3]
    vmem = pl.BlockSpec(memory_space=pltpu.VMEM)
    return pl.pallas_call(
        functools.partial(grow_kernel, len(parts), sizes),
        in_specs=[pl.BlockSpec(memory_space=pltpu.SMEM)] + [vmem] * (len(parts) + 3),
        out_specs=[vmem] * len(sizes),
        out_shape=[jax.ShapeDtypeStruct((s, 2 * columns), BF) for s in sizes],
        cost_estimate=COST,
        compiler_params=pltpu.CompilerParams(vmem_limit_bytes=VMEM_LIMIT),
        name="grow_rows",
    )(core, *parts, place, mine, sibling)


def base_kernel(shifts, place_ref, tokens_ref, weight_ref, *outs):
    step = pl.program_id(0)
    weight = jnp.swapaxes(weight_ref[...], 0, 1)
    columns = weight.shape[2]
    both = [dot(tokens_ref[...], weight[j]) for j in range(2)]
    for i, out in enumerate(outs):

        @pl.when(step == i)
        def _():
            for j in range(2):
                out[:, j * columns:(j + 1) * columns] = both[j].astype(out.dtype)


def base_parts(t, tokens, weight, blocks, shifts, vmem=VMEM_LIMIT):
    rows, width = tokens.shape
    columns = weight.shape[2] // blocks
    types = [BF if r % 2 else F32 for r in shifts]
    if columns % 128:
        cut = [lax.dynamic_slice_in_dim(weight, (t ^ r) * columns, columns, 2) for r in shifts]
        return [dot(tokens, c.reshape(width, 2 * columns)).astype(k) for c, k in zip(cut, types)]

    def block(i, place):
        shift = shifts[0]
        for k, r in enumerate(shifts[1:], 1):
            shift = jnp.where(i == k, r, shift)
        return 0, 0, place[0] ^ shift

    return pl.pallas_call(
        functools.partial(base_kernel, shifts),
        grid_spec=pltpu.PrefetchScalarGridSpec(
            num_scalar_prefetch=1,
            grid=(len(shifts),),
            in_specs=[
                pl.BlockSpec((rows, width), lambda i, p: (0, 0)),
                pl.BlockSpec((width, 2, columns), block),
            ],
            out_specs=[pl.BlockSpec((rows, 2 * columns), lambda i, p: (0, 0))] * len(shifts),
        ),
        out_shape=[jax.ShapeDtypeStruct((rows, 2 * columns), k) for k in types],
        cost_estimate=pl.CostEstimate(
            flops=16 * len(shifts) * rows * width * columns, bytes_accessed=8 * width * columns, transcendentals=0
        ),
        compiler_params=pltpu.CompilerParams(vmem_limit_bytes=vmem),
        name="base_parts",
    )(t.reshape(1), tokens, weight)


def spread_kernel(sizes, first_rows, key_ref, out):
    start = 0
    for m, size in enumerate(sizes):
        padded = round_up(size, 128)
        lane = lax.broadcasted_iota(jnp.int32, (key_ref.shape[0], padded), 1)
        hit = (lane == key_ref[:, 0:1] - first_rows[m] - m * 65536) & (lane < size - 1)
        out[:, start:start + padded] = hit.astype(F32).astype(BF)
        start += padded


def spread_of(key, sizes, first_rows):
    vmem = pl.BlockSpec(memory_space=pltpu.VMEM)
    total = sum(round_up(size, 128) for size in sizes)
    return pl.pallas_call(
        functools.partial(spread_kernel, sizes, first_rows),
        in_specs=[vmem],
        out_specs=vmem,
        out_shape=jax.ShapeDtypeStruct((key.shape[0], total), BF),
        cost_estimate=COST,
        compiler_params=pltpu.CompilerParams(vmem_limit_bytes=VMEM_LIMIT),
        name="spread_rows",
    )(key)


def finish_kernel(sizes, count, *refs):
    bases, spreads, out = refs[:count], refs[count:count + len(sizes)], refs[-1]
    updates = refs[count + len(sizes):-1]
    total = bases[0][...]
    for base in bases[1:]:
        total = total + base[...].astype(F32)
    update_rows = jnp.zeros(total.shape, F32)
    done = 0
    for spread, group in zip(spreads, sizes):
        start = 0
        for size in group:
            padded = round_up(size, 128)
            rows = updates[done][...]
            if padded > size:
                rows = jnp.concatenate([rows, jnp.zeros((padded - size, rows.shape[1]), rows.dtype)], axis=0)
            update_rows = update_rows + dot(spread[:, start:start + padded], rows)
            start += padded
            done += 1
    total = total + update_rows
    columns = out.shape[2]
    if columns % 128:
        out[:, 0, :] = total[:, :columns].astype(BF)
        out[:, 1, :] = total[:, columns:].astype(BF)
    else:
        both = jnp.stack([total[:, :columns], total[:, columns:]], axis=0).astype(BF)
        out[...] = jnp.swapaxes(both, 0, 1)


def finish(bases, spreads, groups):
    sizes = tuple(tuple(u.shape[0] for u in group) for group in groups)
    rows, both = bases[0].shape
    updates = [u for group in groups for u in group]
    block = rows // 2
    return pl.pallas_call(
        functools.partial(finish_kernel, sizes, len(bases)),
        grid=(2,),
        in_specs=[pl.BlockSpec((block, x.shape[1]), lambda i: (i, 0)) for x in bases + spreads]
        + [pl.BlockSpec(u.shape, lambda i: (0, 0)) for u in updates],
        out_specs=pl.BlockSpec((block, 2, both // 2), lambda i: (i, 0, 0)),
        out_shape=jax.ShapeDtypeStruct((rows, 2, both // 2), BF),
        cost_estimate=COST,
        compiler_params=pltpu.CompilerParams(vmem_limit_bytes=VMEM_LIMIT),
        name="finish_rows",
    )(*bases, *spreads, *updates)


def exchange(array, axis, shift):
    size = lax.axis_size(axis)
    return lax.ppermute(array, axis, [(i, i ^ shift) for i in range(size)])


def after(array, *others):
    return lax.optimization_barrier((array,) + others)[0]


def bits(value):
    return bin(value).count("1")


def per_device(
    tokens,
    row_adapter_index,
    adapter_storage_slot,
    key_value_base_weight,
    adapter_down_weight,
    adapter_up_weight,
):
    row_count, width = tokens.shape
    local = adapter_down_weight.shape[0]
    groups = lax.axis_size("dp")
    blocks = lax.axis_size("tensor")
    experts = local * groups
    chips = groups // 2
    capacity = max(2, 2 * row_count // experts)
    chip_slots = 2 * local
    full = chip_slots * capacity

    me = lax.axis_index("dp").astype(jnp.int32)
    chip, core = (me // 2).reshape(1), (me % 2).reshape(1)
    adapters = row_adapter_index.reshape(1, row_count)
    slots = adapter_storage_slot.reshape(1, experts)
    flag_lane = width // 2 - 1

    down_sibling = exchange(adapter_down_weight, "dp", 1)

    near = [m for m in range(chips) if bits(m) <= 1]
    far = [m for m in range(chips) if bits(m) > 1]
    message = round_up(full * 11 // 16, 16)
    rest = round_up(full - message + 2, 16)
    sizes, first_rows = (message,) * chips, (0,) * chips

    t = lax.axis_index("tensor").astype(jnp.int32)
    first_shift = blocks - 1
    parts, came = {}, {}

    def compute(shifts, ready, vmem=VMEM_LIMIT):
        parts.update(zip(shifts, base_parts(t, ready, key_value_base_weight, blocks, shifts, vmem)))

    def arrived_for(r):
        return [came[key] for key in sorted(came) if key[1] == r]

    def send(r):
        part = parts[r]
        for one in arrived_for(r):
            part = part + one.astype(F32)
        part = part.astype(BF)
        came[(r & -r, r ^ (r & -r))] = exchange(part, "tensor", r & -r)
        return part

    odd, even = list(range(first_shift, 0, -2)), list(range(2, first_shift, 2))
    compute(odd, tokens, VMEM_MOST)
    for r in odd:
        send(r)
    packed = pack(chip, adapters, slots, after(tokens, parts[first_shift]), sizes, first_rows, chip_slots)
    sent, key = list(packed[:-1]), packed[-1]
    arrived, returned = {0: sent[0]}, {}
    for m in near[1:]:
        arrived[m] = exchange(sent[m], "dp", 2 * m)
    compute(even, after(tokens, *sent), VMEM_MOST)
    for r in sorted(even, key=lambda r: (r & -r, -r)):
        last_sent = send(r)

    up_sibling = exchange(after(adapter_up_weight, down_sibling), "dp", 1)
    held = hold(after(down_sibling, last_sent))
    carry = shrink(core, [sent[0]], adapter_down_weight, held, flag_lane)
    carry = (carry[0], carry[2], carry[3])
    near_done = [arrived[m] for m in near[1:]]
    for m in far:
        arrived[m] = exchange(after(sent[m], *near_done, carry[0]), "dp", 2 * m)

    both_down = after(held, up_sibling)
    flags, updates = [], {}
    for part in (near, far):
        if not part:
            continue
        group = [arrived[m] for m in part if m]
        if part is near:
            share, _, place, flag = shrink(core, group, adapter_down_weight, both_down, flag_lane, carry)
            compute([0], after(tokens, share))
            step = 1
            while 2 * step < blocks:
                share = share + exchange(share if step == 1 else share.astype(BF), "tensor", step).astype(F32)
                step *= 2
            shares = [share, exchange(share.astype(BF), "tensor", step)]
            base = after(parts[0], share)
            for one in arrived_for(0):
                base = base + one.astype(F32)
        else:
            group[0] = after(group[0], base)
            share, rounded, place, flag = shrink(core, group, adapter_down_weight, both_down, flag_lane)
            shares = [after(share, returned[0])] + [exchange(rounded, "tensor", z) for z in range(1, blocks)]
        flags.append(flag)
        grown = grow(core, shares, place, adapter_up_weight, up_sibling, tuple(sizes[m] for m in part))
        for m, update in zip(part, grown):
            returned[m] = update if m == 0 else exchange(update, "dp", 2 * m)
    bases = [base]
    spread = spread_of(after(key, base), sizes, first_rows)
    flag = functools.reduce(jnp.maximum, flags)
    flag = jnp.maximum(flag, exchange(flag, "dp", 1))
    updates = [returned[m] for m in range(chips)]

    def as_is():
        return finish(bases, [spread], [updates])

    def second_round():
        later_sizes, later_rows = (rest,) * chips, (message - 1,) * chips
        packed = pack(chip, adapters, slots, tokens, later_sizes, later_rows, chip_slots)
        group = [packed[0]] + [exchange(packed[m], "dp", 2 * m) for m in range(1, chips)]
        share, _, place, _ = shrink(core, group, adapter_down_weight, down_sibling, flag_lane)
        shares = [share] + [exchange(share, "tensor", z) for z in range(1, blocks)]
        grown = grow(core, shares, place, adapter_up_weight, up_sibling, later_sizes)
        back = [grown[0]] + [exchange(grown[m], "dp", 2 * m) for m in range(1, chips)]
        return finish(bases, [spread, spread_of(packed[-1], later_sizes, later_rows)], [updates, back])

    return lax.cond(flag[0, 0] > 0.0, second_round, as_is)


def solution(mesh):
    placed = (
        P("dp", "tensor"),
        P("dp", None),
        P(),
        P("tensor", None, None),
        P("dp", "tensor", None),
        P("dp", None, None, "tensor"),
    )
    return jax.shard_map(
        per_device, mesh=mesh, in_specs=placed, out_specs=P("dp", None, "tensor"), check_vma=False
    )
```

```python
import functools

import jax
import jax.numpy as jnp
from jax import lax
from jax.experimental import pallas as pl
from jax.experimental.pallas import tpu as pltpu
from jax.sharding import PartitionSpec as P

adapter_scale = 0.5
BF = jnp.bfloat16
F32 = jnp.float32
VMEM_LIMIT = 28 * 1024 * 1024
VMEM_MOST = 57 * 1024 * 1024
COST = pl.CostEstimate(flops=1000, bytes_accessed=1000, transcendentals=0)


def round_up(value, unit):
    return (value + unit - 1) // unit * unit


def dot(a, b, contract=((1,), (0,))):
    return lax.dot_general(a, b, (contract, ((), ())), preferred_element_type=F32)


def pack_kernel(shape, place_ref, adapter_ref, slot_ref, tokens_ref, *refs):
    sizes, first_rows, chip_slots, flag_lane = shape
    messages = len(sizes)
    outs, key_ref, pick, tail = refs[:messages], *refs[messages:]
    rows, width = tokens_ref.shape
    experts = slot_ref.shape[1]
    offsets = [sum(sizes[:m]) for m in range(messages)]

    @pl.when(pl.program_id(0) == 0)
    def _():
        named = (lax.broadcasted_iota(jnp.int32, (experts, rows), 0) == adapter_ref[...]).astype(BF)
        slots = jnp.broadcast_to(slot_ref[...].astype(F32), (16, experts)).astype(BF)
        slot = dot(slots, named)[0:1, :].astype(jnp.int32)
        shift = (slot // chip_slots) ^ place_ref[0]
        within = (slot % chip_slots + 1).astype(F32)
        lanes = round_up(messages, 16)
        goes = lax.broadcasted_iota(jnp.int32, (lanes, rows), 0) == shift
        earlier = lax.broadcasted_iota(jnp.int32, (rows, rows), 0) < lax.broadcasted_iota(jnp.int32, (rows, rows), 1)
        goes_f = goes.astype(F32)
        rank = dot(goes_f.astype(BF), earlier.astype(F32).astype(BF))
        position = jnp.sum(rank * goes_f, axis=0, keepdims=True).astype(jnp.int32)
        counts = jnp.sum(goes_f, axis=1, keepdims=True)
        sub = lax.broadcasted_iota(jnp.int32, (lanes, 1), 0)
        limit = jnp.zeros((lanes, 1), F32)
        for m in range(messages):
            limit = jnp.where(sub == m, F32(first_rows[m] + sizes[m] - 1), limit)
        over = jnp.max(jnp.where((sub < messages) & (counts > limit), 1.0, 0.0), axis=0, keepdims=True)
        key = jnp.broadcast_to(position + shift * 65536, (8, rows))
        key_ref[...] = jnp.broadcast_to(key.astype(F32).T[:, 0:1].astype(jnp.int32), key_ref.shape)
        within8 = jnp.broadcast_to(within, (16, rows)).astype(BF)
        for m in range(messages):
            padded = round_up(sizes[m], 128)
            target = lax.broadcasted_iota(jnp.int32, (padded, rows), 0)
            wanted = position - first_rows[m]
            wanted = jnp.where((shift == m) & (wanted < sizes[m] - 1), wanted, -1)
            chosen = jnp.where(target == wanted, 1.0, 0.0).astype(BF)
            pick[offsets[m]:offsets[m] + sizes[m], :] = chosen[:sizes[m], :]
            places = dot(within8, chosen, ((1,), (1,)))[0:1, :]
            if padded < width:
                places = jnp.concatenate([places, jnp.zeros((1, width - padded), F32)], axis=1)
            lane = lax.broadcasted_iota(jnp.int32, (1, width), 1)
            tail[m:m + 1, :] = jnp.where(lane == flag_lane, over, places)

    body = dot(pick[...], tokens_ref[...])
    for m in range(messages):
        outs[m][...] = body[offsets[m]:offsets[m] + sizes[m], :].astype(BF)

    @pl.when(pl.program_id(0) == 0)
    def _():
        for m in range(messages):
            end = outs[m][sizes[m] - 16:sizes[m], :].astype(F32)
            row = lax.broadcasted_iota(jnp.int32, (16, 1), 0)
            outs[m][sizes[m] - 16:sizes[m], :] = jnp.where(row == 15, tail[m:m + 1, :], end).astype(BF)


def pack(chip, adapters, slots, tokens, sizes, first_rows, chip_slots, steps=2):
    rows, width = tokens.shape
    block = width // steps
    return pl.pallas_call(
        functools.partial(pack_kernel, (sizes, first_rows, chip_slots, block - 1)),
        grid=(steps,),
        in_specs=[
            pl.BlockSpec(memory_space=pltpu.SMEM),
            pl.BlockSpec((1, rows), lambda i: (0, 0)),
            pl.BlockSpec((1, slots.shape[1]), lambda i: (0, 0)),
            pl.BlockSpec((rows, block), lambda i: (0, i)),
        ],
        out_specs=[pl.BlockSpec((s, block), lambda i: (0, i)) for s in sizes]
        + [pl.BlockSpec((rows, 128), lambda i: (0, 0))],
        out_shape=[jax.ShapeDtypeStruct((s, width), BF) for s in sizes] + [jax.ShapeDtypeStruct((rows, 128), jnp.int32)],
        scratch_shapes=[
            pltpu.VMEM((sum(sizes), rows), BF),
            pltpu.VMEM((round_up(len(sizes), 8), block), F32),
        ],
        cost_estimate=COST,
        compiler_params=pltpu.CompilerParams(vmem_limit_bytes=VMEM_LIMIT),
        name="pack_rows",
    )(chip, adapters, slots, tokens)


def shrink_kernel(count, carried, flag_lane, core_ref, *refs):
    messages, (mine, sibling) = refs[:count], refs[count:count + 2]
    carry, refs = refs[count + 2:count + 2 + carried], refs[count + 2 + carried:]
    out, send_out, place_out, flag_out, places = refs
    kept = carry[0].shape[0] if carried else 0
    total = out.at[kept:, :]
    step = pl.program_id(0)
    local = mine.shape[0] * pl.num_programs(0)
    sizes = [m.shape[0] for m in messages]

    @pl.when(step == 0)
    def _():
        flag = jnp.zeros((1, 1), F32)
        start = 0
        for m, size in zip(messages, sizes):
            padded = round_up(size, 128)
            tail = m[size - 16:size, 0:padded].astype(F32)[15:16, :]
            same = lax.broadcasted_iota(jnp.int32, (size, padded), 0) == lax.broadcasted_iota(jnp.int32, (size, padded), 1)
            column = jnp.sum(jnp.where(same, tail, 0.0), axis=1, keepdims=True)
            places[start:start + size, :] = jnp.broadcast_to(column, (size, 128))
            block = m[size - 16:size, flag_lane - 127:flag_lane + 1].astype(F32)[15:16, :]
            last = lax.broadcasted_iota(jnp.int32, (1, 128), 1) == 127
            flag = jnp.maximum(flag, jnp.max(jnp.where(last, block, 0.0), axis=1, keepdims=True))
            start += size
        place_out[kept:, :] = places[...].astype(BF)
        if carried:
            out[:kept, :] = carry[0][...]
            place_out[:kept, :] = carry[1][...]
            flag = jnp.maximum(flag, carry[2][0:1, 0:1])
        flag_out[...] = jnp.broadcast_to(flag, (8, 128))
        total[...] = jnp.zeros_like(total)

    rows = messages[0][...] if count == 1 else jnp.concatenate([m[...] for m in messages], axis=0)
    place = places[...]
    core = core_ref[0]
    each = mine.shape[0]
    every = [weights[e] for weights in (mine, sibling) for e in range(each)]
    product = dot(rows, jnp.concatenate(every, axis=1))
    picked = total[...]
    for k, side in enumerate((core, 1 - core)):
        first = (side * local + each * step + 1).astype(F32)
        for e in range(each):
            start = 128 * (each * k + e)
            picked = picked + jnp.where(place == first + e, product[:, start:start + 128], 0.0)
    total[...] = picked

    @pl.when(step == pl.num_programs(0) - 1)
    def _():
        send_out[...] = out[...].astype(BF)


def shrink(core, messages, mine, sibling, flag_lane, carry=()):
    local, width, both = mine.shape
    rows = sum(m.shape[0] for m in messages)
    whole = [pl.BlockSpec(m.shape, lambda i: (0, 0)) for m in messages]
    pair = pl.BlockSpec((4, width, both), lambda i: (i, 0, 0))
    every = rows + (carry[0].shape[0] if carry else 0)
    keep = pl.BlockSpec((every, both), lambda i: (0, 0))
    kept = [pl.BlockSpec(c.shape, lambda i: (0, 0)) for c in carry]
    return pl.pallas_call(
        functools.partial(shrink_kernel, len(messages), len(carry), flag_lane),
        grid=(local // 4,),
        in_specs=[pl.BlockSpec(memory_space=pltpu.SMEM)] + whole + [pair, pair] + kept,
        out_specs=[keep, keep, keep, pl.BlockSpec((8, 128), lambda i: (0, 0))],
        out_shape=[
            jax.ShapeDtypeStruct((every, both), F32),
            jax.ShapeDtypeStruct((every, both), BF),
            jax.ShapeDtypeStruct((every, both), BF),
            jax.ShapeDtypeStruct((8, 128), F32),
        ],
        scratch_shapes=[pltpu.VMEM((rows, both), F32)],
        cost_estimate=pl.CostEstimate(
            flops=1000, bytes_accessed=1000, transcendentals=0
        ),
        compiler_params=pltpu.CompilerParams(vmem_limit_bytes=VMEM_LIMIT),
        name="shrink_rows",
    )(core, *messages, mine, sibling, *carry)


def hold_kernel(source, out):
    out[...] = source[...]


def hold(array):
    block = pl.BlockSpec((2,) + array.shape[1:], lambda i: (i, 0, 0))
    return pl.pallas_call(
        hold_kernel,
        grid=(array.shape[0] // 2,),
        in_specs=[block],
        out_specs=block,
        out_shape=jax.ShapeDtypeStruct(array.shape, array.dtype),
        cost_estimate=COST,
        compiler_params=pltpu.CompilerParams(vmem_limit_bytes=VMEM_LIMIT),
        name="hold_weights",
    )(array)


def grow_kernel(shares, sizes, core_ref, *refs):
    parts, place_ref, mine, sibling = refs[:shares], refs[shares], refs[shares + 1], refs[shares + 2]
    outs = refs[shares + 3:]
    summed = parts[0][...].astype(F32)
    for part in parts[1:]:
        summed = summed + part[...].astype(F32)
    shrunk = summed.astype(BF).astype(F32)
    place = place_ref[...].astype(F32)
    local, _, rank, columns = mine.shape
    core = core_ref[0]
    low = lax.broadcasted_iota(jnp.int32, shrunk.shape, 1) < rank
    turned = pltpu.roll(shrunk, rank, 1)
    result = []
    for j in range(2):
        twice = jnp.where(low, shrunk, turned) if j == 0 else jnp.where(low, turned, shrunk)
        total = None
        for weights, side in ((mine, core), (sibling, 1 - core)):
            left = []
            for e in range(0, local, 2):
                first = (side * local + e + 1).astype(F32)
                wanted = jnp.where(low, first, first + 1.0)
                left.append(jnp.where(place == wanted, twice, 0.0).astype(BF))
            right = weights[:, j].reshape(local * rank, columns)
            product = dot(jnp.concatenate(left, axis=1), right)
            total = product if total is None else total + product
        result.append((adapter_scale * total).astype(BF))
    start = 0
    for out, size in zip(outs, sizes):
        out[:, :columns] = result[0][start:start + size, :]
        out[:, columns:] = result[1][start:start + size, :]
        start += size


def grow(core, parts, place, mine, sibling, sizes):
    columns = mine.shape[3]
    vmem = pl.BlockSpec(memory_space=pltpu.VMEM)
    return pl.pallas_call(
        functools.partial(grow_kernel, len(parts), sizes),
        in_specs=[pl.BlockSpec(memory_space=pltpu.SMEM)] + [vmem] * (len(parts) + 3),
        out_specs=[vmem] * len(sizes),
        out_shape=[jax.ShapeDtypeStruct((s, 2 * columns), BF) for s in sizes],
        cost_estimate=COST,
        compiler_params=pltpu.CompilerParams(vmem_limit_bytes=VMEM_LIMIT),
        name="grow_rows",
    )(core, *parts, place, mine, sibling)


def base_kernel(shifts, place_ref, tokens_ref, weight_ref, *outs):
    step = pl.program_id(0)
    weight = jnp.swapaxes(weight_ref[...], 0, 1)
    columns = weight.shape[2]
    both = [dot(tokens_ref[...], weight[j]) for j in range(2)]
    for i, out in enumerate(outs):

        @pl.when(step == i)
        def _():
            for j in range(2):
                out[:, j * columns:(j + 1) * columns] = both[j].astype(out.dtype)


def base_parts(t, tokens, weight, blocks, shifts, vmem=VMEM_LIMIT):
    rows, width = tokens.shape
    columns = weight.shape[2] // blocks
    types = [BF if r % 2 else F32 for r in shifts]
    if columns % 128:
        cut = [lax.dynamic_slice_in_dim(weight, (t ^ r) * columns, columns, 2) for r in shifts]
        return [dot(tokens, c.reshape(width, 2 * columns)).astype(k) for c, k in zip(cut, types)]

    def block(i, place):
        shift = shifts[0]
        for k, r in enumerate(shifts[1:], 1):
            shift = jnp.where(i == k, r, shift)
        return 0, 0, place[0] ^ shift

    return pl.pallas_call(
        functools.partial(base_kernel, shifts),
        grid_spec=pltpu.PrefetchScalarGridSpec(
            num_scalar_prefetch=1,
            grid=(len(shifts),),
            in_specs=[
                pl.BlockSpec((rows, width), lambda i, p: (0, 0)),
                pl.BlockSpec((width, 2, columns), block),
            ],
            out_specs=[pl.BlockSpec((rows, 2 * columns), lambda i, p: (0, 0))] * len(shifts),
        ),
        out_shape=[jax.ShapeDtypeStruct((rows, 2 * columns), k) for k in types],
        cost_estimate=pl.CostEstimate(
            flops=16 * len(shifts) * rows * width * columns, bytes_accessed=8 * width * columns, transcendentals=0
        ),
        compiler_params=pltpu.CompilerParams(vmem_limit_bytes=vmem),
        name="base_parts",
    )(t.reshape(1), tokens, weight)


def spread_kernel(sizes, first_rows, key_ref, out):
    start = 0
    for m, size in enumerate(sizes):
        padded = round_up(size, 128)
        lane = lax.broadcasted_iota(jnp.int32, (key_ref.shape[0], padded), 1)
        hit = (lane == key_ref[:, 0:1] - first_rows[m] - m * 65536) & (lane < size - 1)
        out[:, start:start + padded] = hit.astype(F32).astype(BF)
        start += padded


def spread_of(key, sizes, first_rows):
    vmem = pl.BlockSpec(memory_space=pltpu.VMEM)
    total = sum(round_up(size, 128) for size in sizes)
    return pl.pallas_call(
        functools.partial(spread_kernel, sizes, first_rows),
        in_specs=[vmem],
        out_specs=vmem,
        out_shape=jax.ShapeDtypeStruct((key.shape[0], total), BF),
        cost_estimate=COST,
        compiler_params=pltpu.CompilerParams(vmem_limit_bytes=VMEM_LIMIT),
        name="spread_rows",
    )(key)


def finish_kernel(sizes, count, *refs):
    bases, spreads, out = refs[:count], refs[count:count + len(sizes)], refs[-1]
    updates = refs[count + len(sizes):-1]
    total = bases[0][...]
    for base in bases[1:]:
        total = total + base[...].astype(F32)
    update_rows = jnp.zeros(total.shape, F32)
    done = 0
    for spread, group in zip(spreads, sizes):
        start = 0
        for size in group:
            padded = round_up(size, 128)
            rows = updates[done][...]
            if padded > size:
                rows = jnp.concatenate([rows, jnp.zeros((padded - size, rows.shape[1]), rows.dtype)], axis=0)
            update_rows = update_rows + dot(spread[:, start:start + padded], rows)
            start += padded
            done += 1
    total = total + update_rows
    columns = out.shape[2]
    if columns % 128:
        out[:, 0, :] = total[:, :columns].astype(BF)
        out[:, 1, :] = total[:, columns:].astype(BF)
    else:
        both = jnp.stack([total[:, :columns], total[:, columns:]], axis=0).astype(BF)
        out[...] = jnp.swapaxes(both, 0, 1)


def finish(bases, spreads, groups):
    sizes = tuple(tuple(u.shape[0] for u in group) for group in groups)
    rows, both = bases[0].shape
    updates = [u for group in groups for u in group]
    block = rows // 2
    return pl.pallas_call(
        functools.partial(finish_kernel, sizes, len(bases)),
        grid=(2,),
        in_specs=[pl.BlockSpec((block, x.shape[1]), lambda i: (i, 0)) for x in bases + spreads]
        + [pl.BlockSpec(u.shape, lambda i: (0, 0)) for u in updates],
        out_specs=pl.BlockSpec((block, 2, both // 2), lambda i: (i, 0, 0)),
        out_shape=jax.ShapeDtypeStruct((rows, 2, both // 2), BF),
        cost_estimate=COST,
        compiler_params=pltpu.CompilerParams(vmem_limit_bytes=VMEM_LIMIT),
        name="finish_rows",
    )(*bases, *spreads, *updates)


def exchange(array, axis, shift):
    size = lax.axis_size(axis)
    return lax.ppermute(array, axis, [(i, i ^ shift) for i in range(size)])


def after(array, *others):
    return lax.optimization_barrier((array,) + others)[0]


def bits(value):
    return bin(value).count("1")


def per_device(
    tokens,
    row_adapter_index,
    adapter_storage_slot,
    key_value_base_weight,
    adapter_down_weight,
    adapter_up_weight,
):
    row_count, width = tokens.shape
    local = adapter_down_weight.shape[0]
    groups = lax.axis_size("dp")
    blocks = lax.axis_size("tensor")
    experts = local * groups
    chips = groups // 2
    capacity = max(2, 2 * row_count // experts)
    chip_slots = 2 * local
    full = chip_slots * capacity

    me = lax.axis_index("dp").astype(jnp.int32)
    chip, core = (me // 2).reshape(1), (me % 2).reshape(1)
    adapters = row_adapter_index.reshape(1, row_count)
    slots = adapter_storage_slot.reshape(1, experts)
    flag_lane = width // 2 - 1

    down_sibling = exchange(adapter_down_weight, "dp", 1)

    near = [m for m in range(chips) if bits(m) <= 1]
    far = [m for m in range(chips) if bits(m) > 1]
    message = round_up(full * 11 // 16, 16)
    rest = round_up(full - message + 2, 16)
    sizes, first_rows = (message,) * chips, (0,) * chips

    t = lax.axis_index("tensor").astype(jnp.int32)
    first_shift = blocks - 1
    parts, came = {}, {}

    def compute(shifts, ready, vmem=VMEM_LIMIT):
        parts.update(zip(shifts, base_parts(t, ready, key_value_base_weight, blocks, shifts, vmem)))

    def arrived_for(r):
        return [came[key] for key in sorted(came) if key[1] == r]

    def send(r):
        part = parts[r]
        for one in arrived_for(r):
            part = part + one.astype(F32)
        part = part.astype(BF)
        came[(r & -r, r ^ (r & -r))] = exchange(part, "tensor", r & -r)
        return part

    odd, even = list(range(first_shift, 0, -2)), list(range(2, first_shift, 2))
    compute(odd, tokens, VMEM_MOST)
    for r in odd:
        send(r)
    packed = pack(chip, adapters, slots, after(tokens, parts[first_shift]), sizes, first_rows, chip_slots)
    sent, key = list(packed[:-1]), packed[-1]
    arrived, returned = {0: sent[0]}, {}
    for m in near[1:]:
        arrived[m] = exchange(sent[m], "dp", 2 * m)
    compute(even, after(tokens, *sent), VMEM_MOST)
    for r in sorted(even, key=lambda r: (r & -r, -r)):
        last_sent = send(r)

    up_sibling = exchange(after(adapter_up_weight, down_sibling), "dp", 1)
    held = hold(after(down_sibling, last_sent))
    carry = shrink(core, [sent[0]], adapter_down_weight, held, flag_lane)
    carry = (carry[0], carry[2], carry[3])
    near_done = [arrived[m] for m in near[1:]]
    for m in far:
        arrived[m] = exchange(after(sent[m], *near_done, carry[0]), "dp", 2 * m)

    both_down = after(held, up_sibling)
    flags, updates = [], {}
    for part in (near, far):
        if not part:
            continue
        group = [arrived[m] for m in part if m]
        if part is near:
            share, _, place, flag = shrink(core, group, adapter_down_weight, both_down, flag_lane, carry)
            compute([0], after(tokens, share))
            step = 1
            while 2 * step < blocks:
                share = share + exchange(share if step == 1 else share.astype(BF), "tensor", step).astype(F32)
                step *= 2
            shares = [share, exchange(share.astype(BF), "tensor", step)]
            base = after(parts[0], share)
            for one in arrived_for(0):
                base = base + one.astype(F32)
        else:
            group[0] = after(group[0], base)
            share, rounded, place, flag = shrink(core, group, adapter_down_weight, both_down, flag_lane)
            shares = [after(share, returned[0])] + [exchange(rounded, "tensor", z) for z in range(1, blocks)]
        flags.append(flag)
        grown = grow(core, shares, place, adapter_up_weight, up_sibling, tuple(sizes[m] for m in part))
        for m, update in zip(part, grown):
            returned[m] = update if m == 0 else exchange(update, "dp", 2 * m)
    bases = [base]
    spread = spread_of(after(key, base), sizes, first_rows)
    flag = functools.reduce(jnp.maximum, flags)
    flag = jnp.maximum(flag, exchange(flag, "dp", 1))
    updates = [returned[m] for m in range(chips)]

    def as_is():
        return finish(bases, [spread], [updates])

    def second_round():
        later_sizes, later_rows = (rest,) * chips, (message - 1,) * chips
        packed = pack(chip, adapters, slots, tokens, later_sizes, later_rows, chip_slots)
        group = [packed[0]] + [exchange(packed[m], "dp", 2 * m) for m in range(1, chips)]
        share, _, place, _ = shrink(core, group, adapter_down_weight, down_sibling, flag_lane)
        shares = [share] + [exchange(share, "tensor", z) for z in range(1, blocks)]
        grown = grow(core, shares, place, adapter_up_weight, up_sibling, later_sizes)
        back = [grown[0]] + [exchange(grown[m], "dp", 2 * m) for m in range(1, chips)]
        return finish(bases, [spread, spread_of(packed[-1], later_sizes, later_rows)], [updates, back])

    return lax.cond(flag[0, 0] > 0.0, second_round, as_is)


def solution(mesh):
    placed = (
        P("dp", "tensor"),
        P("dp", None),
        P(),
        P("tensor", None, None),
        P("dp", "tensor", None),
        P("dp", None, None, "tensor"),
    )
    return jax.shard_map(
        per_device, mesh=mesh, in_specs=placed, out_specs=P("dp", None, "tensor"), check_vma=False
    )
```
